32 devices in a mesh: seq: 32 (over z, y, x, core).
Axes of the slice: x: 2, y: 2, z: 4, core: 2. Of those that a mesh axis runs over, the one named last changes fastest.
Arguments:
- inputs: bfloat16 [2, 8192, 1536], P(None, 'seq'), may hold values from -8 to 8
- ln_gain: float32 [1536], replicated, may hold values from 0.25 to 1.75
- w_in: bfloat16 [1536, 3072], replicated, may hold values from -0.15625 to 0.15625
- kernel: float32 [32, 1536], replicated, may hold values from -1 to 1
- bn_gain: float32 [1536], replicated, may hold values from 0.25 to 1.75
- bn_bias: float32 [1536], replicated, may hold values from -0.6 to 0.6
- w_out: bfloat16 [1536, 1536], replicated, may hold values from -0.15625 to 0.15625
- cotangent: bfloat16 [2, 8192, 1536], P(None, 'seq'), may hold values from -6 to 6
Outputs:
- outputs: bfloat16 [2, 8192, 1536], P(None, 'seq')
- d_inputs: bfloat16 [2, 8192, 1536], P(None, 'seq')
- d_w_out: float32 [1536, 1536], P('seq')
- d_kernel: float32 [32, 1536], replicated
- d_bn_gain: float32 [1536], replicated
- d_bn_bias: float32 [1536], replicated
The draws below stay inside these ranges and needn't reach their ends.
All inputs are finite; a program needn't handle non-finite values.
Results may differ from the reference program's by a relative error of at most 0.0075.
Values may be sent and summed in bfloat16 or wider, within the bound.
No kernel may reach another device: no remote copies, remote signals or barrier semaphores. Data moves between devices by JAX's collectives and lax.ppermute only.
A program may use at most 128 MiB of HBM per device.

```python
import math
import jax
import jax.numpy as jnp
from jax import lax

D = 1536
K = 32
UTT = 2
FRAMES = 8192


def draw_inputs(key, part):
    noise_key = jax.random.fold_in(key, 11)
    along_key = jax.random.fold_in(key, 23)
    position = jnp.arange(FRAMES, dtype=jnp.float32) / FRAMES
    direction = jax.random.normal(along_key, (UTT, 1, D), jnp.float32)
    noise = jax.random.normal(noise_key, (UTT, FRAMES, D), jnp.float32)
    amplitude = 0.3 * jnp.power(5.0, position)
    result = noise + amplitude[None, :, None] * direction
    return jnp.clip(result, -8.0, 8.0).astype(jnp.bfloat16)


def spiked(values, own_key, source, target, parts, factor):
    def block_of(dim):
        return (jnp.arange(values.shape[dim]) // (values.shape[dim] // parts)).reshape((-1,) + (1,) * (values.ndim - 1 - dim))

    near = jax.random.permutation(own_key, parts)[block_of(target)]
    other_side = (block_of(target) + parts // 2) % parts
    return jnp.where((block_of(source) == near) | (block_of(source) == other_side), factor * values, values)


def shard_levels(own_key, shape, shards, least, top_value):
    def one(dim, parts):
        steps = jax.random.uniform(jax.random.fold_in(jax.random.fold_in(own_key, 6), dim), (parts,), jnp.float32, least / len(shards), top_value / len(shards))
        return jnp.repeat(jnp.exp(steps), shape[dim] // parts).reshape((-1,) + (1,) * (len(shape) - dim - 1))

    level = one(*shards[0])
    for cut in shards[1:]:
        level = level * one(*cut)
    return level


def scatter_about(own_key, dims, scale, limit, split=(), kind=jnp.bfloat16):
    values = scale * jax.random.normal(own_key, dims, jnp.float32)
    if split:
        values = values * shard_levels(own_key, dims, split, -0.22, 0.18)
    return jnp.clip(values, -limit, limit).astype(kind)


def heavy_noise(own_key, extent, deviation, reach, split, heavy, held_as=jnp.bfloat16):
    drawn = deviation * jax.random.normal(own_key, extent, jnp.float32)
    if split:
        drawn = drawn * shard_levels(own_key, extent, split, -0.22, 0.18)
    return jnp.clip(spiked(drawn, jax.random.fold_in(own_key, 3), *heavy), -reach, reach).astype(held_as)


def setup_inputs(seed: int = 0) -> dict:
    splits = jax.random.split(jax.random.key(seed), 9)
    inputs = draw_inputs(jax.random.fold_in(splits[8], 71), 0)
    ln_gain = jnp.clip(1.0 + 0.15 * jax.random.normal(splits[1], (D,), jnp.float32), 0.25, 1.75)
    w_in = scatter_about(splits[2], (D, 2 * D), D ** -0.5, 0.15625)
    kernel = scatter_about(splits[3], (K, D), K ** -0.5, 1.0, (), jnp.float32)
    bn_gain = jnp.clip(1.0 + 0.15 * jax.random.normal(splits[4], (D,), jnp.float32), 0.25, 1.75)
    bn_bias = jnp.clip(jax.random.uniform(splits[5], (D,), jnp.float32, -0.6, 0.6), -0.6, 0.6)
    w_out = scatter_about(splits[6], (D, D), D ** -0.5, 0.15625)
    cotangent = heavy_noise(splits[7], (UTT, FRAMES, D), 1.0, 6.0, ((1, 32),), (1, 2, 32, 2.75))
    return {"inputs": inputs, "ln_gain": ln_gain, "w_in": w_in, "kernel": kernel, "bn_gain": bn_gain, "bn_bias": bn_bias, "w_out": w_out, "cotangent": cotangent}


EPSILON = 1e-05

def frame_slice(array, utt_index, start, length):
    zero = jnp.zeros((), jnp.int32)
    piece = lax.dynamic_slice(array, (utt_index.astype(jnp.int32), start.astype(jnp.int32), zero), (1, length, array.shape[2]))
    return piece[0]

def layer_norm(x_float):
    ln_mean = lax.optimization_barrier(jnp.mean(x_float, axis=-1, keepdims=True))
    centred = x_float - ln_mean
    ln_rstd = lax.rsqrt(lax.optimization_barrier(jnp.mean(centred * centred, axis=-1, keepdims=True)) + EPSILON)
    return (centred * ln_rstd, ln_rstd)

def reference(inputs, ln_gain, w_in, kernel, bn_gain, bn_bias, w_out, cotangent):
    block_len = math.gcd(FRAMES, 1024)
    per_utt = FRAMES // block_len
    block_ids = jnp.arange(UTT * per_utt, dtype=jnp.int32)
    frame_total = UTT * FRAMES

    def locate(index):
        utt_index = index // per_utt
        start = index % per_utt * block_len
        return (utt_index, start)

    def front(index):
        utt_index, start = locate(index)
        x_float = frame_slice(inputs, utt_index, start, block_len).astype(jnp.float32)
        ln_hat, ln_rstd = layer_norm(x_float)
        normed = (ln_hat * ln_gain).astype(jnp.bfloat16)
        proj = jnp.dot(normed, w_in, preferred_element_type=jnp.float32)
        value_half = proj[:, :D]
        gate_sig = jax.nn.sigmoid(proj[:, D:])
        return (x_float, ln_hat, ln_rstd, value_half, gate_sig)

    def make_gated(index):
        x_float, ln_hat, ln_rstd, value_half, gate_sig = front(index)
        return (value_half * gate_sig).astype(jnp.bfloat16)
    gated = lax.map(make_gated, block_ids).reshape(UTT, FRAMES, D)
    padded = jnp.pad(gated, ((0, 0), (16, 16), (0, 0)))

    def conv_block(index):
        utt_index, start = locate(index)
        window = frame_slice(padded, utt_index, start, block_len + 32).astype(jnp.float32)
        conv_out = jnp.zeros((block_len, D), jnp.float32)
        for tap_index in range(K):
            conv_out = conv_out + kernel[tap_index] * window[tap_index + 1:tap_index + 1 + block_len]
        return (conv_out, window)
    sums = lax.map(lambda index: lax.optimization_barrier(jnp.sum(conv_block(index)[0], axis=0)), block_ids)
    bn_mean = lax.optimization_barrier(jnp.sum(sums, axis=0)) / frame_total

    def spread(index):
        deviate = conv_block(index)[0] - bn_mean
        return lax.optimization_barrier(jnp.sum(deviate * deviate, axis=0))
    bn_var = lax.optimization_barrier(jnp.sum(lax.map(spread, block_ids), axis=0)) / frame_total
    bn_rstd = lax.rsqrt(bn_var + EPSILON)

    def bn_forward(index):
        conv_out, window = conv_block(index)
        normed_bn = (conv_out - bn_mean) * bn_rstd
        bn_out = normed_bn * bn_gain + bn_bias
        return (normed_bn, bn_out, window)

    def tail_step(carry, index):
        weight_acc, bias_acc, gain_acc = carry
        utt_index, start = locate(index)
        normed_bn, bn_out, window = bn_forward(index)
        act_sig = jax.nn.sigmoid(bn_out)
        act = (bn_out * act_sig).astype(jnp.bfloat16)
        x_float = frame_slice(inputs, utt_index, start, block_len).astype(jnp.float32)
        branch = lax.dot_general(act, w_out, (((1,), (1,)), ((), ())), preferred_element_type=jnp.float32)
        out_block = (x_float + branch).astype(jnp.bfloat16)
        cot_rows = frame_slice(cotangent, utt_index, start, block_len)
        d_act = jnp.dot(cot_rows, w_out, preferred_element_type=jnp.float32)
        weight_acc = weight_acc + lax.dot_general(cot_rows, act, (((0,), (0,)), ((), ())), preferred_element_type=jnp.float32)
        d_bn = d_act * (act_sig + bn_out * act_sig * (1.0 - act_sig))
        bias_acc = bias_acc + lax.optimization_barrier(jnp.sum(d_bn, axis=0))
        gain_acc = gain_acc + lax.optimization_barrier(jnp.sum(d_bn * normed_bn, axis=0))
        return ((weight_acc, bias_acc, gain_acc), (out_block, d_bn))
    start_carry = (jnp.zeros((D, D), jnp.float32), jnp.zeros((D,), jnp.float32), jnp.zeros((D,), jnp.float32))
    (d_w_out, d_bn_bias, d_bn_gain), (out_blocks, d_bn_blocks) = lax.scan(tail_step, start_carry, block_ids)
    outputs = out_blocks.reshape(UTT, FRAMES, D)
    mean_grad = bn_gain * d_bn_bias / frame_total
    mean_cross = bn_gain * d_bn_gain / frame_total

    def make_dconv(pair):
        index, d_bn = pair
        normed_bn, bn_out, window = bn_forward(index)
        return bn_rstd * (d_bn * bn_gain - mean_grad - normed_bn * mean_cross)
    d_conv_blocks = lax.map(make_dconv, (block_ids, d_bn_blocks))
    grad_padded = jnp.pad(d_conv_blocks.reshape(UTT, FRAMES, D), ((0, 0), (16, 16), (0, 0)))

    def back_step(kernel_acc, pair):
        index, d_conv = pair
        utt_index, start = locate(index)
        window = frame_slice(padded, utt_index, start, block_len + 32).astype(jnp.float32)
        kernel_rows = []
        for tap_index in range(K):
            kernel_rows.append(lax.optimization_barrier(jnp.sum(window[tap_index + 1:tap_index + 1 + block_len] * d_conv, axis=0)))
        kernel_acc = kernel_acc + jnp.stack(kernel_rows)
        grad_window = frame_slice(grad_padded, utt_index, start, block_len + 32)
        d_gated = jnp.zeros((block_len, D), jnp.float32)
        for tap_index in range(K):
            d_gated = d_gated + kernel[tap_index] * grad_window[31 - tap_index:31 - tap_index + block_len]
        x_float, ln_hat, ln_rstd, value_half, gate_sig = front(index)
        d_value = d_gated * gate_sig
        d_gate = d_gated * value_half * gate_sig * (1.0 - gate_sig)
        d_proj = jnp.concatenate([d_value, d_gate], axis=-1).astype(jnp.bfloat16)
        d_normed = lax.dot_general(d_proj, w_in, (((1,), (1,)), ((), ())), preferred_element_type=jnp.float32)
        d_hat = d_normed * ln_gain
        d_layer = ln_rstd * (d_hat - lax.optimization_barrier(jnp.mean(d_hat, axis=-1, keepdims=True)) - ln_hat * lax.optimization_barrier(jnp.mean(d_hat * ln_hat, axis=-1, keepdims=True)))
        cot_float = frame_slice(cotangent, utt_index, start, block_len).astype(jnp.float32)
        return (kernel_acc, (cot_float + d_layer).astype(jnp.bfloat16))
    d_kernel, grad_blocks = lax.scan(back_step, jnp.zeros((K, D), jnp.float32), (block_ids, d_conv_blocks))
    d_inputs = grad_blocks.reshape(UTT, FRAMES, D)
    return (outputs, d_inputs, d_w_out, d_kernel, d_bn_gain, d_bn_bias)
```

```python
import functools

import jax
import jax.numpy as jnp
from jax import lax
from jax.experimental import pallas as pl
from jax.experimental.pallas import tpu as pltpu
from jax.sharding import PartitionSpec as P

EPSILON = 1e-05
BF = jnp.bfloat16
F32 = jnp.float32
LANES = 128
PAD = 16
MIB = 1 << 20


def params(mib):
    return pltpu.CompilerParams(
        vmem_limit_bytes=mib * MIB, dimension_semantics=("arbitrary",)
    )


def resident(shape):
    return pl.BlockSpec(shape, lambda j: (0,) * len(shape))


def columns(shape, width):
    return pl.BlockSpec(shape[:-1] + (width,), lambda j: (0,) * (len(shape) - 1) + (j,))


def front_body(x_ref, gain_ref, wv_ref, wg_ref, gated_ref, p_ref, q_ref, normed_ref):
    rows, d = x_ref.shape

    @pl.when(pl.program_id(0) == 0)
    def _():
        def step(i, _):
            r = pl.multiple_of(i * 16, 16)
            x = x_ref[pl.ds(r, 16), :].astype(F32)
            mu = jnp.sum(x, axis=-1, keepdims=True) * (1.0 / d)
            c = x - mu
            var = jnp.sum(c * c, axis=-1, keepdims=True) * (1.0 / d)
            hat = c * lax.rsqrt(var + EPSILON)
            normed_ref[pl.ds(r, 16), :] = (hat * gain_ref[...]).astype(BF)
            return 0

        lax.fori_loop(0, rows // 16, step, 0, unroll=4)

    value = jnp.dot(normed_ref[...], wv_ref[...], preferred_element_type=F32)
    gate = jnp.dot(normed_ref[...], wg_ref[...], preferred_element_type=F32)
    sig = jax.nn.sigmoid(gate)
    gated = value * sig
    gated_ref[...] = gated.astype(BF)
    p_ref[...] = sig.astype(BF)
    q_ref[...] = (gated * (1.0 - sig)).astype(BF)


def front(x, gain, w_in):
    rows, d = x.shape
    cw = 256
    steps = d // cw
    out = jax.ShapeDtypeStruct((rows, d), BF)
    return pl.pallas_call(
        front_body,
        grid=(steps,),
        in_specs=[
            resident((rows, d)),
            resident((1, d)),
            pl.BlockSpec((d, cw), lambda j: (0, j)),
            pl.BlockSpec((d, cw), lambda j: (0, j + steps)),
        ],
        out_specs=[columns((rows, d), cw)] * 3,
        out_shape=[out] * 3,
        scratch_shapes=[pltpu.VMEM((rows, d), BF)],
        compiler_params=params(32),
        cost_estimate=pl.CostEstimate(
            flops=4 * rows * d * d, bytes_accessed=4 * d * d + 8 * rows * d, transcendentals=rows * d
        ),
        name="front",
    )(x, gain, w_in, w_in)


def conv_body(g_ref, lo_ref, hi_ref, k_ref, conv_ref, sums_ref, pad_ref):
    utt, frames, cw = g_ref.shape
    taps = k_ref.shape[0]
    block = 64
    for l in range(cw // LANES):
        lanes = slice(l * LANES, (l + 1) * LANES)
        for u in range(utt):
            pad_ref[u, 0:PAD, :] = lo_ref[u, :, lanes].astype(F32)
            pad_ref[u, PAD : PAD + frames, :] = g_ref[u, :, lanes].astype(F32)
            pad_ref[u, PAD + frames : PAD + frames + PAD, :] = hi_ref[u, :, lanes].astype(F32)
            pad_ref[u, 2 * PAD + frames :, :] = jnp.zeros((8, LANES), F32)
        per = frames // block

        def step(i, carry):
            first, square = carry
            u = i // per
            base = pl.multiple_of((i % per) * block, block)
            acc = jnp.zeros((block, LANES), F32)
            for r in range(8):
                w = pad_ref[u, pl.ds(base + r + 1, block + taps - 8), :]
                for q in range(taps // 8):
                    acc = acc + k_ref[8 * q + r, lanes][None, :] * w[8 * q : 8 * q + block]
            conv_ref[u, pl.ds(base, block), lanes] = acc
            part = acc.reshape(block // 8, 8, LANES)
            return first + jnp.sum(part, axis=0), square + jnp.sum(part * part, axis=0)

        zero = jnp.zeros((8, LANES), F32)
        first, square = lax.fori_loop(0, utt * per, step, (zero, zero))
        sums_ref[0:1, lanes] = jnp.sum(first, axis=0, keepdims=True)
        sums_ref[1:2, lanes] = jnp.sum(square, axis=0, keepdims=True)


def conv(gated, lo, hi, kernel):
    utt, frames, d = gated.shape
    cw = 256
    return pl.pallas_call(
        conv_body,
        grid=(d // cw,),
        in_specs=[
            columns(gated.shape, cw),
            columns(lo.shape, cw),
            columns(hi.shape, cw),
            columns(kernel.shape, cw),
        ],
        out_specs=[columns(gated.shape, cw), columns((2, d), cw)],
        out_shape=[
            jax.ShapeDtypeStruct(gated.shape, F32),
            jax.ShapeDtypeStruct((2, d), F32),
        ],
        scratch_shapes=[pltpu.VMEM((utt, frames + 2 * PAD + 8, LANES), F32)],
        compiler_params=params(32),
        cost_estimate=pl.CostEstimate(
            flops=64 * gated.size, bytes_accessed=6 * gated.size, transcendentals=0
        ),
        name="conv",
    )(gated, lo, hi, kernel)


def middle_body(
    n, total, me_ref, conv_ref, sums_ref, gain_ref, bias_ref, cot_ref, w_ref,
    act_ref, dbn_ref, dsums_ref, dw_ref, cot_t, dw_s,
):
    rows, d = cot_ref.shape
    me = me_ref[0]

    @pl.when(pl.program_id(0) == 0)
    def _():
        cot_t[...] = cot_ref[...].T

    mean = sums_ref[0:1, :] * (1.0 / total)
    var = sums_ref[1:2, :] * (1.0 / total) - mean * mean
    rstd = lax.rsqrt(var + EPSILON)
    xhat = (conv_ref[...] - mean) * rstd
    out = xhat * gain_ref[...] + bias_ref[...]
    sig = jax.nn.sigmoid(out)
    act = out * sig
    act_bf = act.astype(BF)
    act_ref[...] = act_bf
    dw = jnp.dot(cot_t[...], act_bf, preferred_element_type=F32)
    if dw_s is None:
        dw_ref[...] = dw
    else:
        dw_s[...] = dw.astype(BF).reshape(dw_s.shape)
        for j in range(n):
            dw_ref[j] = dw_s[lax.bitwise_xor(me, j)]
    d_act = jnp.dot(cot_ref[...], w_ref[...], preferred_element_type=F32)
    dbn = d_act * (sig + act * (1.0 - sig))
    dbn_ref[...] = dbn
    dsums_ref[0:1, :] = jnp.sum(dbn, axis=0, keepdims=True)
    dsums_ref[1:2, :] = jnp.sum(dbn * xhat, axis=0, keepdims=True)


def middle(n, total, me, conv_out, sums, gain, bias, cot, w_out, by_owner):
    rows, d = cot.shape
    cw = 256
    if by_owner:
        dw_shape, dw_type = (n, d // n, d), BF
        scratch = [pltpu.VMEM((d, rows), BF), pltpu.VMEM((n, d // n, cw), BF)]
        body = functools.partial(middle_body, n, total)
    else:
        dw_shape, dw_type = (d, d), F32
        scratch = [pltpu.VMEM((d, rows), BF)]
        body = lambda *refs: middle_body(n, total, *refs, None)
    return pl.pallas_call(
        body,
        grid=(d // cw,),
        in_specs=[
            pl.BlockSpec(memory_space=pltpu.SMEM),
            columns((rows, d), cw),
            columns((2, d), cw),
            columns((1, d), cw),
            columns((1, d), cw),
            resident((rows, d)),
            columns((d, d), cw),
        ],
        out_specs=[
            columns((rows, d), cw),
            columns((rows, d), cw),
            columns((2, d), cw),
            columns(dw_shape, cw),
        ],
        out_shape=[
            jax.ShapeDtypeStruct((rows, d), BF),
            jax.ShapeDtypeStruct((rows, d), F32),
            jax.ShapeDtypeStruct((2, d), F32),
            jax.ShapeDtypeStruct(dw_shape, dw_type),
        ],
        scratch_shapes=scratch,
        compiler_params=params(40),
        cost_estimate=pl.CostEstimate(
            flops=4 * rows * d * d, bytes_accessed=4 * d * d + 12 * rows * d, transcendentals=rows * d
        ),
        name="middle",
    )(me, conv_out, sums, gain, bias, cot, w_out)


def branch_body(x_ref, act_ref, w_ref, out_ref):
    branch = lax.dot_general(
        act_ref[...], w_ref[...], (((1,), (1,)), ((), ())), preferred_element_type=F32
    )
    out_ref[...] = (x_ref[...].astype(F32) + branch).astype(BF)


def branch(x, act, w_out):
    rows, d = x.shape
    cw = 256
    return pl.pallas_call(
        branch_body,
        grid=(d // cw,),
        in_specs=[
            columns((rows, d), cw),
            resident((rows, d)),
            pl.BlockSpec((cw, d), lambda j: (j, 0)),
        ],
        out_specs=columns((rows, d), cw),
        out_shape=jax.ShapeDtypeStruct((rows, d), BF),
        compiler_params=params(24),
        cost_estimate=pl.CostEstimate(
            flops=2 * rows * d * d, bytes_accessed=2 * d * d + 6 * rows * d, transcendentals=0
        ),
        name="branch",
    )(x, act, w_out)


def back_conv_body(
    total, edge_ref, dbn_ref, conv_ref, dlo_ref, dhi_ref, clo_ref, chi_ref, sums_ref, dsums_ref,
    gain_ref, k_ref, g_ref, p_ref, q_ref, dk_ref, dv_ref, dg_ref, pad_ref, kacc_ref,
):
    utt, frames, cw = g_ref.shape
    taps = k_ref.shape[0]
    block = 64
    per = frames // block
    mean = sums_ref[0:1, :] * (1.0 / total)
    var = sums_ref[1:2, :] * (1.0 / total) - mean * mean
    rstd = lax.rsqrt(var + EPSILON)
    gain = gain_ref[...]
    a = rstd * gain
    b = a * rstd * (dsums_ref[1:2, :] * (1.0 / total))
    mean_grad = a * (dsums_ref[0:1, :] * (1.0 / total))
    keep_lo = edge_ref[0]
    keep_hi = edge_ref[1]
    for l in range(cw // LANES):
        lanes = slice(l * LANES, (l + 1) * LANES)
        al, bl, ml, meanl = a[:, lanes], b[:, lanes], mean_grad[:, lanes], mean[:, lanes]

        def d_conv(dbn, conv):
            return dbn.astype(F32) * al - ml - (conv.astype(F32) - meanl) * bl

        for u in range(utt):
            pad_ref[u, 0:PAD, :] = d_conv(dlo_ref[u, :, lanes], clo_ref[u, :, lanes]) * keep_lo
            pad_ref[u, PAD : PAD + frames, :] = d_conv(dbn_ref[u, :, lanes], conv_ref[u, :, lanes])
            pad_ref[u, PAD + frames : PAD + frames + PAD, :] = (
                d_conv(dhi_ref[u, :, lanes], chi_ref[u, :, lanes]) * keep_hi
            )
        kacc_ref[...] = jnp.zeros(kacc_ref.shape, F32)

        def step(i, _):
            u = i // per
            base = pl.multiple_of((i % per) * block, block)
            g = g_ref[u, pl.ds(base, block), lanes].astype(F32)
            acc = jnp.zeros((block, LANES), F32)
            for r in range(8):
                w = pad_ref[u, pl.ds(base + r, block + taps - 8), :]
                for q in range(taps // 8):
                    tap = taps - 1 - (8 * q + r)
                    part = w[8 * q : 8 * q + block]
                    acc = acc + k_ref[tap, lanes][None, :] * part
                    prod = (g * part).reshape(block // 8, 8, LANES)
                    kacc_ref[tap] += jnp.sum(prod, axis=0)
            dv_ref[u, pl.ds(base, block), lanes] = (
                acc * p_ref[u, pl.ds(base, block), lanes].astype(F32)
            ).astype(BF)
            dg_ref[u, pl.ds(base, block), lanes] = (
                acc * q_ref[u, pl.ds(base, block), lanes].astype(F32)
            ).astype(BF)
            return 0

        lax.fori_loop(0, utt * per, step, 0)
        dk_ref[:, lanes] = jnp.sum(kacc_ref[...], axis=1)


def back_conv(total, edge, dbn, conv_out, halos, sums, dsums, gain, kernel, gated, p, q):
    utt, frames, d = gated.shape
    cw = 256
    taps = kernel.shape[0]
    full = columns(gated.shape, cw)
    halo = columns((utt, PAD, d), cw)
    return pl.pallas_call(
        functools.partial(back_conv_body, total),
        grid=(d // cw,),
        in_specs=[pl.BlockSpec(memory_space=pltpu.SMEM), full, full, halo, halo, halo, halo]
        + [columns((2, d), cw), columns((2, d), cw), columns((1, d), cw), columns(kernel.shape, cw)]
        + [full, full, full],
        out_specs=[columns(kernel.shape, cw), full, full],
        out_shape=[
            jax.ShapeDtypeStruct(kernel.shape, F32),
            jax.ShapeDtypeStruct(gated.shape, BF),
            jax.ShapeDtypeStruct(gated.shape, BF),
        ],
        scratch_shapes=[
            pltpu.VMEM((utt, frames + 2 * PAD, LANES), F32),
            pltpu.VMEM((taps, 8, LANES), F32),
        ],
        compiler_params=params(32),
        cost_estimate=pl.CostEstimate(
            flops=128 * gated.size, bytes_accessed=18 * gated.size, transcendentals=0
        ),
        name="back_conv",
    )(edge, dbn, conv_out, *halos, sums, dsums, gain, kernel, gated, p, q)


def back_norm_body(x_ref, cot_ref, gain_ref, dv_ref, dg_ref, wv_ref, wg_ref, out_ref, acc_ref):
    rows, d = x_ref.shape
    j = pl.program_id(0)
    dims = (((1,), (1,)), ((), ()))
    part = lax.dot_general(dv_ref[...], wv_ref[...], dims, preferred_element_type=F32)
    part += lax.dot_general(dg_ref[...], wg_ref[...], dims, preferred_element_type=F32)

    @pl.when(j == 0)
    def _():
        acc_ref[...] = part

    @pl.when(j > 0)
    def _():
        acc_ref[...] += part

    @pl.when(j == pl.num_programs(0) - 1)
    def _():
        def step(i, _):
            r = pl.multiple_of(i * 16, 16)
            x = x_ref[pl.ds(r, 16), :].astype(F32)
            mu = jnp.sum(x, axis=-1, keepdims=True) * (1.0 / d)
            c = x - mu
            var = jnp.sum(c * c, axis=-1, keepdims=True) * (1.0 / d)
            rstd = lax.rsqrt(var + EPSILON)
            hat = c * rstd
            dh = acc_ref[pl.ds(r, 16), :] * gain_ref[...]
            m1 = jnp.sum(dh, axis=-1, keepdims=True) * (1.0 / d)
            m2 = jnp.sum(dh * hat, axis=-1, keepdims=True) * (1.0 / d)
            layer = rstd * (dh - m1 - hat * m2)
            out_ref[pl.ds(r, 16), :] = (cot_ref[pl.ds(r, 16), :].astype(F32) + layer).astype(BF)
            return 0

        lax.fori_loop(0, rows // 16, step, 0, unroll=2)


def back_norm(x, cot, gain, dv, dg, w_in):
    rows, d = x.shape
    cw = 256
    steps = d // cw
    return pl.pallas_call(
        back_norm_body,
        grid=(steps,),
        in_specs=[
            resident((rows, d)),
            resident((rows, d)),
            resident((1, d)),
            columns((rows, d), cw),
            columns((rows, d), cw),
            pl.BlockSpec((d, cw), lambda j: (0, j)),
            pl.BlockSpec((d, cw), lambda j: (0, j + steps)),
        ],
        out_specs=resident((rows, d)),
        out_shape=jax.ShapeDtypeStruct((rows, d), BF),
        scratch_shapes=[pltpu.VMEM((rows, d), F32)],
        compiler_params=params(40),
        cost_estimate=pl.CostEstimate(
            flops=4 * rows * d * d, bytes_accessed=4 * d * d + 10 * rows * d, transcendentals=0
        ),
        name="back_norm",
    )(x, cot, gain, dv, dg, w_in, w_in)


def swap(block, axis, bit):
    count = lax.axis_size(axis)
    return lax.ppermute(block, axis, [(i, i ^ bit) for i in range(count)])


def is_power(count):
    return count & (count - 1) == 0


def all_sum(block, axis, wire=None):
    count = lax.axis_size(axis)
    if not is_power(count):
        return lax.psum(block, axis)
    bit = 1
    while bit < count:
        if wire is not None:
            block = block.astype(wire)
        other = swap(block, axis, bit)
        block = block.astype(F32) + other.astype(F32)
        bit *= 2
    return block


def neighbours(block, axis, width):
    count = lax.axis_size(axis)
    up = [(i, i + 1) for i in range(count - 1)]
    down = [(i + 1, i) for i in range(count - 1)]
    low = lax.ppermute(block[:, -width:], axis, up)
    high = lax.ppermute(block[:, :width], axis, down)
    return low, high


def scatter_sum(parts, axis):
    count = parts.shape[0]
    wide = parts.shape[2] // 2
    bits = [1 << s for s in range(count.bit_length() - 1)]
    if len(bits) >= 3:
        orders = [bits, [bits[0], bits[2], bits[1]] + bits[3:]]
    else:
        orders = [bits, bits]
    held = [parts[:, :, :wide], parts[:, :, wide:]]
    labels = [list(range(count)), list(range(count))]
    for step in range(len(bits)):
        for h in range(2):
            bit = orders[h][step]
            keep = [i for i, j in enumerate(labels[h]) if not j & bit]
            send = [i for i, j in enumerate(labels[h]) if j & bit]
            block = held[h]
            size = len(labels[h])
            stride = 1
            while not labels[h][stride] & bit:
                stride *= 2
            shaped = block.reshape((size // (2 * stride), 2, stride) + block.shape[1:])
            mine = shaped[:, 0].reshape((size // 2,) + block.shape[1:])
            theirs = shaped[:, 1].reshape((size // 2,) + block.shape[1:])
            got = swap(theirs, axis, bit)
            total = mine.astype(F32) + got.astype(F32)
            held[h] = total if step == len(bits) - 1 else total.astype(BF)
            labels[h] = [labels[h][i] for i in keep]
    return jnp.concatenate([held[0][0], held[1][0]], axis=-1)


def on_device(inputs, ln_gain, w_in, kernel, bn_gain, bn_bias, w_out, cotangent):
    axis = "seq"
    n = lax.axis_size(axis)
    me = lax.axis_index(axis)
    utt, frames, d = inputs.shape
    rows = utt * frames
    total = rows * n
    x = inputs.reshape(rows, d)
    cot = cotangent.reshape(rows, d)
    ln_row, gain_row, bias_row = ln_gain[None], bn_gain[None], bn_bias[None]
    by_owner = is_power(n) and d % n == 0 and (d // n) % 16 == 0

    gated, p, q = front(x, ln_row, w_in)
    gated = gated.reshape(inputs.shape)
    lo, hi = neighbours(gated, axis, PAD)
    conv_out, sums = conv(gated, lo, hi, kernel)
    clo, chi = neighbours(conv_out.astype(BF), axis, PAD)
    sums = all_sum(sums, axis)

    act, dbn, dsums, dw = middle(
        n, total, me.reshape(1).astype(jnp.int32), conv_out.reshape(rows, d), sums, gain_row,
        bias_row, cot, w_out, by_owner,
    )
    dbn = dbn.reshape(inputs.shape)
    dlo, dhi = neighbours(dbn.astype(BF), axis, PAD)
    dsums = all_sum(dsums, axis)
    if by_owner:
        d_w_out = scatter_sum(dw, axis)
    else:
        d_w_out = lax.psum_scatter(dw, axis, scatter_dimension=0, tiled=True)
    outputs = branch(x, act, w_out)

    edge = jnp.stack([me > 0, me < n - 1]).astype(F32)
    d_kernel, dv, dg = back_conv(
        total, edge, dbn, conv_out, (dlo, dhi, clo, chi), sums, dsums, gain_row, kernel, gated,
        p.reshape(inputs.shape), q.reshape(inputs.shape),
    )
    d_kernel = all_sum(d_kernel, axis, BF)
    d_inputs = back_norm(x, cot, ln_row, dv.reshape(rows, d), dg.reshape(rows, d), w_in)
    return (
        outputs.reshape(inputs.shape), d_inputs.reshape(inputs.shape), d_w_out, d_kernel,
        dsums[1], dsums[0],
    )


def solution(mesh):
    return jax.shard_map(
        on_device,
        mesh=mesh,
        in_specs=(P(None, "seq", None), P(), P(), P(), P(), P(), P(), P(None, "seq", None)),
        out_specs=(P(None, "seq", None), P(None, "seq", None), P("seq", None), P(), P(), P()),
        check_vma=False,
    )
```

```python
import functools

import jax
import jax.numpy as jnp
from jax import lax
from jax.experimental import pallas as pl
from jax.experimental.pallas import tpu as pltpu
from jax.sharding import PartitionSpec as P

EPSILON = 1e-05
BF = jnp.bfloat16
F32 = jnp.float32
LANES = 128
PAD = 16
MIB = 1 << 20
VMEM_MIB = 8


def params(mib):
    return pltpu.CompilerParams(vmem_limit_bytes=mib * MIB)


WHOLE = pl.BlockSpec(memory_space=pltpu.VMEM)
SCALARS = pl.BlockSpec(memory_space=pltpu.SMEM)
ANYWHERE = pl.BlockSpec(memory_space=pl.ANY)
CW = 256


def cost(micros):
    return pl.CostEstimate(flops=0, bytes_accessed=int(micros * 3.0e6), transcendentals=0)


def shape(dims, dtype):
    return jax.ShapeDtypeStruct(dims, dtype)


def near(dims, dtype):
    return pltpu.VMEM(dims, dtype)


def turn_body(place_ref, cot_ref, *rest):
    mine_ref, other_ref, held_ref = rest[-3:]
    blocks = mine_ref.shape[0]
    per = mine_ref.shape[1]
    held_ref[...] = cot_ref[...].T
    core = place_ref[0]
    half = place_ref[1]

    def step(j, _):
        row = pl.multiple_of(lax.bitwise_xor(half, j) * (2 * per), 2 * per)
        mine_ref[j] = held_ref[pl.ds(pl.multiple_of(row + core * per, per), per), :]
        other_ref[j] = held_ref[pl.ds(pl.multiple_of(row + (1 - core) * per, per), per), :]
        return 0

    lax.fori_loop(0, blocks, step, 0, unroll=2)


def turn(n, place, cot, after):
    rows, d = cot.shape
    out = shape((n // 2, d // n, rows), BF)
    return pl.pallas_call(
        turn_body,
        in_specs=[SCALARS, WHOLE] + [ANYWHERE] * len(after),
        out_specs=[WHOLE] * 2,
        out_shape=[out] * 2,
        scratch_shapes=[pltpu.VMEM((d, rows), BF)],
        compiler_params=params(VMEM_MIB),
        cost_estimate=cost(2),
        name="turn",
    )(place, cot, *after)


def edges_out(odd, first, last, a_ref, b_ref):
    @pl.when(odd == 0)
    def _():
        a_ref[...] = last
        b_ref[...] = first

    @pl.when(odd != 0)
    def _():
        a_ref[...] = first
        b_ref[...] = last


def front_body(
    utt, place_ref, x_hbm, vec_ref, w_hbm,
    gated_ref, p_ref, q_ref, hat_ref, rstd_ref, a_ref, b_ref, normed_ref, x_ref, w_ref, x_sem, w_sem,
):
    rows, d = x_ref.shape
    frames = rows // utt
    pieces = x_sem.shape[0]
    span = rows // pieces
    steps = d // CW

    def x_copy(i):
        at = pl.ds(i * span, span)
        return pltpu.make_async_copy(x_hbm.at[at], x_ref.at[at], x_sem.at[i])

    def w_copy(j, half):
        at = pl.ds(half * d + j * CW, CW)
        return pltpu.make_async_copy(w_hbm.at[:, at], w_ref.at[:, at], w_sem.at[j, half])

    for i in range(pieces):
        x_copy(i).start()
    for j in range(steps):
        for half in range(2):
            w_copy(j, half).start()

    for i in range(pieces):
        x_copy(i).wait()

        for k in range(i * span, (i + 1) * span, 16):
            at = slice(k, k + 16)
            x = x_ref[at, :].astype(F32)
            mu = jnp.sum(x, axis=-1, keepdims=True) * (1.0 / d)
            c = x - mu
            var = jnp.sum(c * c, axis=-1, keepdims=True) * (1.0 / d)
            rstd = lax.rsqrt(var + EPSILON)
            hat = c * rstd
            rstd_ref[at, :] = rstd
            hat_ref[at, :] = hat.astype(BF)
            normed_ref[at, :] = (hat * vec_ref[0:1, :]).astype(BF)

    odd = place_ref[0] != 0
    for j in range(steps):
        cols = slice(j * CW, (j + 1) * CW)
        for half in range(2):
            w_copy(j, half).wait()
        value = jnp.dot(normed_ref[...], w_ref[:, cols], preferred_element_type=F32)
        gate = jnp.dot(
            normed_ref[...], w_ref[:, d + j * CW : d + (j + 1) * CW], preferred_element_type=F32
        )
        sig = jax.nn.sigmoid(gate)
        gated = value * sig
        held = gated.astype(BF)
        gated_ref[:, cols] = held
        p_ref[:, cols] = sig.astype(BF)
        q_ref[:, cols] = (gated * (1.0 - sig)).astype(BF)
        shaped = held.reshape(utt, frames, CW)
        first, last = shaped[:, :PAD], shaped[:, frames - PAD :]
        a_ref[:, :, cols] = jnp.where(odd, first, last)
        b_ref[:, :, cols] = jnp.where(odd, last, first)


def front(utt, place, x, vec, w_in):
    rows, d = x.shape
    out = near((rows, d), BF)
    edge = shape((utt, PAD, d), BF)
    return pl.pallas_call(
        functools.partial(front_body, utt),
        in_specs=[SCALARS, ANYWHERE, WHOLE, ANYWHERE],
        out_specs=[WHOLE] * 7,
        out_shape=[out] * 4 + [near((rows, 1), F32)] + [edge] * 2,
        scratch_shapes=[
            pltpu.VMEM((rows, d), BF),
            pltpu.VMEM((rows, d), BF),
            pltpu.VMEM((d, 2 * d), BF),
            pltpu.SemaphoreType.DMA((4,)),
            pltpu.SemaphoreType.DMA((d // CW, 2)),
        ],
        compiler_params=params(52),
        cost_estimate=cost(10),
        name="front",
    )(place, x, vec, w_in)


def lane_groups(first, last, work):
    def step(i, _):
        for slot in range(2):
            group = 2 * i + slot
            work(group, pl.ds(pl.multiple_of(group * LANES, LANES), LANES), slot)
        return 0

    lax.fori_loop(first // (2 * LANES), last // (2 * LANES), step, 0)


def conv_body(utt, place_ref, g_ref, a_ref, b_ref, k_ref, conv_ref, sums_ref, pad_ref):
    d = g_ref.shape[1]
    frames = g_ref.shape[0] // utt
    taps = k_ref.shape[0]
    block = 64
    odd = place_ref[0] != 0

    def work(_, lanes, slot):
        first = square = jnp.zeros((8, LANES), F32)
        for u in range(utt):
            a = a_ref[u, :, lanes].astype(F32)
            b = b_ref[u, :, lanes].astype(F32)
            pad_ref[slot, u, 0:PAD, :] = jnp.where(odd, a, b)
            rows = slice(u * frames, (u + 1) * frames)
            pad_ref[slot, u, PAD : PAD + frames, :] = g_ref[rows, lanes].astype(F32)
            pad_ref[slot, u, PAD + frames : PAD + frames + PAD, :] = jnp.where(odd, b, a)
            for base in range(0, frames, block):
                acc = jnp.zeros((block, LANES), F32)
                for r in range(8):
                    w = pad_ref[slot, u, base + r + 1 : base + r + 1 + block + taps - 8, :]
                    for q in range(taps // 8):
                        tap = 8 * q + r
                        acc = acc + k_ref[tap : tap + 1, lanes] * w[8 * q : 8 * q + block]
                conv_ref[u * frames + base : u * frames + base + block, lanes] = acc
                part = acc.reshape(block // 8, 8, LANES)
                first = first + jnp.sum(part, axis=0)
                square = square + jnp.sum(part * part, axis=0)
        sums_ref[0:1, lanes] = jnp.sum(first, axis=0, keepdims=True)
        sums_ref[1:2, lanes] = jnp.sum(square, axis=0, keepdims=True)

    lane_groups(0, d, work)


def conv(utt, place, gated, a, b, kernel):
    rows, d = gated.shape
    frames = rows // utt
    return pl.pallas_call(
        functools.partial(conv_body, utt),
        in_specs=[SCALARS] + [WHOLE] * 4,
        out_specs=[WHOLE] * 2,
        out_shape=[near(gated.shape, F32), shape((2, d), F32)],
        scratch_shapes=[pltpu.VMEM((2, utt, frames + 2 * PAD + 8, LANES), F32)],
        compiler_params=params(VMEM_MIB),
        cost_estimate=cost(7),
        name="conv",
    )(place, gated, a, b, kernel)


def middle_body(
    utt, total, place_ref, conv_ref, sums_ref, vec_ref, cot_ref, w_ref,
    *rest,
):
    act_ref, dbn_ref, dsums_ref, a_ref, b_ref = rest[-5:]
    rows, d = conv_ref.shape
    frames = rows // utt
    odd = place_ref[0] != 0
    for j in range(d // CW):
        cols = slice(j * CW, (j + 1) * CW)
        mean = sums_ref[0:1, cols] * (1.0 / total)
        var = sums_ref[1:2, cols] * (1.0 / total) - mean * mean
        rstd = lax.rsqrt(var + EPSILON)
        conv = conv_ref[:, cols]
        xhat = (conv - mean) * rstd
        out = xhat * vec_ref[1:2, cols] + vec_ref[2:3, cols]
        sig = jax.nn.sigmoid(out)
        act = out * sig
        act_ref[:, cols] = act.astype(BF)
        d_act = jnp.dot(cot_ref[...], w_ref[:, cols], preferred_element_type=F32)
        dbn = d_act * (sig + act * (1.0 - sig))
        dbn_ref[:, cols] = dbn
        dsums_ref[0:1, cols] = jnp.sum(dbn, axis=0, keepdims=True)
        dsums_ref[1:2, cols] = jnp.sum(dbn * xhat, axis=0, keepdims=True)
        for u in range(utt):
            low = slice(u * frames, u * frames + PAD)
            high = slice((u + 1) * frames - PAD, (u + 1) * frames)
            for at, piece in ((slice(0, PAD), dbn), (slice(PAD, 2 * PAD), conv)):
                first, last = piece[low].astype(BF), piece[high].astype(BF)
                a_ref[u, at, cols] = jnp.where(odd, first, last)
                b_ref[u, at, cols] = jnp.where(odd, last, first)


def middle(utt, total, place, conv_out, sums, vec, cot, w_out, after):
    rows, d = cot.shape
    edge = shape((utt, 2 * PAD, d), BF)
    return pl.pallas_call(
        functools.partial(middle_body, utt, total),
        in_specs=[SCALARS] + [WHOLE] * 5 + [ANYWHERE] * len(after),
        out_specs=[WHOLE] * 5,
        out_shape=[shape((rows, d), BF), near((rows, d), F32), shape((2, d), F32), edge, edge],
        compiler_params=params(VMEM_MIB),
        cost_estimate=cost(4),
        name="middle",
    )(place, conv_out, sums, vec, cot, w_out, *after)


def grad_body(bits, ca_ref, cb_ref, acta_ref, actb_ref, *rest):
    out_refs = rest[-4:]
    blocks, per, rows = ca_ref.shape
    half = out_refs[0].shape[-1]
    ca = ca_ref[...].reshape(blocks * per, rows)
    cb = cb_ref[...].reshape(blocks * per, rows)
    for side, bit in enumerate(bits):
        send_ref, keep_ref = out_refs[2 * side], out_refs[2 * side + 1]
        for c in range(half // CW):
            cols = slice(c * CW, (c + 1) * CW)
            src = slice(side * half + c * CW, side * half + (c + 1) * CW)
            dw = jnp.dot(ca, acta_ref[:, src], preferred_element_type=F32)
            dw += jnp.dot(cb, actb_ref[:, src], preferred_element_type=F32)
            sent = kept = 0
            for j in range(blocks):
                block = dw[j * per : (j + 1) * per]
                if j & bit:
                    send_ref[sent, :, cols] = block.astype(BF)
                    sent += 1
                else:
                    keep_ref[kept, :, cols] = block
                    kept += 1


def grad(bits, cot_a, cot_b, act_a, act_b, after):
    blocks, per, _ = cot_a.shape
    d = act_a.shape[1]
    half = (blocks // 2, per, d // 2)
    return pl.pallas_call(
        functools.partial(grad_body, bits),
        in_specs=[WHOLE] * 4 + [ANYWHERE] * len(after),
        out_specs=[WHOLE] * 4,
        out_shape=[shape(half, BF), shape(half, F32)] * 2,
        compiler_params=params(VMEM_MIB),
        cost_estimate=cost(3.5),
        name="grad",
    )(cot_a, cot_b, act_a, act_b, *after)


def branch_body(x_ref, act_ref, w_ref, *rest):
    out_ref = rest[-1]
    for j in range(out_ref.shape[-1] // CW):
        cols = slice(j * CW, (j + 1) * CW)
        part = lax.dot_general(
            act_ref[...], w_ref[cols, :], (((1,), (1,)), ((), ())), preferred_element_type=F32
        )
        out_ref[:, cols] = (x_ref[:, cols].astype(F32) + part).astype(BF)


def branch(x, act, w_out, after):
    rows, d = x.shape
    return pl.pallas_call(
        branch_body,
        in_specs=[WHOLE] * 3 + [ANYWHERE] * len(after),
        out_specs=WHOLE,
        out_shape=shape((rows, d), BF),
        compiler_params=params(VMEM_MIB),
        cost_estimate=cost(4),
        name="branch",
    )(x, act, w_out, *after)


def grad_taps_body(
    utt, total, place_ref, dbn_ref, conv_ref, a_ref, b_ref, sums_ref, dsums_ref, vec_ref, g_ref,
    dk_ref, dc_ref, acc_ref,
):
    d = g_ref.shape[1]
    frames = g_ref.shape[0] // utt
    taps = dk_ref.shape[0]
    block = 64
    odd = place_ref[0] != 0
    keep_lo = place_ref[2].astype(F32)
    keep_hi = place_ref[3].astype(F32)

    def work(group, lanes, slot):
        mean = sums_ref[0:1, lanes] * (1.0 / total)
        var = sums_ref[1:2, lanes] * (1.0 / total) - mean * mean
        rstd = lax.rsqrt(var + EPSILON)
        scale = rstd * vec_ref[1:2, lanes]
        cross = scale * rstd * (dsums_ref[1:2, lanes] * (1.0 / total))
        mean_grad = scale * (dsums_ref[0:1, lanes] * (1.0 / total))

        def d_conv(dbn, conv):
            return dbn.astype(F32) * scale - mean_grad - (conv.astype(F32) - mean) * cross

        for u in range(utt):
            a = d_conv(a_ref[u, :PAD, lanes], a_ref[u, PAD:, lanes])
            b = d_conv(b_ref[u, :PAD, lanes], b_ref[u, PAD:, lanes])
            rows = slice(u * frames, (u + 1) * frames)
            dc_ref[group, u, 0:PAD, :] = jnp.where(odd, a, b) * keep_lo
            dc_ref[group, u, PAD : PAD + frames, :] = d_conv(dbn_ref[rows, lanes], conv_ref[rows, lanes])
            dc_ref[group, u, PAD + frames : PAD + frames + PAD, :] = jnp.where(odd, b, a) * keep_hi
            for base in range(0, frames, block):
                g = g_ref[u * frames + base : u * frames + base + block, lanes].astype(F32)
                for r in range(8):
                    w = dc_ref[group, u, base + r : base + r + block + taps - 8, :]
                    for q in range(taps // 8):
                        tap = taps - 1 - (8 * q + r)
                        prod = g * w[8 * q : 8 * q + block]
                        prod = jnp.sum(prod.reshape(block // 8, 8, LANES), axis=0)
                        if u or base:
                            prod = acc_ref[slot, tap] + prod
                        acc_ref[slot, tap] = prod
        dk_ref[:, lanes] = jnp.sum(acc_ref[slot], axis=1).astype(BF)

    lane_groups(0, d, work)


def grad_taps(utt, total, taps, place, dbn, conv_out, halos, sums, dsums, vec, gated):
    rows, d = gated.shape
    return pl.pallas_call(
        functools.partial(grad_taps_body, utt, total),
        in_specs=[SCALARS] + [WHOLE] * 8,
        out_specs=[WHOLE] * 2,
        out_shape=[
            shape((taps, d), BF),
            near((d // LANES, utt, rows // utt + 2 * PAD, LANES), F32),
        ],
        scratch_shapes=[pltpu.VMEM((2, taps, 8, LANES), F32)],
        compiler_params=params(VMEM_MIB),
        cost_estimate=cost(9),
        name="grad_taps",
    )(place, dbn, conv_out, *halos, sums, dsums, vec, gated)


def grad_proj_body(utt, start, dc_ref, k_ref, p_ref, q_ref, *rest):
    dv_ref, dg_ref = rest[-2:]
    rows, width = dv_ref.shape
    frames = rows // utt
    taps = k_ref.shape[0]
    block = 64

    def work(group, out, slot):
        lanes = pl.ds(pl.multiple_of(out.start + start, LANES), LANES)
        for u in range(utt):
            for base in range(0, frames, block):
                at = slice(u * frames + base, u * frames + base + block)
                acc = jnp.zeros((block, LANES), F32)
                for r in range(8):
                    w = dc_ref[group + start // LANES, u, base + r : base + r + block + taps - 8, :]
                    for q in range(taps // 8):
                        tap = taps - 1 - (8 * q + r)
                        acc = acc + k_ref[tap : tap + 1, lanes] * w[8 * q : 8 * q + block]
                dv_ref[at, out] = (acc * p_ref[at, lanes].astype(F32)).astype(BF)
                dg_ref[at, out] = (acc * q_ref[at, lanes].astype(F32)).astype(BF)

    lane_groups(0, width, work)


def grad_proj(utt, start, width, d_conv, kernel, p, q, after):
    rows = p.shape[0]
    out = near((rows, width), BF)
    return pl.pallas_call(
        functools.partial(grad_proj_body, utt, start),
        in_specs=[WHOLE] * 4 + [ANYWHERE] * len(after),
        out_specs=[WHOLE] * 2,
        out_shape=[out, out],
        compiler_params=params(VMEM_MIB),
        cost_estimate=cost(4),
        name="grad_proj",
    )(d_conv, kernel, p, q, *after)


def back_norm_body(hat_ref, rstd_ref, cot_ref, vec_ref, w_ref, *rest):
    pieces = rest[:4]
    out_ref, acc_ref = rest[-2:]
    rows, d = hat_ref.shape
    wide = pieces[0].shape[1]
    dims = (((1,), (1,)), ((), ()))
    for j in range(d // CW):
        cols = slice(j * CW, (j + 1) * CW)
        part = 0.0
        for k, piece in enumerate(pieces):
            part += lax.dot_general(
                piece[...], w_ref[cols, k * wide : (k + 1) * wide], dims, preferred_element_type=F32
            )
        acc_ref[:, cols] = part * vec_ref[0:1, cols]
    for i in range(0, rows, 16):
        at = slice(i, i + 16)
        hat = hat_ref[at, :].astype(F32)
        grads = acc_ref[at, :]
        m1 = jnp.sum(grads, axis=-1, keepdims=True) * (1.0 / d)
        m2 = jnp.sum(grads * hat, axis=-1, keepdims=True) * (1.0 / d)
        layer = rstd_ref[at, :] * (grads - m1 - hat * m2)
        out_ref[at, :] = (cot_ref[at, :].astype(F32) + layer).astype(BF)


def back_norm(hat, rstd, cot, vec, w_in, pieces, after):
    rows, d = hat.shape
    return pl.pallas_call(
        back_norm_body,
        in_specs=[WHOLE] * 9 + [ANYWHERE] * len(after),
        out_specs=WHOLE,
        out_shape=shape((rows, d), BF),
        scratch_shapes=[pltpu.VMEM((rows, d), F32)],
        compiler_params=params(VMEM_MIB),
        cost_estimate=cost(7),
        name="back_norm",
    )(hat, rstd, cot, vec, w_in, *pieces, *after)


def swap(block, axis, bit):
    count = lax.axis_size(axis)
    return lax.ppermute(block, axis, [(i, i ^ bit) for i in range(count)])


def is_power(count):
    return count & (count - 1) == 0


def add_body(own_ref, got_ref, *rest):
    out_ref = rest[-1]
    out_ref[...] = (own_ref[...].astype(F32) + got_ref[...].astype(F32)).astype(out_ref.dtype)


def add(own, got, dtype, after):
    return pl.pallas_call(
        add_body,
        in_specs=[WHOLE] * 2 + [ANYWHERE] * len(after),
        out_specs=WHOLE,
        out_shape=shape(own.shape, dtype),
        compiler_params=params(4),
        cost_estimate=cost(0.5),
        name="add",
    )(own, got, *after)


def all_sum(block, axis, fill=(), far_first=False):
    count = lax.axis_size(axis)
    if not is_power(count):
        for work in fill:
            work([])
        return lax.psum(block.astype(F32), axis)
    bits = [1 << i for i in range(count.bit_length() - 1)]
    if far_first:
        bits = bits[:1] + bits[3:] + bits[1:3]
    for step, bit in enumerate(bits):
        other = swap(block, axis, bit)
        after = fill[step]([block]) if step < len(fill) else []
        block = add(block, other, F32 if bit == bits[-1] else block.dtype, after)
    return block


def nothing(_):
    return []


def beside(a, b, axis):
    count = lax.axis_size(axis)
    pairs = []
    for low in range(1, count - 1, 2):
        pairs += [(low, low + 1), (low + 1, low)]
    return swap(a, axis, 1), lax.ppermute(b, axis, pairs)


def merge_body(sides, after, *refs):
    keep_out, send_out = refs[2 * sides + after :]
    blocks = refs[0].shape[0]
    wide = refs[0].shape[2]
    for side in range(sides):
        keep_ref, got_ref = refs[2 * side : 2 * side + 2]
        cols = slice(side * wide, (side + 1) * wide)
        for j in range(blocks):
            total = keep_ref[j] + got_ref[j].astype(F32)
            if j % 2:
                send_out[j // 2, :, cols] = total.astype(BF)
            else:
                keep_out[j // 2, :, cols] = total


def merge(pairs, after):
    blocks, per, wide = pairs[0][0].shape
    dims = (blocks // 2, per, wide * len(pairs))
    return pl.pallas_call(
        functools.partial(merge_body, len(pairs), len(after)),
        in_specs=[WHOLE] * (2 * len(pairs)) + [ANYWHERE] * len(after),
        out_specs=[WHOLE] * 2,
        out_shape=[shape(dims, F32), shape(dims, BF)],
        compiler_params=params(8),
        cost_estimate=cost(1),
        name="merge",
    )(*[a for pair in pairs for a in pair], *after)


def first_swaps(parts, axis, after):
    return [
        merge([(keep, swap(send, axis, device_bit))], after)
        for (keep, send), device_bit in zip(parts, (2, 4))
    ]


def last_swaps(held, axis, after):
    count = lax.axis_size(axis)
    after = list(after)
    pairs = [
        (keep, swap(send, axis, device_bit)) for (keep, send), device_bit in zip(held, (4, 2))
    ]
    bit = 8
    if bit == count:
        return jnp.concatenate([keep + got for keep, got in pairs], axis=-1)[0]
    while True:
        keep, send = merge(pairs, after.pop(0) if after else [])
        got = swap(send, axis, bit)
        bit *= 2
        if bit == count:
            return add(keep[0], got[0], F32, [])
        pairs = [(keep, got)]


def on_device(inputs, ln_gain, w_in, kernel, bn_gain, bn_bias, w_out, cotangent):
    axis = "seq"
    n = lax.axis_size(axis)
    me = lax.axis_index(axis).astype(jnp.int32)
    utt, frames, d = inputs.shape
    rows = utt * frames
    half = d // 2
    total = rows * n
    x = inputs.reshape(rows, d)
    cot = cotangent.reshape(rows, d)
    vec = jnp.concatenate([ln_gain, bn_gain, bn_bias]).reshape(3, d)
    place = jnp.stack([me % 2, me // 2, (me > 0).astype(jnp.int32), (me < n - 1).astype(jnp.int32)])
    by_owner = is_power(n) and n >= 8 and d % n == 0 and (d // n) % 16 == 0

    gated, p, q, hat, rstd, ga, gb = front(utt, place, x, vec, w_in)
    ga, gb = beside(ga, gb, axis)
    conv_out, sums = conv(utt, place, gated, ga, gb, kernel)
    made = {}

    def turning(after):
        made["a"], other = turn(n, place, cot, after)
        made["b"] = swap(other, axis, 1)
        return [made["a"]]

    if by_owner:
        sums = all_sum(sums, axis, [nothing, turning])
        waits = [made["b"]]
    else:
        sums = all_sum(sums, axis)
        waits = []

    act, dbn, dsums, da, db = middle(utt, total, place, conv_out, sums, vec, cot, w_out, waits)
    da, db = beside(da, db, axis)

    def branching(after):
        made["outputs"] = branch(x, act, w_out, after)
        return [made["outputs"]]

    def grading(after):
        made["grad"] = grad((1, 2), made["a"], made["b"], act, act_b, after)
        return [made["grad"][0]]

    if by_owner:
        act_b = swap(act, axis, 1)
        dsums = all_sum(dsums, axis, [nothing, branching, lambda _: [da, db], grading])
        send_l, keep_l, send_r, keep_r = made["grad"]
        held = first_swaps([(keep_l, send_l), (keep_r, send_r)], axis, [dsums])
    else:
        dsums = all_sum(dsums, axis, [nothing, branching])
        dw = lax.dot_general(cot, act, (((0,), (0,)), ((), ())), preferred_element_type=F32)
        d_w_out = lax.psum_scatter(dw, axis, scatter_dimension=0, tiled=True)

    d_kernel, d_conv = grad_taps(
        utt, total, kernel.shape[0], place, dbn, conv_out, (da, db), sums, dsums, vec, gated
    )
    half = d // 2

    def projecting(start):
        def work(after):
            made[start] = grad_proj(utt, start, half, d_conv, kernel, p, q, after)
            return [made[start][0]]

        return work

    def norming(after):
        left, right = made[0], made[half]
        made["d_inputs"] = back_norm(
            hat, rstd, cot, vec, w_in, (left[0], right[0], left[1], right[1]), after
        )
        return [made["d_inputs"]]

    d_kernel_sum = all_sum(
        d_kernel, axis, [nothing, projecting(0), projecting(half), norming], far_first=True
    )
    if by_owner:
        d_w_out = last_swaps(held, axis, [[d_kernel], [made[half][0]]])
    return (
        made["outputs"].reshape(inputs.shape), made["d_inputs"].reshape(inputs.shape), d_w_out,
        d_kernel_sum, dsums[1], dsums[0],
    )


def solution(mesh):
    return jax.shard_map(
        on_device,
        mesh=mesh,
        in_specs=(P(None, "seq", None), P(), P(), P(), P(), P(), P(), P(None, "seq", None)),
        out_specs=(P(None, "seq", None), P(None, "seq", None), P("seq", None), P(), P(), P()),
        check_vma=False,
    )
```

```python
import functools

import jax
import jax.numpy as jnp
from jax import lax
from jax.experimental import pallas as pl
from jax.experimental.pallas import tpu as pltpu
from jax.sharding import PartitionSpec as P

EPSILON = 1e-05
BF = jnp.bfloat16
F32 = jnp.float32
LANES = 128
PAD = 16
MIB = 1 << 20
AXIS = "seq"
VMEM_MIB = 8


def params(mib):
    return pltpu.CompilerParams(vmem_limit_bytes=mib * MIB)


WHOLE = pl.BlockSpec(memory_space=pltpu.VMEM)
ANYWHERE = pl.BlockSpec(memory_space=pl.ANY)
CW = 256


def cost(micros):
    return pl.CostEstimate(flops=0, bytes_accessed=int(micros * 3.0e6), transcendentals=0)


def shape(dims, dtype):
    return jax.ShapeDtypeStruct(dims, dtype)


def place():
    me = lax.axis_index(AXIS)
    last = lax.axis_size(AXIS) - 1
    return me % 2, me // 2, (me > 0).astype(F32), (me < last).astype(F32)


def near(dims, dtype):
    return pltpu.VMEM(dims, dtype)


def turn_body(cot_ref, *rest):
    mine_ref, other_ref, held_ref = rest[-3:]
    blocks = mine_ref.shape[0]
    per = mine_ref.shape[1]
    held_ref[...] = cot_ref[...].T
    core, half, _, _ = place()

    def step(j, _):
        row = pl.multiple_of(lax.bitwise_xor(half, j) * (2 * per), 2 * per)
        mine_ref[j] = held_ref[pl.ds(pl.multiple_of(row + core * per, per), per), :]
        other_ref[j] = held_ref[pl.ds(pl.multiple_of(row + (1 - core) * per, per), per), :]
        return 0

    lax.fori_loop(0, blocks, step, 0, unroll=2)


def turn(n, cot, after):
    rows, d = cot.shape
    out = shape((n // 2, d // n, rows), BF)
    return pl.pallas_call(
        turn_body,
        in_specs=[WHOLE] + [ANYWHERE] * len(after),
        out_specs=[WHOLE] * 2,
        out_shape=[out] * 2,
        scratch_shapes=[pltpu.VMEM((d, rows), BF)],
        compiler_params=params(VMEM_MIB),
        cost_estimate=cost(2),
        name="turn",
    )(cot, *after)


def edges_out(odd, first, last, a_ref, b_ref):
    @pl.when(odd == 0)
    def _():
        a_ref[...] = last
        b_ref[...] = first

    @pl.when(odd != 0)
    def _():
        a_ref[...] = first
        b_ref[...] = last


def front_body(
    utt, x_hbm, ln_ref, gain_ref, bias_ref, w_hbm,
    gated_ref, p_ref, q_ref, hat_ref, rstd_ref, vec_ref, a_ref, b_ref, normed_ref, x_ref, w_ref, x_sem, w_sem,
):
    rows, d = x_ref.shape
    frames = rows // utt
    pieces = x_sem.shape[0]
    span = rows // pieces
    steps = d // CW

    def x_copy(i):
        at = pl.ds(i * span, span)
        return pltpu.make_async_copy(x_hbm.at[at], x_ref.at[at], x_sem.at[i])

    def w_copy(j, half):
        at = pl.ds(half * d + j * CW, CW)
        return pltpu.make_async_copy(w_hbm.at[:, at], w_ref.at[:, at], w_sem.at[j, half])

    for i in range(pieces):
        x_copy(i).start()
    for half in range(2):
        w_copy(0, half).start()
    vec_ref[0:1, :] = ln_ref[...].reshape(1, d)
    vec_ref[1:2, :] = gain_ref[...].reshape(1, d)
    vec_ref[2:3, :] = bias_ref[...].reshape(1, d)

    for i in range(pieces):
        x_copy(i).wait()
        for j in range(1 + i, steps if i == pieces - 1 else 2 + i):
            for half in range(2):
                w_copy(j, half).start()

        for k in range(i * span, (i + 1) * span, 16):
            at = slice(k, k + 16)
            x = x_ref[at, :].astype(F32)
            mu = jnp.sum(x, axis=-1, keepdims=True) * (1.0 / d)
            c = x - mu
            var = jnp.sum(c * c, axis=-1, keepdims=True) * (1.0 / d)
            rstd = lax.rsqrt(var + EPSILON)
            hat = c * rstd
            rstd_ref[at, :] = rstd
            hat_ref[at, :] = hat.astype(BF)
            normed_ref[at, :] = (hat * vec_ref[0:1, :]).astype(BF)

    odd = place()[0] != 0
    for j in range(steps):
        cols = slice(j * CW, (j + 1) * CW)
        for half in range(2):
            w_copy(j, half).wait()
        value = jnp.dot(normed_ref[...], w_ref[:, cols], preferred_element_type=F32)
        gate = jnp.dot(
            normed_ref[...], w_ref[:, d + j * CW : d + (j + 1) * CW], preferred_element_type=F32
        )
        sig = jax.nn.sigmoid(gate)
        gated = value * sig
        held = gated.astype(BF)
        gated_ref[:, cols] = held
        p_ref[:, cols] = sig.astype(BF)
        q_ref[:, cols] = (gated * (1.0 - sig)).astype(BF)
        shaped = held.reshape(utt, frames, CW)
        first, last = shaped[:, :PAD], shaped[:, frames - PAD :]
        a_ref[:, :, cols] = jnp.where(odd, first, last)
        b_ref[:, :, cols] = jnp.where(odd, last, first)


def front(utt, x, ln_gain, bn_gain, bn_bias, w_in):
    rows, d = x.shape
    out = near((rows, d), BF)
    edge = shape((utt, PAD, d), BF)
    return pl.pallas_call(
        functools.partial(front_body, utt),
        in_specs=[ANYWHERE] + [WHOLE] * 3 + [ANYWHERE],
        out_specs=[WHOLE] * 8,
        out_shape=[out] * 4 + [near((rows, 1), F32), near((3, d), F32)] + [edge] * 2,
        scratch_shapes=[
            pltpu.VMEM((rows, d), BF),
            pltpu.VMEM((rows, d), BF),
            pltpu.VMEM((d, 2 * d), BF),
            pltpu.SemaphoreType.DMA((4,)),
            pltpu.SemaphoreType.DMA((d // CW, 2)),
        ],
        compiler_params=params(52),
        cost_estimate=cost(10),
        name="front",
    )(x, ln_gain, bn_gain, bn_bias, w_in)


def lane_groups(first, last, work):
    def step(i, _):
        for slot in range(2):
            group = 2 * i + slot
            work(group, pl.ds(pl.multiple_of(group * LANES, LANES), LANES), slot)
        return 0

    lax.fori_loop(first // (2 * LANES), last // (2 * LANES), step, 0)


PHASES = 4
PIECES = 9


def thirds(x0, x1, x2):
    return [x1, x0 - x1, x2 - x1]


def sequences(x):
    tops = [
        (x[1], x[3], x[5]),
        (x[0] - x[1], x[2] - x[3], x[4] - x[5]),
        (x[2] - x[1], x[4] - x[3], x[6] - x[5]),
    ]
    return [piece for top in tops for piece in thirds(*top)]


def combined(h):
    tops = [(h[0] + h[1], h[2] + h[3]), (h[0], h[2]), (h[1], h[3])]
    return [piece for a, b in tops for piece in (a + b, a, b)]


def assembled(products):
    halves = []
    for top in range(3):
        m, p, q = (next(products) for _ in range(3))
        halves.append((m + p, m + q))
        if top:
            for j in range(2):
                yield 2 * j + top - 1, halves[0][j] + halves[top][j]


def phase(first, size):
    return pl.ds(first, size, PHASES)


def fill_sequences(pad_ref, shift, seq_ref, size):
    x = [pad_ref[phase(j + shift, size), :] for j in range(2 * PHASES - 1)]
    for i, piece in enumerate(sequences(x)):
        seq_ref[i] = piece


def filtered(seq_ref, taps_ref, order, count):
    for i in range(PIECES):
        acc = jnp.zeros((count, LANES), F32)
        for a in range(taps_ref.shape[1]):
            row = order(a)
            acc = acc + taps_ref[i, row : row + 1, :] * seq_ref[i, a : a + count, :]
        yield acc


def conv_body(utt, g_ref, a_ref, b_ref, k_ref, conv_ref, sums_ref, pad_ref, seq_ref, taps_ref):
    d = g_ref.shape[1]
    frames = g_ref.shape[0] // utt
    count = frames // PHASES
    per = k_ref.shape[0] // PHASES
    odd = place()[0] != 0

    def work(_, lanes, slot):
        first = square = jnp.zeros((8, LANES), F32)
        pad_ref[slot, 0, 0 : per * PHASES, :] = k_ref[:, lanes]
        k = [pad_ref[slot, 0, phase(i, per), :] for i in range(PHASES)]
        for i, piece in enumerate(combined(k)):
            taps_ref[slot, i] = piece
        for u in range(utt):
            a = a_ref[u, :, lanes].astype(F32)
            b = b_ref[u, :, lanes].astype(F32)
            rows = slice(u * frames, (u + 1) * frames)
            pad_ref[slot, u, 0:PAD, :] = jnp.where(odd, a, b)
            pad_ref[slot, u, PAD : PAD + frames, :] = g_ref[rows, lanes].astype(F32)
            pad_ref[slot, u, PAD + frames : PAD + frames + PAD, :] = jnp.where(odd, b, a)
            fill_sequences(pad_ref.at[slot, u], 1, seq_ref.at[slot, u], count + per)
            products = filtered(seq_ref.at[slot, u], taps_ref.at[slot], lambda a: a, count)
            for i, y in assembled(products):
                pad_ref[slot, u, phase(i, count), :] = y
                part = y.reshape(count // 8, 8, LANES)
                first = first + jnp.sum(part, axis=0)
                square = square + jnp.sum(part * part, axis=0)
            conv_ref[rows, lanes] = pad_ref[slot, u, 0:frames, :]
        sums_ref[0:1, lanes] = jnp.sum(first, axis=0, keepdims=True)
        sums_ref[1:2, lanes] = jnp.sum(square, axis=0, keepdims=True)

    lane_groups(0, d, work)


def conv(utt, gated, a, b, kernel):
    rows, d = gated.shape
    frames = rows // utt
    per = kernel.shape[0] // PHASES
    return pl.pallas_call(
        functools.partial(conv_body, utt),
        in_specs=[WHOLE] * 4,
        out_specs=[WHOLE] * 2,
        out_shape=[near(gated.shape, F32), shape((2, d), F32)],
        scratch_shapes=[
            pltpu.VMEM((2, utt, frames + 2 * PAD + 8, LANES), F32),
            pltpu.VMEM((2, utt, PIECES, frames // PHASES + per, LANES), F32),
            pltpu.VMEM((2, PIECES, per, LANES), F32),
        ],
        compiler_params=params(VMEM_MIB),
        cost_estimate=cost(7),
        name="conv",
    )(gated, a, b, kernel)


def middle_body(
    utt, total, conv_ref, sums_ref, vec_ref, cot_ref, w_ref,
    *rest,
):
    act_ref, dbn_ref, dsums_ref, a_ref, b_ref = rest[-5:]
    rows, d = conv_ref.shape
    frames = rows // utt
    odd = place()[0] != 0
    for j in range(d // CW):
        cols = slice(j * CW, (j + 1) * CW)
        mean = sums_ref[0:1, cols] * (1.0 / total)
        var = sums_ref[1:2, cols] * (1.0 / total) - mean * mean
        rstd = lax.rsqrt(var + EPSILON)
        conv = conv_ref[:, cols]
        xhat = (conv - mean) * rstd
        out = xhat * vec_ref[1:2, cols] + vec_ref[2:3, cols]
        sig = jax.nn.sigmoid(out)
        act = out * sig
        act_ref[:, cols] = act.astype(BF)
        d_act = jnp.dot(cot_ref[...], w_ref[:, cols], preferred_element_type=F32)
        dbn = d_act * (sig + act * (1.0 - sig))
        dbn_ref[:, cols] = dbn
        dsums_ref[0:1, cols] = jnp.sum(dbn, axis=0, keepdims=True)
        dsums_ref[1:2, cols] = jnp.sum(dbn * xhat, axis=0, keepdims=True)
        for u in range(utt):
            low = slice(u * frames, u * frames + PAD)
            high = slice((u + 1) * frames - PAD, (u + 1) * frames)
            for at, piece in ((slice(0, PAD), dbn), (slice(PAD, 2 * PAD), conv)):
                first, last = piece[low].astype(BF), piece[high].astype(BF)
                a_ref[u, at, cols] = jnp.where(odd, first, last)
                b_ref[u, at, cols] = jnp.where(odd, last, first)


def middle(utt, total, conv_out, sums, vec, cot, w_out, after):
    rows, d = cot.shape
    edge = shape((utt, 2 * PAD, d), BF)
    return pl.pallas_call(
        functools.partial(middle_body, utt, total),
        in_specs=[WHOLE] * 5 + [ANYWHERE] * len(after),
        out_specs=[WHOLE] * 5,
        out_shape=[shape((rows, d), BF), near((rows, d), F32), shape((2, d), F32), edge, edge],
        compiler_params=params(VMEM_MIB),
        cost_estimate=cost(4),
        name="middle",
    )(conv_out, sums, vec, cot, w_out, *after)


def grad_body(bits, ca_ref, cb_ref, acta_ref, actb_ref, *rest):
    out_refs = rest[-4:]
    blocks, per, rows = ca_ref.shape
    half = out_refs[0].shape[-1]
    ca = ca_ref[...].reshape(blocks * per, rows)
    cb = cb_ref[...].reshape(blocks * per, rows)
    for side, bit in enumerate(bits):
        send_ref, keep_ref = out_refs[2 * side], out_refs[2 * side + 1]
        for c in range(half // CW):
            cols = slice(c * CW, (c + 1) * CW)
            src = slice(side * half + c * CW, side * half + (c + 1) * CW)
            dw = jnp.dot(ca, acta_ref[:, src], preferred_element_type=F32)
            dw += jnp.dot(cb, actb_ref[:, src], preferred_element_type=F32)
            sent = kept = 0
            for j in range(blocks):
                block = dw[j * per : (j + 1) * per]
                if j & bit:
                    send_ref[sent, :, cols] = block.astype(BF)
                    sent += 1
                else:
                    keep_ref[kept, :, cols] = block
                    kept += 1


def grad(bits, cot_a, cot_b, act_a, act_b, after):
    blocks, per, _ = cot_a.shape
    d = act_a.shape[1]
    half = (blocks // 2, per, d // 2)
    return pl.pallas_call(
        functools.partial(grad_body, bits),
        in_specs=[WHOLE] * 4 + [ANYWHERE] * len(after),
        out_specs=[WHOLE] * 4,
        out_shape=[shape(half, BF), shape(half, F32)] * 2,
        compiler_params=params(VMEM_MIB),
        cost_estimate=cost(3.5),
        name="grad",
    )(cot_a, cot_b, act_a, act_b, *after)


def branch_body(x_ref, act_ref, w_ref, *rest):
    out_hbm, out_ref, sem = rest[-3:]
    copies = []
    for j in range(out_ref.shape[-1] // CW):
        cols = slice(j * CW, (j + 1) * CW)
        part = lax.dot_general(
            act_ref[...], w_ref[cols, :], (((1,), (1,)), ((), ())), preferred_element_type=F32
        )
        out_ref[:, cols] = (x_ref[:, cols].astype(F32) + part).astype(BF)
        copies.append(pltpu.make_async_copy(out_ref.at[:, cols], out_hbm.at[:, cols], sem.at[j]))
        copies[-1].start()
    for copy in copies:
        copy.wait()


def branch(x, act, w_out, after):
    rows, d = x.shape
    return pl.pallas_call(
        branch_body,
        in_specs=[WHOLE] * 3 + [ANYWHERE] * len(after),
        out_specs=pl.BlockSpec(memory_space=pltpu.HBM),
        out_shape=pltpu.HBM((rows, d), BF),
        scratch_shapes=[pltpu.VMEM((rows, d), BF), pltpu.SemaphoreType.DMA((d // CW,))],
        compiler_params=params(VMEM_MIB),
        cost_estimate=cost(4),
        name="branch",
    )(x, act, w_out, *after)


def grad_taps_body(
    utt, total, dbn_ref, conv_ref, a_ref, b_ref, sums_ref, dsums_ref, vec_ref, g_ref,
    dk_ref, seq_ref, pad_ref, held_ref, acc_ref,
):
    d = g_ref.shape[1]
    frames = g_ref.shape[0] // utt
    count = frames // PHASES
    taps = dk_ref.shape[0]
    per = taps // PHASES
    odd, _, keep_lo, keep_hi = place()
    odd = odd != 0

    def work(group, lanes, slot):
        mean = sums_ref[0:1, lanes] * (1.0 / total)
        var = sums_ref[1:2, lanes] * (1.0 / total) - mean * mean
        rstd = lax.rsqrt(var + EPSILON)
        scale = rstd * vec_ref[1:2, lanes]
        cross = scale * rstd * (dsums_ref[1:2, lanes] * (1.0 / total))
        mean_grad = scale * (dsums_ref[0:1, lanes] * (1.0 / total))

        def d_conv(dbn, conv):
            return dbn.astype(F32) * scale - mean_grad - (conv.astype(F32) - mean) * cross

        for u in range(utt):
            a = d_conv(a_ref[u, :PAD, lanes], a_ref[u, PAD:, lanes])
            b = d_conv(b_ref[u, :PAD, lanes], b_ref[u, PAD:, lanes])
            rows = slice(u * frames, (u + 1) * frames)
            pad_ref[slot, u, 0:PAD, :] = jnp.where(odd, a, b) * keep_lo
            pad_ref[slot, u, PAD : PAD + frames, :] = d_conv(dbn_ref[rows, lanes], conv_ref[rows, lanes])
            pad_ref[slot, u, PAD + frames : PAD + frames + PAD, :] = jnp.where(odd, b, a) * keep_hi
            fill_sequences(pad_ref.at[slot, u], 0, seq_ref.at[group, u], count + per)
            pad_ref[slot, u, 0:frames, :] = g_ref[rows, lanes].astype(F32)
            g = [pad_ref[slot, u, phase(i, count), :] for i in range(PHASES)]
            for i, piece in enumerate(combined(g)):
                held_ref[slot, u, i] = piece

        def products():
            for i in range(PIECES):
                sums = [jnp.zeros((8, LANES), F32)] * per
                for u in range(utt):
                    for base in range(0, count, 32):
                        g = held_ref[slot, u, i, base : base + 32, :]
                        for a in range(per):
                            prod = g * seq_ref[group, u, i, base + a : base + a + 32, :]
                            sums[a] = sums[a] + jnp.sum(prod.reshape(4, 8, LANES), axis=0)
                yield jnp.stack(sums)

        for i, y in assembled(products()):
            for a in range(per):
                acc_ref[slot, taps - 1 - (PHASES * a + i)] = y[a]
        dk_ref[:, lanes] = jnp.sum(acc_ref[slot], axis=1).astype(BF)

    lane_groups(0, d, work)


def grad_taps(utt, total, taps, dbn, conv_out, halos, sums, dsums, vec, gated):
    rows, d = gated.shape
    frames = rows // utt
    long = frames // PHASES + taps // PHASES
    return pl.pallas_call(
        functools.partial(grad_taps_body, utt, total),
        in_specs=[WHOLE] * 8,
        out_specs=[WHOLE] * 2,
        out_shape=[
            shape((taps, d), BF),
            near((d // LANES, utt, PIECES, long, LANES), F32),
        ],
        scratch_shapes=[
            pltpu.VMEM((2, utt, frames + 2 * PAD + 8, LANES), F32),
            pltpu.VMEM((2, utt, PIECES, frames // PHASES, LANES), F32),
            pltpu.VMEM((2, taps, 8, LANES), F32),
        ],
        compiler_params=params(VMEM_MIB),
        cost_estimate=cost(9),
        name="grad_taps",
    )(dbn, conv_out, *halos, sums, dsums, vec, gated)


def grad_proj_body(utt, start, seq_ref, k_ref, p_ref, q_ref, *rest):
    dv_ref, dg_ref, out_ref, taps_ref = rest[-4:]
    rows, width = dv_ref.shape
    frames = rows // utt
    count = frames // PHASES
    per = k_ref.shape[0] // PHASES

    def work(group, out, slot):
        lanes = pl.ds(pl.multiple_of(out.start + start, LANES), LANES)
        out_ref[slot, 0 : per * PHASES, :] = k_ref[:, lanes]
        k = [out_ref[slot, phase(PHASES - 1 - i, per), :] for i in range(PHASES)]
        for i, piece in enumerate(combined(k)):
            taps_ref[slot, i] = piece
        for u in range(utt):
            products = filtered(
                seq_ref.at[group + start // LANES, u], taps_ref.at[slot], lambda a: per - 1 - a, count
            )
            for i, y in assembled(products):
                out_ref[slot, phase(u * frames + i, count), :] = y
        acc = out_ref[slot]
        dv_ref[:, out] = (acc * p_ref[:, lanes].astype(F32)).astype(BF)
        dg_ref[:, out] = (acc * q_ref[:, lanes].astype(F32)).astype(BF)

    lane_groups(0, width, work)


def grad_proj(utt, start, width, seqs, kernel, p, q, after):
    rows = p.shape[0]
    out = near((rows, width), BF)
    return pl.pallas_call(
        functools.partial(grad_proj_body, utt, start),
        in_specs=[WHOLE] * 4 + [ANYWHERE] * len(after),
        out_specs=[WHOLE] * 2,
        out_shape=[out, out],
        scratch_shapes=[
            pltpu.VMEM((2, rows, LANES), F32),
            pltpu.VMEM((2, PIECES, kernel.shape[0] // PHASES, LANES), F32),
        ],
        compiler_params=params(VMEM_MIB),
        cost_estimate=cost(4),
        name="grad_proj",
    )(seqs, kernel, p, q, *after)


def back_proj_body(vec_ref, w_ref, *rest):
    pieces = rest[:4]
    out_ref = rest[-1]
    rows, d = out_ref.shape
    wide = pieces[0].shape[1]
    dims = (((1,), (1,)), ((), ()))
    for j in range(d // CW):
        cols = slice(j * CW, (j + 1) * CW)
        part = 0.0
        for k, piece in enumerate(pieces):
            part += lax.dot_general(
                piece[...], w_ref[cols, k * wide : (k + 1) * wide], dims, preferred_element_type=F32
            )
        out_ref[:, cols] = part * vec_ref[0:1, cols]


def back_proj(vec, w_in, pieces, after):
    rows = pieces[0].shape[0]
    d = w_in.shape[0]
    return pl.pallas_call(
        back_proj_body,
        in_specs=[WHOLE] * 6 + [ANYWHERE] * len(after),
        out_specs=WHOLE,
        out_shape=near((rows, d), F32),
        compiler_params=params(VMEM_MIB),
        cost_estimate=cost(5),
        name="back_proj",
    )(vec, w_in, *pieces, *after)


def back_norm_body(hat_ref, rstd_ref, cot_ref, acc_ref, *rest):
    out_hbm, out_ref, sem = rest[-3:]
    copies = []
    rows, d = hat_ref.shape
    span = rows // sem.shape[0]
    for i in range(0, rows, 16):
        at = slice(i, i + 16)
        hat = hat_ref[at, :].astype(F32)
        grads = acc_ref[at, :]
        m1 = jnp.sum(grads, axis=-1, keepdims=True) * (1.0 / d)
        m2 = jnp.sum(grads * hat, axis=-1, keepdims=True) * (1.0 / d)
        layer = rstd_ref[at, :] * (grads - m1 - hat * m2)
        out_ref[at, :] = (cot_ref[at, :].astype(F32) + layer).astype(BF)
        if (i + 16) % span == 0:
            piece = pl.ds(i + 16 - span, span)
            copies.append(
                pltpu.make_async_copy(out_ref.at[piece], out_hbm.at[piece], sem.at[i // span])
            )
            copies[-1].start()
    for copy in copies:
        copy.wait()


def back_norm(hat, rstd, cot, grads, after):
    rows, d = hat.shape
    return pl.pallas_call(
        back_norm_body,
        in_specs=[WHOLE] * 4 + [ANYWHERE] * len(after),
        out_specs=pl.BlockSpec(memory_space=pltpu.HBM),
        out_shape=pltpu.HBM((rows, d), BF),
        scratch_shapes=[pltpu.VMEM((rows, d), BF), pltpu.SemaphoreType.DMA((8,))],
        compiler_params=params(VMEM_MIB),
        cost_estimate=cost(3),
        name="back_norm",
    )(hat, rstd, cot, grads, *after)


def swap(block, axis, bit):
    count = lax.axis_size(axis)
    return lax.ppermute(block, axis, [(i, i ^ bit) for i in range(count)])


def is_power(count):
    return count & (count - 1) == 0


def add_body(own_ref, got_ref, *rest):
    out_ref = rest[-1]
    out_ref[...] = (own_ref[...].astype(F32) + got_ref[...].astype(F32)).astype(out_ref.dtype)


def add(own, got, dtype, after):
    return pl.pallas_call(
        add_body,
        in_specs=[WHOLE] * 2 + [ANYWHERE] * len(after),
        out_specs=WHOLE,
        out_shape=shape(own.shape, dtype),
        compiler_params=params(4),
        cost_estimate=cost(0.5),
        name="add",
    )(own, got, *after)


def all_sum(block, axis, fill=(), far_first=False):
    count = lax.axis_size(axis)
    if not is_power(count):
        for work in fill:
            work([])
        return lax.psum(block.astype(F32), axis)
    bits = [1 << i for i in range(count.bit_length() - 1)]
    if far_first:
        bits = bits[:1] + bits[3:] + bits[1:3]
    for step, bit in enumerate(bits):
        other = swap(block, axis, bit)
        after = fill[step]([block]) if step < len(fill) else []
        block = add(block, other, F32 if bit == bits[-1] else block.dtype, after)
    return block


def nothing(_):
    return []


def beside(a, b, axis):
    count = lax.axis_size(axis)
    pairs = []
    for low in range(1, count - 1, 2):
        pairs += [(low, low + 1), (low + 1, low)]
    return swap(a, axis, 1), lax.ppermute(b, axis, pairs)


def merge_body(sides, after, *refs):
    keep_out, send_out = refs[2 * sides + after :]
    blocks = refs[0].shape[0]
    wide = refs[0].shape[2]
    for side in range(sides):
        keep_ref, got_ref = refs[2 * side : 2 * side + 2]
        cols = slice(side * wide, (side + 1) * wide)
        for j in range(blocks):
            total = keep_ref[j] + got_ref[j].astype(F32)
            if j % 2:
                send_out[j // 2, :, cols] = total.astype(BF)
            else:
                keep_out[j // 2, :, cols] = total


def merge(pairs, after):
    blocks, per, wide = pairs[0][0].shape
    dims = (blocks // 2, per, wide * len(pairs))
    return pl.pallas_call(
        functools.partial(merge_body, len(pairs), len(after)),
        in_specs=[WHOLE] * (2 * len(pairs)) + [ANYWHERE] * len(after),
        out_specs=[WHOLE] * 2,
        out_shape=[shape(dims, F32), shape(dims, BF)],
        compiler_params=params(8),
        cost_estimate=cost(1),
        name="merge",
    )(*[a for pair in pairs for a in pair], *after)


def first_swaps(parts, axis, after):
    return [
        merge([(keep, swap(send, axis, device_bit))], after)
        for (keep, send), device_bit in zip(parts, (2, 4))
    ]


def last_swaps(held, axis, after):
    count = lax.axis_size(axis)
    after = list(after)
    pairs = [
        (keep, swap(send, axis, device_bit)) for (keep, send), device_bit in zip(held, (4, 2))
    ]
    bit = 8
    if bit == count:
        return jnp.concatenate([keep + got for keep, got in pairs], axis=-1)[0]
    while True:
        keep, send = merge(pairs, after.pop(0) if after else [])
        got = swap(send, axis, bit)
        bit *= 2
        if bit == count:
            return add(keep[0], got[0], F32, [])
        pairs = [(keep, got)]


def on_device(inputs, ln_gain, w_in, kernel, bn_gain, bn_bias, w_out, cotangent):
    axis = AXIS
    n = lax.axis_size(axis)
    me = lax.axis_index(axis).astype(jnp.int32)
    utt, frames, d = inputs.shape
    rows = utt * frames
    half = d // 2
    total = rows * n
    x = inputs.reshape(rows, d)
    cot = cotangent.reshape(rows, d)
    by_owner = is_power(n) and n >= 8 and d % n == 0 and (d // n) % 16 == 0

    gated, p, q, hat, rstd, vec, ga, gb = front(utt, x, ln_gain, bn_gain, bn_bias, w_in)
    ga, gb = beside(ga, gb, axis)
    conv_out, sums = conv(utt, gated, ga, gb, kernel)
    made = {}

    def turning(after):
        made["a"], other = turn(n, cot, after)
        made["b"] = swap(other, axis, 1)
        return [made["a"]]

    if by_owner:
        sums = all_sum(sums, axis, [nothing, turning])
        waits = [made["b"]]
    else:
        sums = all_sum(sums, axis)
        waits = []

    act, dbn, dsums, da, db = middle(utt, total, conv_out, sums, vec, cot, w_out, waits)
    da, db = beside(da, db, axis)

    def branching(after):
        made["outputs"] = branch(x, act, w_out, after)
        return [made["outputs"]]

    def grading(after):
        made["grad"] = grad((1, 2), made["a"], made["b"], act, act_b, after)
        return [made["grad"][0]]

    if by_owner:
        act_b = swap(act, axis, 1)
        dsums = all_sum(dsums, axis, [nothing, branching, lambda _: [da, db], grading])
        send_l, keep_l, send_r, keep_r = made["grad"]
        held = first_swaps([(keep_l, send_l), (keep_r, send_r)], axis, [dsums])
    else:
        dsums = all_sum(dsums, axis, [nothing, branching])
        dw = lax.dot_general(cot, act, (((0,), (0,)), ((), ())), preferred_element_type=F32)
        d_w_out = lax.psum_scatter(dw, axis, scatter_dimension=0, tiled=True)

    d_kernel, d_conv = grad_taps(
        utt, total, kernel.shape[0], dbn, conv_out, (da, db), sums, dsums, vec, gated
    )
    half = d // 2

    def projecting(start):
        def work(after):
            made[start] = grad_proj(utt, start, half, d_conv, kernel, p, q, after)
            return [made[start][0]]

        return work

    def back_projecting(after):
        left, right = made[0], made[half]
        made["far"] = after
        made["grads"] = back_proj(vec, w_in, (left[0], right[0], left[1], right[1]), after)
        return [made["grads"]]

    def norming(after):
        made["d_inputs"] = back_norm(hat, rstd, cot, made["grads"], after)
        return [made["d_inputs"]]

    d_kernel_sum = all_sum(
        d_kernel,
        axis,
        [nothing, projecting(0), projecting(half), back_projecting, norming],
        far_first=True,
    )
    if by_owner:
        d_w_out = last_swaps(held, axis, [made["far"], [made["grads"]]])
    return (
        made["outputs"].reshape(inputs.shape), made["d_inputs"].reshape(inputs.shape), d_w_out,
        d_kernel_sum, dsums[1], dsums[0],
    )


def solution(mesh):
    return jax.shard_map(
        on_device,
        mesh=mesh,
        in_specs=(P(None, "seq", None), P(), P(), P(), P(), P(), P(), P(None, "seq", None)),
        out_specs=(P(None, "seq", None), P(None, "seq", None), P("seq", None), P(), P(), P()),
        check_vma=False,
    )
```

```python
import functools

import jax
import jax.numpy as jnp
from jax import lax
from jax.experimental import pallas as pl
from jax.experimental.pallas import tpu as pltpu
from jax.sharding import PartitionSpec as P

EPSILON = 1e-05
BF = jnp.bfloat16
F32 = jnp.float32
LANES = 128
PAD = 16
HALO = 2 * PAD
MIB = 1 << 20
AXIS = "seq"
VMEM_MIB = 8


def params(mib):
    return pltpu.CompilerParams(vmem_limit_bytes=mib * MIB)


WHOLE = pl.BlockSpec(memory_space=pltpu.VMEM)
ANYWHERE = pl.BlockSpec(memory_space=pl.ANY)
FAR = pl.BlockSpec(memory_space=pltpu.HBM)
CW = 256


def cost(micros):
    return pl.CostEstimate(flops=0, bytes_accessed=int(micros * 3.0e6), transcendentals=0)


def shape(dims, dtype):
    return jax.ShapeDtypeStruct(dims, dtype)


def place():
    me = lax.axis_index(AXIS)
    last = lax.axis_size(AXIS) - 1
    return me % 2, me // 2, (me > 0).astype(F32), (me < last).astype(F32)


def far(array):
    return pltpu.with_memory_space_constraint(array, pltpu.HBM)


def near(dims, dtype):
    return pltpu.VMEM(dims, dtype)


def turn_body(cot_ref, *rest):
    mine_ref, other_ref, held_ref = rest[-3:]
    blocks = mine_ref.shape[0]
    per = mine_ref.shape[1]
    held_ref[...] = cot_ref[...].T
    core, half, _, _ = place()

    def step(j, _):
        row = pl.multiple_of(lax.bitwise_xor(half, j) * (2 * per), 2 * per)
        mine_ref[j] = held_ref[pl.ds(pl.multiple_of(row + core * per, per), per), :]
        other_ref[j] = held_ref[pl.ds(pl.multiple_of(row + (1 - core) * per, per), per), :]
        return 0

    lax.fori_loop(0, blocks, step, 0, unroll=2)


def turn(n, cot, after):
    rows, d = cot.shape
    out = shape((n // 2, d // n, rows), BF)
    return pl.pallas_call(
        turn_body,
        in_specs=[WHOLE] + [ANYWHERE] * len(after),
        out_specs=[WHOLE] * 2,
        out_shape=[out] * 2,
        scratch_shapes=[pltpu.VMEM((d, rows), BF)],
        compiler_params=params(VMEM_MIB),
        cost_estimate=cost(2),
        name="turn",
    )(cot, *after)


def edges_out(odd, first, last, a_ref, b_ref):
    @pl.when(odd == 0)
    def _():
        a_ref[...] = last
        b_ref[...] = first

    @pl.when(odd != 0)
    def _():
        a_ref[...] = first
        b_ref[...] = last


def front_body(
    utt, x_hbm, ln_hbm, gain_hbm, bias_hbm, w_hbm, cot_hbm,
    gated_ref, p_ref, q_ref, hat_ref, rstd_ref, vec_ref, a_ref, b_ref, normed_ref, x_ref, w_ref, cot_ref,
    ln_ref, gain_ref, bias_ref, x_sem, w_sem, cot_sem, row_sem,
):
    rows, d = x_ref.shape
    frames = rows // utt
    pieces = x_sem.shape[0]
    span = rows // pieces
    steps = d // CW

    def x_copy(i):
        at = pl.ds(i * span, span)
        return pltpu.make_async_copy(x_hbm.at[at], x_ref.at[at], x_sem.at[i])

    def w_copy(j, half):
        at = pl.ds(half * d + j * CW, CW)
        return pltpu.make_async_copy(w_hbm.at[:, at], w_ref.at[:, at], w_sem.at[j, half])

    row_copies = [
        pltpu.make_async_copy(source, target, row_sem.at[i])
        for i, (source, target) in enumerate(
            ((ln_hbm, ln_ref), (gain_hbm, gain_ref), (bias_hbm, bias_ref))
        )
    ]
    for copy in row_copies:
        copy.start()
    for i in range(pieces):
        x_copy(i).start()
    for half in range(2):
        w_copy(0, half).start()
    cots = []
    for u in range(utt):
        for side, at in enumerate((u * frames, (u + 1) * frames - PAD)):
            cots.append(
                pltpu.make_async_copy(
                    cot_hbm.at[pl.ds(at, PAD)], cot_ref.at[u, side], cot_sem.at[u, side]
                )
            )
            cots[-1].start()
    for copy in row_copies:
        copy.wait()
    for i, row_ref in enumerate((ln_ref, gain_ref, bias_ref)):
        vec_ref[i : i + 1, :] = row_ref[...].reshape(1, d)

    for i in range(pieces):
        x_copy(i).wait()
        for j in range(1 + i, steps if i == pieces - 1 else 2 + i):
            for half in range(2):
                w_copy(j, half).start()

        for k in range(i * span, (i + 1) * span, 16):
            at = slice(k, k + 16)
            x = x_ref[at, :].astype(F32)
            mu = jnp.sum(x, axis=-1, keepdims=True) * (1.0 / d)
            c = x - mu
            var = jnp.sum(c * c, axis=-1, keepdims=True) * (1.0 / d)
            rstd = lax.rsqrt(var + EPSILON)
            hat = c * rstd
            rstd_ref[at, :] = rstd
            hat_ref[at, :] = hat.astype(BF)
            normed_ref[at, :] = (hat * vec_ref[0:1, :]).astype(BF)

    odd = place()[0] != 0
    for j in range(steps):
        cols = slice(j * CW, (j + 1) * CW)
        for half in range(2):
            w_copy(j, half).wait()
        value = jnp.dot(normed_ref[...], w_ref[:, cols], preferred_element_type=F32)
        gate = jnp.dot(
            normed_ref[...], w_ref[:, d + j * CW : d + (j + 1) * CW], preferred_element_type=F32
        )
        sig = jax.nn.sigmoid(gate)
        gated = value * sig
        held = gated.astype(BF)
        gated_ref[:, cols] = held
        p_ref[:, cols] = sig.astype(BF)
        q_ref[:, cols] = (gated * (1.0 - sig)).astype(BF)
        shaped = held.reshape(utt, frames, CW)
        first, last = shaped[:, :HALO], shaped[:, frames - HALO :]
        a_ref[:, :HALO, cols] = jnp.where(odd, first, last)
        b_ref[:, :HALO, cols] = jnp.where(odd, last, first)
    for copy in cots:
        copy.wait()
    first, last = cot_ref[:, 0], cot_ref[:, 1]
    a_ref[:, HALO:, :] = jnp.where(odd, first, last)
    b_ref[:, HALO:, :] = jnp.where(odd, last, first)


def front(utt, x, ln_gain, bn_gain, bn_bias, w_in, cot):
    rows, d = x.shape
    out = near((rows, d), BF)
    edge = shape((utt, HALO + PAD, d), BF)
    return pl.pallas_call(
        functools.partial(front_body, utt),
        in_specs=[FAR] * 6,
        out_specs=[WHOLE] * 8,
        out_shape=[out] * 4 + [near((rows, 1), F32), near((3, d), F32)] + [edge] * 2,
        scratch_shapes=[
            pltpu.VMEM((rows, d), BF),
            pltpu.VMEM((rows, d), BF),
            pltpu.VMEM((d, 2 * d), BF),
            pltpu.VMEM((utt, 2, PAD, d), BF),
            pltpu.VMEM((d,), F32),
            pltpu.VMEM((d,), F32),
            pltpu.VMEM((d,), F32),
            pltpu.SemaphoreType.DMA((4,)),
            pltpu.SemaphoreType.DMA((d // CW, 2)),
            pltpu.SemaphoreType.DMA((utt, 2)),
            pltpu.SemaphoreType.DMA((3,)),
        ],
        compiler_params=params(24),
        cost_estimate=cost(10),
        name="front",
    )(*[far(a) for a in (x, ln_gain, bn_gain, bn_bias, w_in, cot)])


def lane_groups(first, last, work):
    def step(i, _):
        for slot in range(2):
            group = 2 * i + slot
            work(group, pl.ds(pl.multiple_of(group * LANES, LANES), LANES), slot)
        return 0

    lax.fori_loop(first // (2 * LANES), last // (2 * LANES), step, 0)


PHASES = 4
PIECES = 9


def thirds(x0, x1, x2):
    return [x1, x0 - x1, x2 - x1]


def sequences(x):
    tops = [
        (x[1], x[3], x[5]),
        (x[0] - x[1], x[2] - x[3], x[4] - x[5]),
        (x[2] - x[1], x[4] - x[3], x[6] - x[5]),
    ]
    return [piece for top in tops for piece in thirds(*top)]


def combined(h):
    tops = [(h[0] + h[1], h[2] + h[3]), (h[0], h[2]), (h[1], h[3])]
    return [piece for a, b in tops for piece in (a + b, a, b)]


def assembled(products):
    halves = []
    for top in range(3):
        m, p, q = (next(products) for _ in range(3))
        halves.append((m + p, m + q))
        if top:
            for j in range(2):
                yield 2 * j + top - 1, halves[0][j] + halves[top][j]


def phase(first, size):
    return pl.ds(first, size, PHASES)


def fill_sequences(pad_ref, shift, seq_ref, size):
    x = [pad_ref[phase(j + shift, size), :] for j in range(2 * PHASES - 1)]
    for i, piece in enumerate(sequences(x)):
        seq_ref[i] = piece


def filtered(seq_ref, taps_ref, order, count):
    for i in range(PIECES):
        acc = jnp.zeros((count, LANES), F32)
        for a in range(taps_ref.shape[1]):
            row = order(a)
            acc = acc + taps_ref[i, row : row + 1, :] * seq_ref[i, a : a + count, :]
        yield acc


def tap_factors(k_ref, lanes, held_ref, taps_ref):
    per = k_ref.shape[0] // PHASES
    held_ref[0 : per * PHASES, :] = k_ref[:, lanes]
    for i, piece in enumerate(combined([held_ref[phase(i, per), :] for i in range(PHASES)])):
        taps_ref[i] = piece


def conv_piece(pad_ref, seq_ref, taps_ref, count):
    fill_sequences(pad_ref, 1, seq_ref, count + taps_ref.shape[1])
    for i, y in assembled(filtered(seq_ref, taps_ref, lambda a: a, count)):
        pad_ref[phase(i, count), :] = y


def squares(values):
    values = values.reshape(values.shape[0] // 8, 8, LANES)
    return jnp.sum(values, axis=0), jnp.sum(values * values, axis=0)


def conv_mid_body(utt, g_ref, k_ref, conv_ref, sums_ref, pad_ref, seq_ref, taps_ref):
    d = g_ref.shape[1]
    frames = g_ref.shape[0] // utt
    mid = frames - HALO

    def work(_, lanes, slot):
        first = square = jnp.zeros((8, LANES), F32)
        tap_factors(k_ref, lanes, pad_ref.at[slot, 0], taps_ref.at[slot])
        for u in range(utt):
            pad = pad_ref.at[slot, u]
            pad[0:frames, :] = g_ref[u * frames : (u + 1) * frames, lanes].astype(F32)
            conv_piece(pad, seq_ref.at[slot, u], taps_ref.at[slot], mid // PHASES)
            y = pad[0:mid, :]
            start = u * (frames + HALO) + HALO
            conv_ref[start : start + mid, lanes] = y
            one, two = squares(y)
            first, square = first + one, square + two
        sums_ref[0:1, lanes] = jnp.sum(first, axis=0, keepdims=True)
        sums_ref[1:2, lanes] = jnp.sum(square, axis=0, keepdims=True)

    lane_groups(0, d, work)


def conv_scratch(utt, pieces, frames, count, per):
    return [
        pltpu.VMEM((2, utt * pieces, frames + 8, LANES), F32),
        pltpu.VMEM((2, utt * pieces, PIECES, count + per, LANES), F32),
        pltpu.VMEM((2, PIECES, per, LANES), F32),
    ]


def conv_mid(utt, gated, kernel):
    rows, d = gated.shape
    frames = rows // utt
    per = kernel.shape[0] // PHASES
    return pl.pallas_call(
        functools.partial(conv_mid_body, utt),
        in_specs=[WHOLE] * 2,
        out_specs=[WHOLE] * 2,
        out_shape=[near((utt * (frames + HALO), d), F32), near((2, d), F32)],
        scratch_shapes=conv_scratch(utt, 1, frames, (frames - HALO) // PHASES, per),
        compiler_params=params(VMEM_MIB),
        cost_estimate=cost(5),
        name="conv_mid",
    )(gated, kernel)


def conv_end_body(utt, g_ref, a_ref, b_ref, k_ref, _, some_ref, *rest):
    conv_ref, sums_ref, pad_ref, seq_ref, taps_ref = rest[-5:]
    d = g_ref.shape[1]
    frames = g_ref.shape[0] // utt
    odd = place()[0] != 0

    def work(_, lanes, slot):
        first = square = jnp.zeros((8, LANES), F32)
        tap_factors(k_ref, lanes, pad_ref.at[slot, 0], taps_ref.at[slot])
        for u in range(utt):
            a = a_ref[u, :HALO, lanes].astype(F32)
            b = b_ref[u, :HALO, lanes].astype(F32)
            start = u * (frames + HALO)
            for side in range(2):
                pad = pad_ref.at[slot, 2 * u + side]
                at = u * frames + side * (frames - HALO)
                here = g_ref[at : at + HALO, lanes].astype(F32)
                beside = jnp.where(odd, b, a) if side else jnp.where(odd, a, b)
                pad[side * HALO : (side + 1) * HALO, :] = beside
                pad[(1 - side) * HALO : (2 - side) * HALO, :] = here
                conv_piece(pad, seq_ref.at[slot, 2 * u + side], taps_ref.at[slot], HALO // PHASES)
                out = start + side * frames
                conv_ref[out : out + HALO, lanes] = pad[0:HALO, :]
                own = (1 - side) * PAD
                one, two = squares(pad[own : own + PAD, :])
                first, square = first + one, square + two
        sums_ref[0:1, lanes] = some_ref[0:1, lanes] + jnp.sum(first, axis=0, keepdims=True)
        sums_ref[1:2, lanes] = some_ref[1:2, lanes] + jnp.sum(square, axis=0, keepdims=True)

    lane_groups(0, d, work)


def conv_end(utt, gated, a, b, kernel, conv_some, sums_some, after):
    rows, d = gated.shape
    per = kernel.shape[0] // PHASES
    return pl.pallas_call(
        functools.partial(conv_end_body, utt),
        in_specs=[WHOLE] * 6 + [ANYWHERE] * len(after),
        out_specs=[WHOLE] * 2,
        out_shape=[near(conv_some.shape, F32), shape((2, d), F32)],
        scratch_shapes=conv_scratch(utt, 2, 2 * HALO, HALO // PHASES, per),
        input_output_aliases={4: 0},
        compiler_params=params(VMEM_MIB),
        cost_estimate=cost(2),
        name="conv_end",
    )(gated, a, b, kernel, conv_some, sums_some, *after)


def act_grad_body(cot_ref, w_ref, out_ref):
    for j in range(out_ref.shape[1] // CW):
        cols = slice(j * CW, (j + 1) * CW)
        out_ref[:, cols] = jnp.dot(cot_ref[...], w_ref[:, cols], preferred_element_type=F32)


def act_grad(cot, w_out):
    return pl.pallas_call(
        act_grad_body,
        in_specs=[WHOLE] * 2,
        out_specs=WHOLE,
        out_shape=near(cot.shape, F32),
        compiler_params=params(VMEM_MIB),
        cost_estimate=cost(3),
        name="act_grad",
    )(cot, w_out)


def act_grad_end_body(a_ref, b_ref, w_ref, *rest):
    out_ref = rest[-1]
    utt = a_ref.shape[0]
    odd = place()[0] != 0
    pieces = []
    for u in range(utt):
        a, b = a_ref[u, HALO:, :], b_ref[u, HALO:, :]
        pieces += [jnp.where(odd, a, b), jnp.where(odd, b, a)]
    cot = jnp.concatenate(pieces, axis=0)
    out_ref[...] = jnp.dot(cot, w_ref[...], preferred_element_type=F32)


def act_grad_end(a, b, w_out, after):
    utt, _, d = a.shape
    return pl.pallas_call(
        act_grad_end_body,
        in_specs=[WHOLE] * 3 + [ANYWHERE] * len(after),
        out_specs=WHOLE,
        out_shape=near((utt * HALO, d), F32),
        compiler_params=params(VMEM_MIB),
        cost_estimate=cost(2),
        name="act_grad_end",
    )(a, b, w_out, *after)


def middle_body(utt, total, conv_ref, sums_ref, vec_ref, own_ref, end_ref, *rest):
    act_ref, dbn_ref, dsums_ref = rest[-3:]
    d = conv_ref.shape[1]
    frames = own_ref.shape[0] // utt
    for j in range(d // CW):
        cols = slice(j * CW, (j + 1) * CW)
        mean = sums_ref[0:1, cols] * (1.0 / total)
        var = sums_ref[1:2, cols] * (1.0 / total) - mean * mean
        rstd = lax.rsqrt(var + EPSILON)

        def back(at, d_act):
            xhat = (conv_ref[at, cols] - mean) * rstd
            out = xhat * vec_ref[1:2, cols] + vec_ref[2:3, cols]
            sig = jax.nn.sigmoid(out)
            act = out * sig
            dbn = d_act * (sig + act * (1.0 - sig))
            dbn_ref[at, cols] = dbn
            return xhat, act, dbn

        bias = gain = 0.0
        for u in range(utt):
            start = u * (frames + HALO)
            back(slice(start, start + PAD), end_ref[u * HALO : u * HALO + PAD, cols])
            rows = slice(u * frames, (u + 1) * frames)
            xhat, act, dbn = back(slice(start + PAD, start + PAD + frames), own_ref[rows, cols])
            act_ref[rows, cols] = act.astype(BF)
            bias += jnp.sum(dbn, axis=0, keepdims=True)
            gain += jnp.sum(dbn * xhat, axis=0, keepdims=True)
            back(
                slice(start + PAD + frames, start + HALO + frames),
                end_ref[u * HALO + PAD : (u + 1) * HALO, cols],
            )
        dsums_ref[0:1, cols] = bias
        dsums_ref[1:2, cols] = gain


def middle(utt, total, conv_out, sums, vec, own, end, after):
    rows, d = own.shape
    return pl.pallas_call(
        functools.partial(middle_body, utt, total),
        in_specs=[WHOLE] * 5 + [ANYWHERE] * len(after),
        out_specs=[WHOLE] * 3,
        out_shape=[shape((rows, d), BF), near(conv_out.shape, F32), shape((2, d), F32)],
        compiler_params=params(VMEM_MIB),
        cost_estimate=cost(3),
        name="middle",
    )(conv_out, sums, vec, own, end, *after)


def grad_body(bits, ca_ref, cb_ref, acta_ref, actb_ref, *rest):
    out_refs = rest[-4:]
    blocks, per, rows = ca_ref.shape
    half = out_refs[0].shape[-1]
    ca = ca_ref[...].reshape(blocks * per, rows)
    cb = cb_ref[...].reshape(blocks * per, rows)
    for side, bit in enumerate(bits):
        send_ref, keep_ref = out_refs[2 * side], out_refs[2 * side + 1]
        for c in range(half // CW):
            cols = slice(c * CW, (c + 1) * CW)
            src = slice(side * half + c * CW, side * half + (c + 1) * CW)
            dw = jnp.dot(ca, acta_ref[:, src], preferred_element_type=F32)
            dw += jnp.dot(cb, actb_ref[:, src], preferred_element_type=F32)
            sent = kept = 0
            for j in range(blocks):
                block = dw[j * per : (j + 1) * per]
                if j & bit:
                    send_ref[sent, :, cols] = block.astype(BF)
                    sent += 1
                else:
                    keep_ref[kept, :, cols] = block
                    kept += 1


def grad(bits, cot_a, cot_b, act_a, act_b, after):
    blocks, per, _ = cot_a.shape
    d = act_a.shape[1]
    half = (blocks // 2, per, d // 2)
    return pl.pallas_call(
        functools.partial(grad_body, bits),
        in_specs=[WHOLE] * 4 + [ANYWHERE] * len(after),
        out_specs=[WHOLE] * 4,
        out_shape=[shape(half, BF), shape(half, F32)] * 2,
        compiler_params=params(VMEM_MIB),
        cost_estimate=cost(3.5),
        name="grad",
    )(cot_a, cot_b, act_a, act_b, *after)


def branch_body(x_ref, act_ref, w_ref, *rest):
    out_hbm, done_ref, out_ref, sem = rest[-4:]
    done_ref[...] = jnp.zeros(done_ref.shape, F32)
    copies = []
    for j in range(out_ref.shape[-1] // CW):
        cols = slice(j * CW, (j + 1) * CW)
        part = lax.dot_general(
            act_ref[...], w_ref[cols, :], (((1,), (1,)), ((), ())), preferred_element_type=F32
        )
        out_ref[:, cols] = (x_ref[:, cols].astype(F32) + part).astype(BF)
        copies.append(pltpu.make_async_copy(out_ref.at[:, cols], out_hbm.at[:, cols], sem.at[j]))
        copies[-1].start()
    for copy in copies:
        copy.wait()


def branch(x, act, w_out, after):
    rows, d = x.shape
    return pl.pallas_call(
        branch_body,
        in_specs=[WHOLE] * 3 + [ANYWHERE] * len(after),
        out_specs=[FAR, WHOLE],
        out_shape=[pltpu.HBM((rows, d), BF), near((8, LANES), F32)],
        scratch_shapes=[pltpu.VMEM((rows, d), BF), pltpu.SemaphoreType.DMA((d // CW,))],
        compiler_params=params(VMEM_MIB),
        cost_estimate=cost(4),
        name="branch",
    )(x, act, w_out, *after)


def grad_taps_body(
    utt, total, dbn_ref, conv_ref, sums_ref, dsums_ref, vec_ref, g_ref,
    dk_ref, seq_ref, pad_ref, held_ref, acc_ref,
):
    d = g_ref.shape[1]
    frames = g_ref.shape[0] // utt
    count = frames // PHASES
    taps = dk_ref.shape[0]
    per = taps // PHASES
    _, _, keep_lo, keep_hi = place()

    def work(group, lanes, slot):
        mean = sums_ref[0:1, lanes] * (1.0 / total)
        var = sums_ref[1:2, lanes] * (1.0 / total) - mean * mean
        rstd = lax.rsqrt(var + EPSILON)
        scale = rstd * vec_ref[1:2, lanes]
        cross = scale * rstd * (dsums_ref[1:2, lanes] * (1.0 / total))
        mean_grad = scale * (dsums_ref[0:1, lanes] * (1.0 / total))

        def d_conv(at):
            return dbn_ref[at, lanes] * scale - mean_grad - (conv_ref[at, lanes] - mean) * cross

        for u in range(utt):
            start = u * (frames + HALO)
            end = start + PAD + frames
            rows = slice(u * frames, (u + 1) * frames)
            pad = pad_ref.at[slot, u]
            pad[0:PAD, :] = d_conv(slice(start, start + PAD)) * keep_lo
            pad[PAD : PAD + frames, :] = d_conv(slice(start + PAD, end))
            pad[PAD + frames : HALO + frames, :] = d_conv(slice(end, end + PAD)) * keep_hi
            fill_sequences(pad_ref.at[slot, u], 0, seq_ref.at[group, u], count + per)
            pad_ref[slot, u, 0:frames, :] = g_ref[rows, lanes].astype(F32)
            g = [pad_ref[slot, u, phase(i, count), :] for i in range(PHASES)]
            for i, piece in enumerate(combined(g)):
                held_ref[slot, u, i] = piece

        def products():
            for i in range(PIECES):
                sums = [jnp.zeros((8, LANES), F32)] * per
                for u in range(utt):
                    for base in range(0, count, 32):
                        g = held_ref[slot, u, i, base : base + 32, :]
                        for a in range(per):
                            prod = g * seq_ref[group, u, i, base + a : base + a + 32, :]
                            sums[a] = sums[a] + jnp.sum(prod.reshape(4, 8, LANES), axis=0)
                yield jnp.stack(sums)

        for i, y in assembled(products()):
            for a in range(per):
                acc_ref[slot, taps - 1 - (PHASES * a + i)] = y[a]
        dk_ref[:, lanes] = jnp.sum(acc_ref[slot], axis=1).astype(BF)

    lane_groups(0, d, work)


def grad_taps(utt, total, taps, dbn, conv_out, sums, dsums, vec, gated):
    rows, d = gated.shape
    frames = rows // utt
    long = frames // PHASES + taps // PHASES
    return pl.pallas_call(
        functools.partial(grad_taps_body, utt, total),
        in_specs=[WHOLE] * 6,
        out_specs=[WHOLE] * 2,
        out_shape=[
            shape((taps, d), BF),
            near((d // LANES, utt, PIECES, long, LANES), F32),
        ],
        scratch_shapes=[
            pltpu.VMEM((2, utt, frames + 2 * PAD + 8, LANES), F32),
            pltpu.VMEM((2, utt, PIECES, frames // PHASES, LANES), F32),
            pltpu.VMEM((2, taps, 8, LANES), F32),
        ],
        compiler_params=params(VMEM_MIB),
        cost_estimate=cost(9),
        name="grad_taps",
    )(dbn, conv_out, sums, dsums, vec, gated)


def grad_proj_body(utt, start, seq_ref, k_ref, p_ref, q_ref, *rest):
    dv_ref, dg_ref, out_ref, taps_ref = rest[-4:]
    rows, width = dv_ref.shape
    frames = rows // utt
    count = frames // PHASES
    per = k_ref.shape[0] // PHASES

    def work(group, out, slot):
        lanes = pl.ds(pl.multiple_of(out.start + start, LANES), LANES)
        out_ref[slot, 0 : per * PHASES, :] = k_ref[:, lanes]
        k = [out_ref[slot, phase(PHASES - 1 - i, per), :] for i in range(PHASES)]
        for i, piece in enumerate(combined(k)):
            taps_ref[slot, i] = piece
        for u in range(utt):
            products = filtered(
                seq_ref.at[group + start // LANES, u], taps_ref.at[slot], lambda a: per - 1 - a, count
            )
            for i, y in assembled(products):
                out_ref[slot, phase(u * frames + i, count), :] = y
        acc = out_ref[slot]
        dv_ref[:, out] = (acc * p_ref[:, lanes].astype(F32)).astype(BF)
        dg_ref[:, out] = (acc * q_ref[:, lanes].astype(F32)).astype(BF)

    lane_groups(0, width, work)


def grad_proj(utt, start, width, seqs, kernel, p, q, after):
    rows = p.shape[0]
    out = near((rows, width), BF)
    return pl.pallas_call(
        functools.partial(grad_proj_body, utt, start),
        in_specs=[WHOLE] * 4 + [ANYWHERE] * len(after),
        out_specs=[WHOLE] * 2,
        out_shape=[out, out],
        scratch_shapes=[
            pltpu.VMEM((2, rows, LANES), F32),
            pltpu.VMEM((2, PIECES, kernel.shape[0] // PHASES, LANES), F32),
        ],
        compiler_params=params(VMEM_MIB),
        cost_estimate=cost(4),
        name="grad_proj",
    )(seqs, kernel, p, q, *after)


def back_proj_body(vec_ref, w_ref, *rest):
    pieces = rest[:4]
    out_ref = rest[-1]
    rows, d = out_ref.shape
    wide = pieces[0].shape[1]
    dims = (((1,), (1,)), ((), ()))
    for j in range(d // CW):
        cols = slice(j * CW, (j + 1) * CW)
        part = 0.0
        for k, piece in enumerate(pieces):
            part += lax.dot_general(
                piece[...], w_ref[cols, k * wide : (k + 1) * wide], dims, preferred_element_type=F32
            )
        out_ref[:, cols] = part * vec_ref[0:1, cols]


def back_proj(vec, w_in, pieces, after):
    rows = pieces[0].shape[0]
    d = w_in.shape[0]
    return pl.pallas_call(
        back_proj_body,
        in_specs=[WHOLE] * 6 + [ANYWHERE] * len(after),
        out_specs=WHOLE,
        out_shape=near((rows, d), F32),
        compiler_params=params(VMEM_MIB),
        cost_estimate=cost(5),
        name="back_proj",
    )(vec, w_in, *pieces, *after)


def back_norm_body(hat_ref, rstd_ref, cot_ref, acc_ref, *rest):
    out_hbm, done_ref, out_ref, sem = rest[-4:]
    done_ref[...] = jnp.zeros(done_ref.shape, F32)
    copies = []
    rows, d = hat_ref.shape
    span = rows // sem.shape[0]
    for i in range(0, rows, 16):
        at = slice(i, i + 16)
        hat = hat_ref[at, :].astype(F32)
        grads = acc_ref[at, :]
        m1 = jnp.sum(grads, axis=-1, keepdims=True) * (1.0 / d)
        m2 = jnp.sum(grads * hat, axis=-1, keepdims=True) * (1.0 / d)
        layer = rstd_ref[at, :] * (grads - m1 - hat * m2)
        out_ref[at, :] = (cot_ref[at, :].astype(F32) + layer).astype(BF)
        if (i + 16) % span == 0:
            piece = pl.ds(i + 16 - span, span)
            copies.append(
                pltpu.make_async_copy(out_ref.at[piece], out_hbm.at[piece], sem.at[i // span])
            )
            copies[-1].start()
    for copy in copies:
        copy.wait()


def back_norm(hat, rstd, cot, grads, after):
    rows, d = hat.shape
    return pl.pallas_call(
        back_norm_body,
        in_specs=[WHOLE] * 4 + [ANYWHERE] * len(after),
        out_specs=[FAR, WHOLE],
        out_shape=[pltpu.HBM((rows, d), BF), near((8, LANES), F32)],
        scratch_shapes=[pltpu.VMEM((rows, d), BF), pltpu.SemaphoreType.DMA((8,))],
        compiler_params=params(VMEM_MIB),
        cost_estimate=cost(3),
        name="back_norm",
    )(hat, rstd, cot, grads, *after)


def swap(block, axis, bit):
    count = lax.axis_size(axis)
    return lax.ppermute(block, axis, [(i, i ^ bit) for i in range(count)])


def is_power(count):
    return count & (count - 1) == 0


def add_body(own_ref, got_ref, *rest):
    out_ref = rest[-1]
    out_ref[...] = (own_ref[...].astype(F32) + got_ref[...].astype(F32)).astype(out_ref.dtype)


def add(own, got, dtype, after):
    return pl.pallas_call(
        add_body,
        in_specs=[WHOLE] * 2 + [ANYWHERE] * len(after),
        out_specs=WHOLE,
        out_shape=shape(own.shape, dtype),
        compiler_params=params(4),
        cost_estimate=cost(0.5),
        name="add",
    )(own, got, *after)


def all_sum(block, axis, fill=(), far_first=False):
    count = lax.axis_size(axis)
    if not is_power(count):
        for work in fill:
            work([])
        return lax.psum(block.astype(F32), axis)
    bits = [1 << i for i in range(count.bit_length() - 1)]
    if far_first:
        bits = bits[:1] + bits[3:] + bits[1:3]
    for step, bit in enumerate(bits):
        other = swap(block, axis, bit)
        after = fill[step]([block]) if step < len(fill) else []
        block = add(block, other, F32 if bit == bits[-1] else block.dtype, after)
    return block


def nothing(_):
    return []


def beside(a, b, axis):
    count = lax.axis_size(axis)
    pairs = []
    for low in range(1, count - 1, 2):
        pairs += [(low, low + 1), (low + 1, low)]
    return swap(a, axis, 1), lax.ppermute(b, axis, pairs)


def merge_body(sides, after, *refs):
    keep_out, send_out = refs[2 * sides + after :]
    blocks = refs[0].shape[0]
    wide = refs[0].shape[2]
    for side in range(sides):
        keep_ref, got_ref = refs[2 * side : 2 * side + 2]
        cols = slice(side * wide, (side + 1) * wide)
        for j in range(blocks):
            total = keep_ref[j] + got_ref[j].astype(F32)
            if j % 2:
                send_out[j // 2, :, cols] = total.astype(BF)
            else:
                keep_out[j // 2, :, cols] = total


def merge(pairs, after):
    blocks, per, wide = pairs[0][0].shape
    dims = (blocks // 2, per, wide * len(pairs))
    return pl.pallas_call(
        functools.partial(merge_body, len(pairs), len(after)),
        in_specs=[WHOLE] * (2 * len(pairs)) + [ANYWHERE] * len(after),
        out_specs=[WHOLE] * 2,
        out_shape=[shape(dims, F32), shape(dims, BF)],
        compiler_params=params(8),
        cost_estimate=cost(1),
        name="merge",
    )(*[a for pair in pairs for a in pair], *after)


def first_swaps(parts, axis, after):
    return [
        merge([(keep, swap(send, axis, device_bit))], after)
        for (keep, send), device_bit in zip(parts, (2, 4))
    ]


def last_swaps(held, axis, after):
    count = lax.axis_size(axis)
    after = list(after)
    pairs = [
        (keep, swap(send, axis, device_bit)) for (keep, send), device_bit in zip(held, (4, 2))
    ]
    bit = 8
    if bit == count:
        return jnp.concatenate([keep + got for keep, got in pairs], axis=-1)[0]
    while True:
        keep, send = merge(pairs, after.pop(0) if after else [])
        got = swap(send, axis, bit)
        bit *= 2
        if bit == count:
            return add(keep[0], got[0], F32, [])
        pairs = [(keep, got)]


def on_device(inputs, ln_gain, w_in, kernel, bn_gain, bn_bias, w_out, cotangent):
    axis = AXIS
    n = lax.axis_size(axis)
    me = lax.axis_index(axis).astype(jnp.int32)
    utt, frames, d = inputs.shape
    rows = utt * frames
    half = d // 2
    total = rows * n
    x = inputs.reshape(rows, d)
    cot = cotangent.reshape(rows, d)
    by_owner = is_power(n) and n >= 8 and d % n == 0 and (d // n) % 16 == 0

    gated, p, q, hat, rstd, vec, ga, gb = front(utt, x, ln_gain, bn_gain, bn_bias, w_in, cot)
    ga, gb = beside(ga, gb, axis)
    conv_some, sums_some = conv_mid(utt, gated, kernel)
    own = act_grad(cot, w_out)
    conv_out, sums = conv_end(utt, gated, ga, gb, kernel, conv_some, sums_some, [own])
    made = {}

    def turning(after):
        made["a"], other = turn(n, cot, after)
        made["b"] = swap(other, axis, 1)
        return [made["a"]]

    def ending(after):
        made["end"] = act_grad_end(ga, gb, w_out, after)
        return [made["end"]]

    if by_owner:
        sums = all_sum(sums, axis, [nothing, turning, nothing, nothing, ending])
        waits = [made["b"]]
    else:
        sums = all_sum(sums, axis, [nothing, ending])
        waits = []

    act, dbn, dsums = middle(utt, total, conv_out, sums, vec, own, made["end"], waits)

    def branching(after):
        made["outputs"], done = branch(x, act, w_out, after)
        return [done]

    def grading(after):
        made["grad"] = grad((1, 2), made["a"], made["b"], act, act_b, after)
        return [made["grad"][0]]

    if by_owner:
        act_b = swap(act, axis, 1)
        dsums = all_sum(dsums, axis, [nothing, branching, nothing, grading])
        send_l, keep_l, send_r, keep_r = made["grad"]
        held = first_swaps([(keep_l, send_l), (keep_r, send_r)], axis, [dsums])
    else:
        dsums = all_sum(dsums, axis, [nothing, branching])
        dw = lax.dot_general(cot, act, (((0,), (0,)), ((), ())), preferred_element_type=F32)
        d_w_out = lax.psum_scatter(dw, axis, scatter_dimension=0, tiled=True)

    d_kernel, d_conv = grad_taps(
        utt, total, kernel.shape[0], dbn, conv_out, sums, dsums, vec, gated
    )
    half = d // 2

    def projecting(start):
        def work(after):
            made[start] = grad_proj(utt, start, half, d_conv, kernel, p, q, after)
            return [made[start][0]]

        return work

    def back_projecting(after):
        left, right = made[0], made[half]
        made["far"] = after
        made["grads"] = back_proj(vec, w_in, (left[0], right[0], left[1], right[1]), after)
        return [made["grads"]]

    def norming(after):
        made["d_inputs"], done = back_norm(hat, rstd, cot, made["grads"], after)
        return [done]

    d_kernel_sum = all_sum(
        d_kernel,
        axis,
        [nothing, projecting(0), projecting(half), back_projecting, norming],
        far_first=True,
    )
    if by_owner:
        d_w_out = last_swaps(held, axis, [made["far"], [made["grads"]]])
    return (
        made["outputs"].reshape(inputs.shape), made["d_inputs"].reshape(inputs.shape), d_w_out,
        d_kernel_sum, dsums[1], dsums[0],
    )


def solution(mesh):
    return jax.shard_map(
        on_device,
        mesh=mesh,
        in_specs=(P(None, "seq", None), P(), P(), P(), P(), P(), P(), P(None, "seq", None)),
        out_specs=(P(None, "seq", None), P(None, "seq", None), P("seq", None), P(), P(), P()),
        check_vma=False,
    )
```

```python
import functools

import jax
import jax.numpy as jnp
from jax import lax
from jax.experimental import pallas as pl
from jax.experimental.pallas import tpu as pltpu
from jax.sharding import PartitionSpec as P

EPSILON = 1e-05
BF = jnp.bfloat16
F32 = jnp.float32
LANES = 128
PAD = 16
HALO = 2 * PAD
MIB = 1 << 20
AXIS = "seq"
VMEM_MIB = 8


def params(mib):
    return pltpu.CompilerParams(vmem_limit_bytes=mib * MIB)


WHOLE = pl.BlockSpec(memory_space=pltpu.VMEM)
ANYWHERE = pl.BlockSpec(memory_space=pl.ANY)
FAR = pl.BlockSpec(memory_space=pltpu.HBM)
CW = 256


def cost(micros):
    return pl.CostEstimate(flops=0, bytes_accessed=int(micros * 3.0e6), transcendentals=0)


def shape(dims, dtype):
    return jax.ShapeDtypeStruct(dims, dtype)


def place():
    me = lax.axis_index(AXIS)
    last = lax.axis_size(AXIS) - 1
    return me % 2, me // 2, (me > 0).astype(F32), (me < last).astype(F32)


def far(array):
    return pltpu.with_memory_space_constraint(array, pltpu.HBM)


def near(dims, dtype):
    return pltpu.VMEM(dims, dtype)


def turn_body(cot_ref, *rest):
    mine_ref, other_ref, held_ref = rest[-3:]
    blocks = mine_ref.shape[0]
    per = mine_ref.shape[1]
    held_ref[...] = cot_ref[...].T
    core, half, _, _ = place()

    def step(j, _):
        row = pl.multiple_of(lax.bitwise_xor(half, j) * (2 * per), 2 * per)
        mine_ref[j] = held_ref[pl.ds(pl.multiple_of(row + core * per, per), per), :]
        other_ref[j] = held_ref[pl.ds(pl.multiple_of(row + (1 - core) * per, per), per), :]
        return 0

    lax.fori_loop(0, blocks, step, 0, unroll=2)


def turn(n, cot, after):
    rows, d = cot.shape
    out = shape((n // 2, d // n, rows), BF)
    return pl.pallas_call(
        turn_body,
        in_specs=[WHOLE] + [ANYWHERE] * len(after),
        out_specs=[WHOLE] * 2,
        out_shape=[out] * 2,
        scratch_shapes=[pltpu.VMEM((d, rows), BF)],
        compiler_params=params(VMEM_MIB),
        cost_estimate=cost(2),
        name="turn",
    )(cot, *after)


def edges_out(odd, first, last, a_ref, b_ref):
    @pl.when(odd == 0)
    def _():
        a_ref[...] = last
        b_ref[...] = first

    @pl.when(odd != 0)
    def _():
        a_ref[...] = first
        b_ref[...] = last


def front_body(
    utt, x_hbm, ln_hbm, gain_hbm, bias_hbm, w_hbm, cot_hbm,
    gated_ref, p_ref, q_ref, hat_ref, rstd_ref, vec_ref, a_ref, b_ref, normed_ref, x_ref, w_ref, cot_ref,
    ln_ref, gain_ref, bias_ref, x_sem, w_sem, cot_sem, row_sem,
):
    rows, d = x_ref.shape
    frames = rows // utt
    pieces = x_sem.shape[0]
    span = rows // pieces
    steps = d // CW

    def x_copy(i):
        at = pl.ds(i * span, span)
        return pltpu.make_async_copy(x_hbm.at[at], x_ref.at[at], x_sem.at[i])

    def w_copy(j, half):
        at = pl.ds(half * d + j * CW, CW)
        return pltpu.make_async_copy(w_hbm.at[:, at], w_ref.at[:, at], w_sem.at[j, half])

    row_copies = [
        pltpu.make_async_copy(source, target, row_sem.at[i])
        for i, (source, target) in enumerate(
            ((ln_hbm, ln_ref), (gain_hbm, gain_ref), (bias_hbm, bias_ref))
        )
    ]
    for copy in row_copies:
        copy.start()
    for i in range(pieces):
        x_copy(i).start()
    for half in range(2):
        w_copy(0, half).start()
    cots = []
    for u in range(utt):
        for side, at in enumerate((u * frames, (u + 1) * frames - PAD)):
            cots.append(
                pltpu.make_async_copy(
                    cot_hbm.at[pl.ds(at, PAD)], cot_ref.at[u, side], cot_sem.at[u, side]
                )
            )
            cots[-1].start()
    for copy in row_copies:
        copy.wait()
    for i, row_ref in enumerate((ln_ref, gain_ref, bias_ref)):
        vec_ref[i : i + 1, :] = row_ref[...].reshape(1, d)

    for i in range(pieces):
        x_copy(i).wait()
        for j in range(1 + i, steps if i == pieces - 1 else 2 + i):
            for half in range(2):
                w_copy(j, half).start()

        for k in range(i * span, (i + 1) * span, 16):
            at = slice(k, k + 16)
            x = x_ref[at, :].astype(F32)
            mu = jnp.sum(x, axis=-1, keepdims=True) * (1.0 / d)
            c = x - mu
            var = jnp.sum(c * c, axis=-1, keepdims=True) * (1.0 / d)
            rstd = lax.rsqrt(var + EPSILON)
            hat = c * rstd
            rstd_ref[at, :] = rstd
            hat_ref[at, :] = hat.astype(BF)
            normed_ref[at, :] = (hat * vec_ref[0:1, :]).astype(BF)

    odd = place()[0] != 0
    for j in range(steps):
        cols = slice(j * CW, (j + 1) * CW)
        for half in range(2):
            w_copy(j, half).wait()
        value = jnp.dot(normed_ref[...], w_ref[:, cols], preferred_element_type=F32)
        gate = jnp.dot(
            normed_ref[...], w_ref[:, d + j * CW : d + (j + 1) * CW], preferred_element_type=F32
        )
        sig = jax.nn.sigmoid(gate)
        gated = value * sig
        held = gated.astype(BF)
        gated_ref[:, cols] = held
        p_ref[:, cols] = sig.astype(BF)
        q_ref[:, cols] = (gated * (1.0 - sig)).astype(BF)
        shaped = held.reshape(utt, frames, CW)
        first, last = shaped[:, :HALO], shaped[:, frames - HALO :]
        a_ref[:, :HALO, cols] = jnp.where(odd, first, last)
        b_ref[:, :HALO, cols] = jnp.where(odd, last, first)
    for copy in cots:
        copy.wait()
    first, last = cot_ref[:, 0], cot_ref[:, 1]
    a_ref[:, HALO:, :] = jnp.where(odd, first, last)
    b_ref[:, HALO:, :] = jnp.where(odd, last, first)


def front(utt, x, ln_gain, bn_gain, bn_bias, w_in, cot):
    rows, d = x.shape
    out = near((rows, d), BF)
    edge = shape((utt, HALO + PAD, d), BF)
    return pl.pallas_call(
        functools.partial(front_body, utt),
        in_specs=[FAR] * 6,
        out_specs=[WHOLE] * 8,
        out_shape=[out] * 4 + [near((rows, 1), F32), near((3, d), F32)] + [edge] * 2,
        scratch_shapes=[
            pltpu.VMEM((rows, d), BF),
            pltpu.VMEM((rows, d), BF),
            pltpu.VMEM((d, 2 * d), BF),
            pltpu.VMEM((utt, 2, PAD, d), BF),
            pltpu.VMEM((d,), F32),
            pltpu.VMEM((d,), F32),
            pltpu.VMEM((d,), F32),
            pltpu.SemaphoreType.DMA((4,)),
            pltpu.SemaphoreType.DMA((d // CW, 2)),
            pltpu.SemaphoreType.DMA((utt, 2)),
            pltpu.SemaphoreType.DMA((3,)),
        ],
        compiler_params=params(24),
        cost_estimate=cost(10),
        name="front",
    )(*[far(a) for a in (x, ln_gain, bn_gain, bn_bias, w_in, cot)])


def lane_groups(first, last, work):
    def step(i, _):
        for slot in range(2):
            group = 2 * i + slot
            work(group, pl.ds(pl.multiple_of(group * LANES, LANES), LANES), slot)
        return 0

    lax.fori_loop(first // (2 * LANES), last // (2 * LANES), step, 0)


PHASES = 4
PIECES = 9


def thirds(x0, x1, x2):
    return [x1, x0 - x1, x2 - x1]


def sequences(x):
    tops = [
        (x[1], x[3], x[5]),
        (x[0] - x[1], x[2] - x[3], x[4] - x[5]),
        (x[2] - x[1], x[4] - x[3], x[6] - x[5]),
    ]
    return [piece for top in tops for piece in thirds(*top)]


def combined(h):
    tops = [(h[0] + h[1], h[2] + h[3]), (h[0], h[2]), (h[1], h[3])]
    return [piece for a, b in tops for piece in (a + b, a, b)]


def assembled(products):
    halves = []
    for top in range(3):
        m, p, q = (next(products) for _ in range(3))
        halves.append((m + p, m + q))
        if top:
            for j in range(2):
                yield 2 * j + top - 1, halves[0][j] + halves[top][j]


def phase(first, size):
    return pl.ds(first, size, PHASES)


def fill_sequences(pad_ref, shift, seq_ref, size):
    x = [pad_ref[phase(j + shift, size), :] for j in range(2 * PHASES - 1)]
    for i, piece in enumerate(sequences(x)):
        seq_ref[i] = piece


def filtered(seq_ref, taps_ref, order, count):
    for i in range(PIECES):
        acc = jnp.zeros((count, LANES), F32)
        for a in range(taps_ref.shape[1]):
            row = order(a)
            acc = acc + taps_ref[i, row : row + 1, :] * seq_ref[i, a : a + count, :]
        yield acc


def tap_factors(k_ref, lanes, held_ref, taps_ref):
    per = k_ref.shape[0] // PHASES
    held_ref[0 : per * PHASES, :] = k_ref[:, lanes]
    for i, piece in enumerate(combined([held_ref[phase(i, per), :] for i in range(PHASES)])):
        taps_ref[i] = piece


def conv_piece(pad_ref, seq_ref, taps_ref, count):
    fill_sequences(pad_ref, 1, seq_ref, count + taps_ref.shape[1])
    for i, y in assembled(filtered(seq_ref, taps_ref, lambda a: a, count)):
        pad_ref[phase(i, count), :] = y


def squares(values):
    values = values.reshape(values.shape[0] // 8, 8, LANES)
    return jnp.sum(values, axis=0), jnp.sum(values * values, axis=0)


def conv_mid_body(utt, g_ref, k_ref, conv_ref, sums_ref, pad_ref, seq_ref, taps_ref):
    d = g_ref.shape[1]
    frames = g_ref.shape[0] // utt
    mid = frames - HALO

    def work(_, lanes, slot):
        first = square = jnp.zeros((8, LANES), F32)
        tap_factors(k_ref, lanes, pad_ref.at[slot, 0], taps_ref.at[slot])
        for u in range(utt):
            pad = pad_ref.at[slot, u]
            pad[0:frames, :] = g_ref[u * frames : (u + 1) * frames, lanes].astype(F32)
            conv_piece(pad, seq_ref.at[slot, u], taps_ref.at[slot], mid // PHASES)
            y = pad[0:mid, :]
            start = u * (frames + HALO) + HALO
            conv_ref[start : start + mid, lanes] = y
            one, two = squares(y)
            first, square = first + one, square + two
        sums_ref[0:1, lanes] = jnp.sum(first, axis=0, keepdims=True)
        sums_ref[1:2, lanes] = jnp.sum(square, axis=0, keepdims=True)

    lane_groups(0, d, work)


def conv_scratch(utt, pieces, frames, count, per):
    return [
        pltpu.VMEM((2, utt * pieces, frames + 8, LANES), F32),
        pltpu.VMEM((2, utt * pieces, PIECES, count + per, LANES), F32),
        pltpu.VMEM((2, PIECES, per, LANES), F32),
    ]


def conv_mid(utt, gated, kernel):
    rows, d = gated.shape
    frames = rows // utt
    per = kernel.shape[0] // PHASES
    return pl.pallas_call(
        functools.partial(conv_mid_body, utt),
        in_specs=[WHOLE] * 2,
        out_specs=[WHOLE] * 2,
        out_shape=[near((utt * (frames + HALO), d), F32), near((2, d), F32)],
        scratch_shapes=conv_scratch(utt, 1, frames, (frames - HALO) // PHASES, per),
        compiler_params=params(VMEM_MIB),
        cost_estimate=cost(5),
        name="conv_mid",
    )(gated, kernel)


def conv_end_body(utt, g_ref, a_ref, b_ref, k_ref, _, some_ref, *rest):
    conv_ref, sums_ref, pad_ref, seq_ref, taps_ref = rest[-5:]
    d = g_ref.shape[1]
    frames = g_ref.shape[0] // utt
    odd = place()[0] != 0

    def work(_, lanes, slot):
        first = square = jnp.zeros((8, LANES), F32)
        tap_factors(k_ref, lanes, pad_ref.at[slot, 0], taps_ref.at[slot])
        for u in range(utt):
            a = a_ref[u, :HALO, lanes].astype(F32)
            b = b_ref[u, :HALO, lanes].astype(F32)
            start = u * (frames + HALO)
            for side in range(2):
                pad = pad_ref.at[slot, 2 * u + side]
                at = u * frames + side * (frames - HALO)
                here = g_ref[at : at + HALO, lanes].astype(F32)
                beside = jnp.where(odd, b, a) if side else jnp.where(odd, a, b)
                pad[side * HALO : (side + 1) * HALO, :] = beside
                pad[(1 - side) * HALO : (2 - side) * HALO, :] = here
                conv_piece(pad, seq_ref.at[slot, 2 * u + side], taps_ref.at[slot], HALO // PHASES)
                out = start + side * frames
                conv_ref[out : out + HALO, lanes] = pad[0:HALO, :]
                own = (1 - side) * PAD
                one, two = squares(pad[own : own + PAD, :])
                first, square = first + one, square + two
        sums_ref[0:1, lanes] = some_ref[0:1, lanes] + jnp.sum(first, axis=0, keepdims=True)
        sums_ref[1:2, lanes] = some_ref[1:2, lanes] + jnp.sum(square, axis=0, keepdims=True)

    lane_groups(0, d, work)


def conv_end(utt, gated, a, b, kernel, conv_some, sums_some, after):
    rows, d = gated.shape
    per = kernel.shape[0] // PHASES
    return pl.pallas_call(
        functools.partial(conv_end_body, utt),
        in_specs=[WHOLE] * 6 + [ANYWHERE] * len(after),
        out_specs=[WHOLE] * 2,
        out_shape=[near(conv_some.shape, F32), shape((2, d), F32)],
        scratch_shapes=conv_scratch(utt, 2, 2 * HALO, HALO // PHASES, per),
        input_output_aliases={4: 0},
        compiler_params=params(VMEM_MIB),
        cost_estimate=cost(2),
        name="conv_end",
    )(gated, a, b, kernel, conv_some, sums_some, *after)


def act_grad_body(start, cot_ref, w_ref, *rest):
    out_ref = rest[-1]
    for j in range(out_ref.shape[1] // CW):
        cols = slice(j * CW, (j + 1) * CW)
        source = slice(start + j * CW, start + (j + 1) * CW)
        out_ref[:, cols] = jnp.dot(cot_ref[...], w_ref[:, source], preferred_element_type=F32)


def act_grad(start, width, cot, w_out, after):
    return pl.pallas_call(
        functools.partial(act_grad_body, start),
        in_specs=[WHOLE] * 2 + [ANYWHERE] * len(after),
        out_specs=WHOLE,
        out_shape=near((cot.shape[0], width), F32),
        compiler_params=params(VMEM_MIB),
        cost_estimate=cost(1.5),
        name="act_grad",
    )(cot, w_out, *after)


def act_grad_end_body(a_ref, b_ref, w_ref, *rest):
    out_ref = rest[-1]
    utt = a_ref.shape[0]
    odd = place()[0] != 0
    pieces = []
    for u in range(utt):
        a, b = a_ref[u, HALO:, :], b_ref[u, HALO:, :]
        pieces += [jnp.where(odd, a, b), jnp.where(odd, b, a)]
    cot = jnp.concatenate(pieces, axis=0)
    out_ref[...] = jnp.dot(cot, w_ref[...], preferred_element_type=F32)


def act_grad_end(a, b, w_out, after):
    utt, _, d = a.shape
    return pl.pallas_call(
        act_grad_end_body,
        in_specs=[WHOLE] * 3 + [ANYWHERE] * len(after),
        out_specs=WHOLE,
        out_shape=near((utt * HALO, d), F32),
        compiler_params=params(VMEM_MIB),
        cost_estimate=cost(2),
        name="act_grad_end",
    )(a, b, w_out, *after)


def middle_body(utt, total, conv_ref, sums_ref, vec_ref, left_ref, right_ref, end_ref, *rest):
    act_ref, dbn_ref, dsums_ref = rest[-3:]
    d = conv_ref.shape[1]
    frames = left_ref.shape[0] // utt
    per_half = left_ref.shape[1] // CW
    for j in range(d // CW):
        cols = slice(j * CW, (j + 1) * CW)
        own_ref = (left_ref, right_ref)[j // per_half]
        own_cols = slice(j % per_half * CW, (j % per_half + 1) * CW)
        mean = sums_ref[0:1, cols] * (1.0 / total)
        var = sums_ref[1:2, cols] * (1.0 / total) - mean * mean
        rstd = lax.rsqrt(var + EPSILON)

        def back(at, d_act):
            xhat = (conv_ref[at, cols] - mean) * rstd
            out = xhat * vec_ref[1:2, cols] + vec_ref[2:3, cols]
            sig = jax.nn.sigmoid(out)
            act = out * sig
            dbn = d_act * (sig + act * (1.0 - sig))
            dbn_ref[at, cols] = dbn
            return xhat, act, dbn

        bias = gain = 0.0
        for u in range(utt):
            start = u * (frames + HALO)
            back(slice(start, start + PAD), end_ref[u * HALO : u * HALO + PAD, cols])
            rows = slice(u * frames, (u + 1) * frames)
            xhat, act, dbn = back(slice(start + PAD, start + PAD + frames), own_ref[rows, own_cols])
            act_ref[rows, cols] = act.astype(BF)
            bias += jnp.sum(dbn, axis=0, keepdims=True)
            gain += jnp.sum(dbn * xhat, axis=0, keepdims=True)
            back(
                slice(start + PAD + frames, start + HALO + frames),
                end_ref[u * HALO + PAD : (u + 1) * HALO, cols],
            )
        dsums_ref[0:1, cols] = bias
        dsums_ref[1:2, cols] = gain


def middle(utt, total, conv_out, sums, vec, left, right, end, after):
    rows = left.shape[0]
    d = conv_out.shape[1]
    return pl.pallas_call(
        functools.partial(middle_body, utt, total),
        in_specs=[WHOLE] * 6 + [ANYWHERE] * len(after),
        out_specs=[WHOLE] * 3,
        out_shape=[shape((rows, d), BF), near(conv_out.shape, F32), shape((2, d), F32)],
        compiler_params=params(VMEM_MIB),
        cost_estimate=cost(3),
        name="middle",
    )(conv_out, sums, vec, left, right, end, *after)


def grad_body(bits, ca_ref, cb_ref, acta_ref, actb_ref, *rest):
    out_refs = rest[-4:]
    blocks, per, rows = ca_ref.shape
    half = out_refs[0].shape[-1]
    ca = ca_ref[...].reshape(blocks * per, rows)
    cb = cb_ref[...].reshape(blocks * per, rows)
    for side, bit in enumerate(bits):
        send_ref, keep_ref = out_refs[2 * side], out_refs[2 * side + 1]
        for c in range(half // CW):
            cols = slice(c * CW, (c + 1) * CW)
            src = slice(side * half + c * CW, side * half + (c + 1) * CW)
            dw = jnp.dot(ca, acta_ref[:, src], preferred_element_type=F32)
            dw += jnp.dot(cb, actb_ref[:, src], preferred_element_type=F32)
            sent = kept = 0
            for j in range(blocks):
                block = dw[j * per : (j + 1) * per]
                if j & bit:
                    send_ref[sent, :, cols] = block.astype(BF)
                    sent += 1
                else:
                    keep_ref[kept, :, cols] = block
                    kept += 1


def grad(bits, cot_a, cot_b, act_a, act_b, after):
    blocks, per, _ = cot_a.shape
    d = act_a.shape[1]
    half = (blocks // 2, per, d // 2)
    return pl.pallas_call(
        functools.partial(grad_body, bits),
        in_specs=[WHOLE] * 4 + [ANYWHERE] * len(after),
        out_specs=[WHOLE] * 4,
        out_shape=[shape(half, BF), shape(half, F32)] * 2,
        compiler_params=params(VMEM_MIB),
        cost_estimate=cost(3.5),
        name="grad",
    )(cot_a, cot_b, act_a, act_b, *after)


def branch_body(start, x_ref, act_ref, w_ref, *rest):
    out_hbm, done_ref, out_ref, sem = rest[-4:]
    done_ref[...] = jnp.zeros(done_ref.shape, F32)
    copies = []
    for j in range(sem.shape[0]):
        cols = slice(start + j * CW, start + (j + 1) * CW)
        here = slice(j * CW, (j + 1) * CW)
        part = lax.dot_general(
            act_ref[...], w_ref[cols, :], (((1,), (1,)), ((), ())), preferred_element_type=F32
        )
        out_ref[:, here] = (x_ref[:, cols].astype(F32) + part).astype(BF)
        copies.append(pltpu.make_async_copy(out_ref.at[:, here], out_hbm.at[:, cols], sem.at[j]))
        copies[-1].start()
    for copy in copies:
        copy.wait()


def branch(start, width, x, act, w_out, some, after):
    rows, d = x.shape
    return pl.pallas_call(
        functools.partial(branch_body, start),
        in_specs=[WHOLE] * 3 + [FAR] * len(some) + [ANYWHERE] * len(after),
        out_specs=[FAR, WHOLE],
        out_shape=[pltpu.HBM((rows, d), BF), near((8, LANES), F32)],
        scratch_shapes=[pltpu.VMEM((rows, width), BF), pltpu.SemaphoreType.DMA((width // CW,))],
        input_output_aliases={3: 0} if some else {},
        compiler_params=params(VMEM_MIB),
        cost_estimate=cost(2),
        name="branch",
    )(x, act, w_out, *some, *after)


def grad_taps_body(
    utt, total, dbn_ref, conv_ref, sums_ref, dsums_ref, vec_ref, g_ref,
    dk_ref, seq_ref, bias_ref, gain_ref, pad_ref, held_ref, acc_ref,
):
    d = g_ref.shape[1]
    frames = g_ref.shape[0] // utt
    count = frames // PHASES
    taps = dk_ref.shape[0]
    per = taps // PHASES
    _, _, keep_lo, keep_hi = place()
    bias_ref[...] = dsums_ref[0:1, :].reshape(d)
    gain_ref[...] = dsums_ref[1:2, :].reshape(d)

    def work(group, lanes, slot):
        mean = sums_ref[0:1, lanes] * (1.0 / total)
        var = sums_ref[1:2, lanes] * (1.0 / total) - mean * mean
        rstd = lax.rsqrt(var + EPSILON)
        scale = rstd * vec_ref[1:2, lanes]
        cross = scale * rstd * (dsums_ref[1:2, lanes] * (1.0 / total))
        mean_grad = scale * (dsums_ref[0:1, lanes] * (1.0 / total))

        def d_conv(at):
            return dbn_ref[at, lanes] * scale - mean_grad - (conv_ref[at, lanes] - mean) * cross

        for u in range(utt):
            start = u * (frames + HALO)
            end = start + PAD + frames
            rows = slice(u * frames, (u + 1) * frames)
            pad = pad_ref.at[slot, u]
            pad[0:PAD, :] = d_conv(slice(start, start + PAD)) * keep_lo
            pad[PAD : PAD + frames, :] = d_conv(slice(start + PAD, end))
            pad[PAD + frames : HALO + frames, :] = d_conv(slice(end, end + PAD)) * keep_hi
            fill_sequences(pad_ref.at[slot, u], 0, seq_ref.at[group, u], count + per)
            pad_ref[slot, u, 0:frames, :] = g_ref[rows, lanes].astype(F32)
            g = [pad_ref[slot, u, phase(i, count), :] for i in range(PHASES)]
            for i, piece in enumerate(combined(g)):
                held_ref[slot, u, i] = piece

        def products():
            for i in range(PIECES):
                sums = [jnp.zeros((8, LANES), F32)] * per
                for u in range(utt):
                    for base in range(0, count, 32):
                        g = held_ref[slot, u, i, base : base + 32, :]
                        for a in range(per):
                            prod = g * seq_ref[group, u, i, base + a : base + a + 32, :]
                            sums[a] = sums[a] + jnp.sum(prod.reshape(4, 8, LANES), axis=0)
                yield jnp.stack(sums)

        for i, y in assembled(products()):
            for a in range(per):
                acc_ref[slot, taps - 1 - (PHASES * a + i)] = y[a]
        dk_ref[:, lanes] = jnp.sum(acc_ref[slot], axis=1).astype(BF)

    lane_groups(0, d, work)


def grad_taps(utt, total, taps, dbn, conv_out, sums, dsums, vec, gated):
    rows, d = gated.shape
    frames = rows // utt
    long = frames // PHASES + taps // PHASES
    return pl.pallas_call(
        functools.partial(grad_taps_body, utt, total),
        in_specs=[WHOLE] * 6,
        out_specs=[WHOLE] * 4,
        out_shape=[
            shape((taps, d), BF),
            near((d // LANES, utt, PIECES, long, LANES), F32),
            shape((d,), F32),
            shape((d,), F32),
        ],
        scratch_shapes=[
            pltpu.VMEM((2, utt, frames + 2 * PAD + 8, LANES), F32),
            pltpu.VMEM((2, utt, PIECES, frames // PHASES, LANES), F32),
            pltpu.VMEM((2, taps, 8, LANES), F32),
        ],
        compiler_params=params(VMEM_MIB),
        cost_estimate=cost(9),
        name="grad_taps",
    )(dbn, conv_out, sums, dsums, vec, gated)


def grad_proj_body(utt, start, seq_ref, k_ref, p_ref, q_ref, *rest):
    dv_ref, dg_ref, out_ref, taps_ref = rest[-4:]
    rows, width = dv_ref.shape
    frames = rows // utt
    count = frames // PHASES
    per = k_ref.shape[0] // PHASES

    def work(group, out, slot):
        lanes = pl.ds(pl.multiple_of(out.start + start, LANES), LANES)
        out_ref[slot, 0 : per * PHASES, :] = k_ref[:, lanes]
        k = [out_ref[slot, phase(PHASES - 1 - i, per), :] for i in range(PHASES)]
        for i, piece in enumerate(combined(k)):
            taps_ref[slot, i] = piece
        for u in range(utt):
            products = filtered(
                seq_ref.at[group + start // LANES, u], taps_ref.at[slot], lambda a: per - 1 - a, count
            )
            for i, y in assembled(products):
                out_ref[slot, phase(u * frames + i, count), :] = y
        acc = out_ref[slot]
        dv_ref[:, out] = (acc * p_ref[:, lanes].astype(F32)).astype(BF)
        dg_ref[:, out] = (acc * q_ref[:, lanes].astype(F32)).astype(BF)

    lane_groups(0, width, work)


def grad_proj(utt, start, width, seqs, kernel, p, q, after):
    rows = p.shape[0]
    out = near((rows, width), BF)
    return pl.pallas_call(
        functools.partial(grad_proj_body, utt, start),
        in_specs=[WHOLE] * 4 + [ANYWHERE] * len(after),
        out_specs=[WHOLE] * 2,
        out_shape=[out, out],
        scratch_shapes=[
            pltpu.VMEM((2, rows, LANES), F32),
            pltpu.VMEM((2, PIECES, kernel.shape[0] // PHASES, LANES), F32),
        ],
        compiler_params=params(VMEM_MIB),
        cost_estimate=cost(4),
        name="grad_proj",
    )(seqs, kernel, p, q, *after)


def back_proj_body(start, vec_ref, w_ref, *rest):
    pieces = rest[:4]
    out_ref = rest[-1]
    wide = pieces[0].shape[1]
    dims = (((1,), (1,)), ((), ()))
    for j in range(out_ref.shape[1] // CW):
        cols = slice(start + j * CW, start + (j + 1) * CW)
        part = 0.0
        for k, piece in enumerate(pieces):
            part += lax.dot_general(
                piece[...], w_ref[cols, k * wide : (k + 1) * wide], dims, preferred_element_type=F32
            )
        out_ref[:, j * CW : (j + 1) * CW] = part * vec_ref[0:1, cols]


def back_proj(start, width, vec, w_in, pieces, after):
    rows = pieces[0].shape[0]
    return pl.pallas_call(
        functools.partial(back_proj_body, start),
        in_specs=[WHOLE] * 6 + [ANYWHERE] * len(after),
        out_specs=WHOLE,
        out_shape=near((rows, width), F32),
        compiler_params=params(VMEM_MIB),
        cost_estimate=cost(2.6),
        name="back_proj",
    )(vec, w_in, *pieces, *after)


def back_norm_body(hat_ref, rstd_ref, cot_ref, left_ref, right_ref, *rest):
    out_hbm, done_ref, out_ref, sem = rest[-4:]
    done_ref[...] = jnp.zeros(done_ref.shape, F32)
    copies = []
    rows, d = hat_ref.shape
    span = rows // sem.shape[0]
    for i in range(0, rows, 16):
        at = slice(i, i + 16)
        hats = [hat_ref[at, : d // 2].astype(F32), hat_ref[at, d // 2 :].astype(F32)]
        grads = [left_ref[at, :], right_ref[at, :]]
        m1 = sum(jnp.sum(g, axis=-1, keepdims=True) for g in grads) * (1.0 / d)
        m2 = sum(jnp.sum(g * h, axis=-1, keepdims=True) for g, h in zip(grads, hats)) * (1.0 / d)
        rstd = rstd_ref[at, :]
        for k, cols in enumerate((slice(0, d // 2), slice(d // 2, d))):
            layer = rstd * (grads[k] - m1 - hats[k] * m2)
            out_ref[at, cols] = (cot_ref[at, cols].astype(F32) + layer).astype(BF)
        if (i + 16) % span == 0:
            piece = pl.ds(i + 16 - span, span)
            copies.append(
                pltpu.make_async_copy(out_ref.at[piece], out_hbm.at[piece], sem.at[i // span])
            )
            copies[-1].start()
    for copy in copies:
        copy.wait()


def back_norm(hat, rstd, cot, left, right, after):
    rows, d = hat.shape
    return pl.pallas_call(
        back_norm_body,
        in_specs=[WHOLE] * 5 + [ANYWHERE] * len(after),
        out_specs=[FAR, WHOLE],
        out_shape=[pltpu.HBM((rows, d), BF), near((8, LANES), F32)],
        scratch_shapes=[pltpu.VMEM((rows, d), BF), pltpu.SemaphoreType.DMA((8,))],
        compiler_params=params(VMEM_MIB),
        cost_estimate=cost(3),
        name="back_norm",
    )(hat, rstd, cot, left, right, *after)


def swap(block, axis, bit):
    count = lax.axis_size(axis)
    return lax.ppermute(block, axis, [(i, i ^ bit) for i in range(count)])


def is_power(count):
    return count & (count - 1) == 0


def add_body(own_ref, got_ref, *rest):
    out_ref = rest[-1]
    out_ref[...] = (own_ref[...].astype(F32) + got_ref[...].astype(F32)).astype(out_ref.dtype)


def add(own, got, dtype, after):
    return pl.pallas_call(
        add_body,
        in_specs=[WHOLE] * 2 + [ANYWHERE] * len(after),
        out_specs=WHOLE,
        out_shape=shape(own.shape, dtype),
        compiler_params=params(4),
        cost_estimate=cost(0.5),
        name="add",
    )(own, got, *after)


def last_add_body(a_ref, b_ref, c_ref, d_ref, *rest):
    one_ref, two_ref = rest[-2:]
    one_ref[...] = a_ref[...].astype(F32) + b_ref[...].astype(F32)
    two_ref[...] = c_ref[...].astype(F32) + d_ref[...].astype(F32)


def last_add(one, two, after):
    return pl.pallas_call(
        last_add_body,
        in_specs=[WHOLE] * 4 + [ANYWHERE] * len(after),
        out_specs=[WHOLE] * 2,
        out_shape=[shape(one[0].shape, F32), shape(two[0].shape, F32)],
        compiler_params=params(4),
        cost_estimate=cost(0.7),
        name="last_add",
    )(*one, *two, *after)


def all_sum(block, axis, fill=(), order=None, whole=True):
    count = lax.axis_size(axis)
    if not is_power(count):
        for work in fill:
            work([])
        return lax.psum(block.astype(F32), axis)
    bits = [1 << i for i in range(count.bit_length() - 1)]
    if order is not None:
        bits = order(bits)
    for step, bit in enumerate(bits):
        other = swap(block, axis, bit)
        after = fill[step]([block]) if step < len(fill) else []
        if bit == bits[-1] and not whole:
            return (block, other), after
        block = add(block, other, F32 if bit == bits[-1] else block.dtype, after)
    return block


def nothing(_):
    return []


def beside(a, b, axis):
    count = lax.axis_size(axis)
    pairs = []
    for low in range(1, count - 1, 2):
        pairs += [(low, low + 1), (low + 1, low)]
    return swap(a, axis, 1), lax.ppermute(b, axis, pairs)


def merge_body(sides, after, *refs):
    keep_out, send_out = refs[2 * sides + after :]
    blocks = refs[0].shape[0]
    wide = refs[0].shape[2]
    for side in range(sides):
        keep_ref, got_ref = refs[2 * side : 2 * side + 2]
        cols = slice(side * wide, (side + 1) * wide)
        for j in range(blocks):
            total = keep_ref[j] + got_ref[j].astype(F32)
            if j % 2:
                send_out[j // 2, :, cols] = total.astype(BF)
            else:
                keep_out[j // 2, :, cols] = total


def merge(pairs, after):
    blocks, per, wide = pairs[0][0].shape
    dims = (blocks // 2, per, wide * len(pairs))
    return pl.pallas_call(
        functools.partial(merge_body, len(pairs), len(after)),
        in_specs=[WHOLE] * (2 * len(pairs)) + [ANYWHERE] * len(after),
        out_specs=[WHOLE] * 2,
        out_shape=[shape(dims, F32), shape(dims, BF)],
        compiler_params=params(8),
        cost_estimate=cost(1),
        name="merge",
    )(*[a for pair in pairs for a in pair], *after)


def first_swaps(parts, axis, after):
    return [
        merge([(keep, swap(send, axis, device_bit))], after)
        for (keep, send), device_bit in zip(parts, (2, 4))
    ]


def last_swaps(held, axis, after):
    count = lax.axis_size(axis)
    after = list(after)
    pairs = [
        (keep, swap(send, axis, device_bit)) for (keep, send), device_bit in zip(held, (4, 2))
    ]
    bit = 8
    if bit == count:
        both = [jnp.concatenate(side, axis=-1)[0] for side in zip(*pairs)]
        return both[0], both[1]
    while True:
        keep, send = merge(pairs, after.pop(0) if after else [])
        got = swap(send, axis, bit)
        bit *= 2
        if bit == count:
            return keep[0], got[0]
        pairs = [(keep, got)]


def on_device(inputs, ln_gain, w_in, kernel, bn_gain, bn_bias, w_out, cotangent):
    axis = AXIS
    n = lax.axis_size(axis)
    me = lax.axis_index(axis).astype(jnp.int32)
    utt, frames, d = inputs.shape
    rows = utt * frames
    half = d // 2
    total = rows * n
    x = inputs.reshape(rows, d)
    cot = cotangent.reshape(rows, d)
    by_owner = is_power(n) and n >= 8 and d % n == 0 and (d // n) % 16 == 0

    gated, p, q, hat, rstd, vec, ga, gb = front(utt, x, ln_gain, bn_gain, bn_bias, w_in, cot)
    ga, gb = beside(ga, gb, axis)
    conv_some, sums_some = conv_mid(utt, gated, kernel)
    conv_out, sums = conv_end(utt, gated, ga, gb, kernel, conv_some, sums_some, [])
    made = {}
    half = d // 2

    def act_grading(start):
        def work(after):
            made["d_act", start] = act_grad(start, half, cot, w_out, after)
            return [made["d_act", start]]

        return work

    def ending(after):
        made["d_act_end"] = act_grad_end(ga, gb, w_out, after)
        if not by_owner:
            return [made["d_act_end"]]
        made["cot"], other = turn(n, cot, after)
        made["cot_beside"] = swap(other, axis, 1)
        return [made["d_act_end"], made["cot"]]

    sums = all_sum(sums, axis, [nothing, act_grading(0), act_grading(half), nothing, ending])
    act, dbn, dsums = middle(
        utt, total, conv_out, sums, vec, made["d_act", 0], made["d_act", half], made["d_act_end"], []
    )

    def branching(start):
        def work(after):
            some = [made["outputs"]] if start else []
            made["outputs"], done = branch(start, half, x, act, w_out, some, after)
            return [done]

        return work

    def grading(after):
        if not by_owner:
            return []
        act_b = swap(act, axis, 1)
        made["grad"] = grad((1, 2), made["cot"], made["cot_beside"], act, act_b, after)
        return [made["grad"][0]]

    dsums = all_sum(
        dsums, axis, [branching(0), branching(half), grading], lambda bits: bits[1:] + bits[:1]
    )
    if by_owner:
        send_l, keep_l, send_r, keep_r = made["grad"]
        held = first_swaps([(keep_l, send_l), (keep_r, send_r)], axis, [dsums])
    else:
        dw = lax.dot_general(cot, act, (((0,), (0,)), ((), ())), preferred_element_type=F32)
        d_w_out = lax.psum_scatter(dw, axis, scatter_dimension=0, tiled=True)

    d_kernel, d_conv, d_bn_bias, d_bn_gain = grad_taps(
        utt, total, kernel.shape[0], dbn, conv_out, sums, dsums, vec, gated
    )

    def projecting(after):
        for start in (0, half):
            made[start] = grad_proj(utt, start, half, d_conv, kernel, p, q, after)
        return [made[0][0], made[half][0]]

    def back_projecting(start):
        def work(after):
            left, right = made[0], made[half]
            pieces = (left[0], right[0], left[1], right[1])
            made["far"] = after
            made["grads", start] = back_proj(start, half, vec, w_in, pieces, after)
            return [made["grads", start]]

        return work

    def norming(after):
        made["d_inputs"], done = back_norm(
            hat, rstd, cot, made["grads", 0], made["grads", half], after
        )
        return [done]

    terms = all_sum(
        d_kernel,
        axis,
        [nothing, projecting, back_projecting(0), back_projecting(half), norming],
        lambda bits: bits[:1] + bits[:2:-1] + bits[1:3],
        whole=not by_owner,
    )
    if by_owner:
        terms, after = terms
        own = last_swaps(held, axis, [made["far"], [made["grads", half]]])
        d_w_out, d_kernel_sum = last_add(own, terms, after)
    else:
        d_kernel_sum = terms
    return (
        made["outputs"].reshape(inputs.shape), made["d_inputs"].reshape(inputs.shape), d_w_out,
        d_kernel_sum, d_bn_gain, d_bn_bias,
    )


def solution(mesh):
    return jax.shard_map(
        on_device,
        mesh=mesh,
        in_specs=(P(None, "seq", None), P(), P(), P(), P(), P(), P(), P(None, "seq", None)),
        out_specs=(P(None, "seq", None), P(None, "seq", None), P("seq", None), P(), P(), P()),
        check_vma=False,
    )
```

```python
import functools

import jax
import jax.numpy as jnp
from jax import lax
from jax.experimental import pallas as pl
from jax.experimental.pallas import tpu as pltpu
from jax.sharding import PartitionSpec as P

EPSILON = 1e-05
BF = jnp.bfloat16
F32 = jnp.float32
LANES = 128
PAD = 16
HALO = 2 * PAD
MIB = 1 << 20
AXIS = "seq"
VMEM_MIB = 8


def params(mib):
    return pltpu.CompilerParams(vmem_limit_bytes=mib * MIB)


WHOLE = pl.BlockSpec(memory_space=pltpu.VMEM)
ANYWHERE = pl.BlockSpec(memory_space=pl.ANY)
FAR = pl.BlockSpec(memory_space=pltpu.HBM)
CW = 256


def cost(micros):
    return pl.CostEstimate(flops=0, bytes_accessed=int(micros * 3.0e6), transcendentals=0)


def shape(dims, dtype):
    return jax.ShapeDtypeStruct(dims, dtype)


def place():
    me = lax.axis_index(AXIS)
    last = lax.axis_size(AXIS) - 1
    return me % 2, me // 2, (me > 0).astype(F32), (me < last).astype(F32)


def far(array):
    return pltpu.with_memory_space_constraint(array, pltpu.HBM)


def near(dims, dtype):
    return pltpu.VMEM(dims, dtype)


def turn_body(cot_ref, *rest):
    mine_ref, other_ref, held_ref = rest[-3:]
    blocks = mine_ref.shape[0]
    per = mine_ref.shape[1]
    held_ref[...] = cot_ref[...].T
    core, half, _, _ = place()

    def step(j, _):
        row = pl.multiple_of(lax.bitwise_xor(half, j) * (2 * per), 2 * per)
        mine_ref[j] = held_ref[pl.ds(pl.multiple_of(row + core * per, per), per), :]
        other_ref[j] = held_ref[pl.ds(pl.multiple_of(row + (1 - core) * per, per), per), :]
        return 0

    lax.fori_loop(0, blocks, step, 0, unroll=2)


def turn(n, cot, after):
    rows, d = cot.shape
    out = shape((n // 2, d // n, rows), BF)
    return pl.pallas_call(
        turn_body,
        in_specs=[WHOLE] + [ANYWHERE] * len(after),
        out_specs=[WHOLE] * 2,
        out_shape=[out] * 2,
        scratch_shapes=[pltpu.VMEM((d, rows), BF)],
        compiler_params=params(VMEM_MIB),
        cost_estimate=cost(2),
        name="turn",
    )(cot, *after)


def edges_out(odd, first, last, a_ref, b_ref):
    @pl.when(odd == 0)
    def _():
        a_ref[...] = last
        b_ref[...] = first

    @pl.when(odd != 0)
    def _():
        a_ref[...] = first
        b_ref[...] = last


def front_body(
    utt, x_hbm, ln_hbm, gain_hbm, bias_hbm, w_hbm, cot_hbm,
    gated_ref, p_ref, q_ref, hat_ref, rstd_ref, vec_ref, a_ref, b_ref, normed_ref, x_ref, w_ref, cot_ref,
    ln_ref, gain_ref, bias_ref, x_sem, w_sem, cot_sem, row_sem,
):
    rows, d = x_ref.shape
    frames = rows // utt
    pieces = x_sem.shape[0]
    span = rows // pieces
    steps = d // CW

    def x_copy(i):
        at = pl.ds(i * span, span)
        return pltpu.make_async_copy(x_hbm.at[at], x_ref.at[at], x_sem.at[i])

    def w_copy(j, half):
        at = pl.ds(half * d + j * CW, CW)
        return pltpu.make_async_copy(w_hbm.at[:, at], w_ref.at[:, at], w_sem.at[j, half])

    row_copies = [
        pltpu.make_async_copy(source, target, row_sem.at[i])
        for i, (source, target) in enumerate(
            ((ln_hbm, ln_ref), (gain_hbm, gain_ref), (bias_hbm, bias_ref))
        )
    ]
    for copy in row_copies:
        copy.start()
    for i in range(pieces):
        x_copy(i).start()
    for half in range(2):
        w_copy(0, half).start()
    cots = []
    for u in range(utt):
        for side, at in enumerate((u * frames, (u + 1) * frames - PAD)):
            cots.append(
                pltpu.make_async_copy(
                    cot_hbm.at[pl.ds(at, PAD)], cot_ref.at[u, side], cot_sem.at[u, side]
                )
            )
            cots[-1].start()
    for copy in row_copies:
        copy.wait()
    for i, row_ref in enumerate((ln_ref, gain_ref, bias_ref)):
        vec_ref[i : i + 1, :] = row_ref[...].reshape(1, d)

    for i in range(pieces):
        x_copy(i).wait()
        for j in range(1 + 3 * i, min(steps, 4 + 3 * i)):
            for half in range(2):
                w_copy(j, half).start()

        for k in range(i * span, (i + 1) * span, 16):
            at = slice(k, k + 16)
            x = x_ref[at, :].astype(F32)
            mu = jnp.sum(x, axis=-1, keepdims=True) * (1.0 / d)
            c = x - mu
            var = jnp.sum(c * c, axis=-1, keepdims=True) * (1.0 / d)
            rstd = lax.rsqrt(var + EPSILON)
            hat = c * rstd
            rstd_ref[at, :] = rstd
            hat_ref[at, :] = hat.astype(BF)
            normed_ref[at, :] = (hat * vec_ref[0:1, :]).astype(BF)

    odd = place()[0] != 0
    for j in range(steps):
        cols = slice(j * CW, (j + 1) * CW)
        for half in range(2):
            w_copy(j, half).wait()
        value = jnp.dot(normed_ref[...], w_ref[:, cols], preferred_element_type=F32)
        gate = jnp.dot(
            normed_ref[...], w_ref[:, d + j * CW : d + (j + 1) * CW], preferred_element_type=F32
        )
        sig = jax.nn.sigmoid(gate)
        gated = value * sig
        held = gated.astype(BF)
        gated_ref[:, cols] = held
        p_ref[:, cols] = sig.astype(BF)
        q_ref[:, cols] = (gated * (1.0 - sig)).astype(BF)
        shaped = held.reshape(utt, frames, CW)
        first, last = shaped[:, :HALO], shaped[:, frames - HALO :]
        a_ref[:, :HALO, cols] = jnp.where(odd, first, last)
        b_ref[:, :HALO, cols] = jnp.where(odd, last, first)
    for copy in cots:
        copy.wait()
    first, last = cot_ref[:, 0], cot_ref[:, 1]
    a_ref[:, HALO:, :] = jnp.where(odd, first, last)
    b_ref[:, HALO:, :] = jnp.where(odd, last, first)


def front(utt, x, ln_gain, bn_gain, bn_bias, w_in, cot):
    rows, d = x.shape
    out = near((rows, d), BF)
    edge = shape((utt, HALO + PAD, d), BF)
    return pl.pallas_call(
        functools.partial(front_body, utt),
        in_specs=[FAR] * 6,
        out_specs=[WHOLE] * 8,
        out_shape=[out] * 4 + [near((rows, 1), F32), near((3, d), F32)] + [edge] * 2,
        scratch_shapes=[
            pltpu.VMEM((rows, d), BF),
            pltpu.VMEM((rows, d), BF),
            pltpu.VMEM((d, 2 * d), BF),
            pltpu.VMEM((utt, 2, PAD, d), BF),
            pltpu.VMEM((d,), F32),
            pltpu.VMEM((d,), F32),
            pltpu.VMEM((d,), F32),
            pltpu.SemaphoreType.DMA((2,)),
            pltpu.SemaphoreType.DMA((d // CW, 2)),
            pltpu.SemaphoreType.DMA((utt, 2)),
            pltpu.SemaphoreType.DMA((3,)),
        ],
        compiler_params=params(24),
        cost_estimate=cost(10),
        name="front",
    )(*[far(a) for a in (x, ln_gain, bn_gain, bn_bias, w_in, cot)])


def lane_groups(first, last, work):
    def step(i, _):
        for slot in range(2):
            group = 2 * i + slot
            work(group, pl.ds(pl.multiple_of(group * LANES, LANES), LANES), slot)
        return 0

    lax.fori_loop(first // (2 * LANES), last // (2 * LANES), step, 0)


PHASES = 4
PIECES = 9


def thirds(x0, x1, x2):
    return [x1, x0 - x1, x2 - x1]


def sequences(x):
    tops = [
        (x[1], x[3], x[5]),
        (x[0] - x[1], x[2] - x[3], x[4] - x[5]),
        (x[2] - x[1], x[4] - x[3], x[6] - x[5]),
    ]
    return [piece for top in tops for piece in thirds(*top)]


def combined(h):
    tops = [(h[0] + h[1], h[2] + h[3]), (h[0], h[2]), (h[1], h[3])]
    return [piece for a, b in tops for piece in (a + b, a, b)]


def assembled(products):
    halves = []
    for top in range(3):
        m, p, q = (next(products) for _ in range(3))
        halves.append((m + p, m + q))
        if top:
            for j in range(2):
                yield 2 * j + top - 1, halves[0][j] + halves[top][j]


def phase(first, size):
    return pl.ds(first, size, PHASES)


def fill_sequences(pad_ref, shift, seq_ref, size):
    x = [pad_ref[phase(j + shift, size), :] for j in range(2 * PHASES - 1)]
    for i, piece in enumerate(sequences(x)):
        seq_ref[i] = piece


def filtered(seq_refs, taps_ref, order, count):
    for i in range(PIECES):
        acc = jnp.zeros((count * len(seq_refs), LANES), F32)
        for a in range(taps_ref.shape[1]):
            row = order(a)
            rows = [seq_ref[i, a : a + count, :] for seq_ref in seq_refs]
            acc = acc + taps_ref[i, row : row + 1, :] * jnp.concatenate(rows, axis=0)
        yield acc


def tap_factors(k_ref, lanes, held_ref, taps_ref):
    per = k_ref.shape[0] // PHASES
    held_ref[0 : per * PHASES, :] = k_ref[:, lanes]
    for i, piece in enumerate(combined([held_ref[phase(i, per), :] for i in range(PHASES)])):
        taps_ref[i] = piece


def conv_pieces(pad_refs, seq_refs, taps_ref, count):
    for pad_ref, seq_ref in zip(pad_refs, seq_refs):
        fill_sequences(pad_ref, 1, seq_ref, count + taps_ref.shape[1])
    for i, y in assembled(filtered(seq_refs, taps_ref, lambda a: a, count)):
        for j, pad_ref in enumerate(pad_refs):
            pad_ref[phase(i, count), :] = y[j * count : (j + 1) * count]


def squares(values):
    values = values.reshape(values.shape[0] // 8, 8, LANES)
    return jnp.sum(values, axis=0), jnp.sum(values * values, axis=0)


def conv_mid_body(utt, g_ref, k_ref, conv_ref, sums_ref, pad_ref, seq_ref, taps_ref):
    d = g_ref.shape[1]
    frames = g_ref.shape[0] // utt
    mid = frames - HALO

    def work(_, lanes, slot):
        first = square = jnp.zeros((8, LANES), F32)
        tap_factors(k_ref, lanes, pad_ref.at[slot, 0], taps_ref.at[slot])
        for u in range(utt):
            pad = pad_ref.at[slot, u]
            pad[0:frames, :] = g_ref[u * frames : (u + 1) * frames, lanes].astype(F32)
            conv_pieces([pad], [seq_ref.at[slot, u]], taps_ref.at[slot], mid // PHASES)
            y = pad[0:mid, :]
            start = u * (frames + HALO) + HALO
            conv_ref[start : start + mid, lanes] = y
            one, two = squares(y)
            first, square = first + one, square + two
        sums_ref[0:1, lanes] = jnp.sum(first, axis=0, keepdims=True)
        sums_ref[1:2, lanes] = jnp.sum(square, axis=0, keepdims=True)

    lane_groups(0, d, work)


def conv_scratch(utt, pieces, frames, count, per):
    return [
        pltpu.VMEM((2, utt * pieces, frames + 8, LANES), F32),
        pltpu.VMEM((2, utt * pieces, PIECES, count + per, LANES), F32),
        pltpu.VMEM((2, PIECES, per, LANES), F32),
    ]


def conv_mid(utt, gated, kernel):
    rows, d = gated.shape
    frames = rows // utt
    per = kernel.shape[0] // PHASES
    return pl.pallas_call(
        functools.partial(conv_mid_body, utt),
        in_specs=[WHOLE] * 2,
        out_specs=[WHOLE] * 2,
        out_shape=[near((utt * (frames + HALO), d), F32), near((2, d), F32)],
        scratch_shapes=conv_scratch(utt, 1, frames, (frames - HALO) // PHASES, per),
        compiler_params=params(VMEM_MIB),
        cost_estimate=cost(5),
        name="conv_mid",
    )(gated, kernel)


def conv_end_body(utt, g_ref, a_ref, b_ref, k_ref, _, some_ref, *rest):
    conv_ref, sums_ref, pad_ref, seq_ref, taps_ref = rest[-5:]
    d = g_ref.shape[1]
    frames = g_ref.shape[0] // utt
    odd = place()[0] != 0

    def work(_, lanes, slot):
        first = square = jnp.zeros((8, LANES), F32)
        tap_factors(k_ref, lanes, pad_ref.at[slot, 0], taps_ref.at[slot])
        for u in range(utt):
            a = a_ref[u, :HALO, lanes].astype(F32)
            b = b_ref[u, :HALO, lanes].astype(F32)
            for side in range(2):
                pad = pad_ref.at[slot, 2 * u + side]
                at = u * frames + side * (frames - HALO)
                here = g_ref[at : at + HALO, lanes].astype(F32)
                beside = jnp.where(odd, b, a) if side else jnp.where(odd, a, b)
                pad[side * HALO : (side + 1) * HALO, :] = beside
                pad[(1 - side) * HALO : (2 - side) * HALO, :] = here
        conv_pieces(
            [pad_ref.at[slot, j] for j in range(2 * utt)],
            [seq_ref.at[slot, j] for j in range(2 * utt)],
            taps_ref.at[slot],
            HALO // PHASES,
        )
        for u in range(utt):
            for side in range(2):
                pad = pad_ref.at[slot, 2 * u + side]
                out = u * (frames + HALO) + side * frames
                conv_ref[out : out + HALO, lanes] = pad[0:HALO, :]
                own = (1 - side) * PAD
                one, two = squares(pad[own : own + PAD, :])
                first, square = first + one, square + two
        sums_ref[0:1, lanes] = some_ref[0:1, lanes] + jnp.sum(first, axis=0, keepdims=True)
        sums_ref[1:2, lanes] = some_ref[1:2, lanes] + jnp.sum(square, axis=0, keepdims=True)

    lane_groups(0, d, work)


def conv_end(utt, gated, a, b, kernel, conv_some, sums_some, after):
    rows, d = gated.shape
    per = kernel.shape[0] // PHASES
    return pl.pallas_call(
        functools.partial(conv_end_body, utt),
        in_specs=[WHOLE] * 6 + [ANYWHERE] * len(after),
        out_specs=[WHOLE] * 2,
        out_shape=[near(conv_some.shape, F32), shape((2, d), F32)],
        scratch_shapes=conv_scratch(utt, 2, 2 * HALO, HALO // PHASES, per),
        input_output_aliases={4: 0},
        compiler_params=params(VMEM_MIB),
        cost_estimate=cost(2),
        name="conv_end",
    )(gated, a, b, kernel, conv_some, sums_some, *after)


def act_grad_body(start, cot_ref, w_ref, *rest):
    out_ref = rest[-1]
    for j in range(out_ref.shape[1] // CW):
        cols = slice(j * CW, (j + 1) * CW)
        source = slice(start + j * CW, start + (j + 1) * CW)
        out_ref[:, cols] = jnp.dot(cot_ref[...], w_ref[:, source], preferred_element_type=F32)


def act_grad(start, width, cot, w_out, after):
    return pl.pallas_call(
        functools.partial(act_grad_body, start),
        in_specs=[WHOLE] * 2 + [ANYWHERE] * len(after),
        out_specs=WHOLE,
        out_shape=near((cot.shape[0], width), F32),
        compiler_params=params(VMEM_MIB),
        cost_estimate=cost(1.5),
        name="act_grad",
    )(cot, w_out, *after)


def act_grad_end_body(a_ref, b_ref, w_ref, *rest):
    out_ref = rest[-1]
    utt = a_ref.shape[0]
    odd = place()[0] != 0
    pieces = []
    for u in range(utt):
        a, b = a_ref[u, HALO:, :], b_ref[u, HALO:, :]
        pieces += [jnp.where(odd, a, b), jnp.where(odd, b, a)]
    cot = jnp.concatenate(pieces, axis=0)
    out_ref[...] = jnp.dot(cot, w_ref[...], preferred_element_type=F32)


def act_grad_end(a, b, w_out, after):
    utt, _, d = a.shape
    return pl.pallas_call(
        act_grad_end_body,
        in_specs=[WHOLE] * 3 + [ANYWHERE] * len(after),
        out_specs=WHOLE,
        out_shape=near((utt * HALO, d), F32),
        compiler_params=params(VMEM_MIB),
        cost_estimate=cost(2),
        name="act_grad_end",
    )(a, b, w_out, *after)


def middle_body(utt, total, conv_ref, sums_ref, vec_ref, left_ref, right_ref, end_ref, *rest):
    act_ref, dbn_ref, dsums_ref = rest[-3:]
    d = conv_ref.shape[1]
    frames = left_ref.shape[0] // utt
    per_half = left_ref.shape[1] // CW
    for j in range(d // CW):
        cols = slice(j * CW, (j + 1) * CW)
        own_ref = (left_ref, right_ref)[j // per_half]
        own_cols = slice(j % per_half * CW, (j % per_half + 1) * CW)
        mean = sums_ref[0:1, cols] * (1.0 / total)
        var = sums_ref[1:2, cols] * (1.0 / total) - mean * mean
        rstd = lax.rsqrt(var + EPSILON)

        def back(at, d_act):
            xhat = (conv_ref[at, cols] - mean) * rstd
            out = xhat * vec_ref[1:2, cols] + vec_ref[2:3, cols]
            sig = jax.nn.sigmoid(out)
            act = out * sig
            dbn = d_act * (sig + act * (1.0 - sig))
            dbn_ref[at, cols] = dbn
            return xhat, act, dbn

        bias = gain = 0.0
        for u in range(utt):
            start = u * (frames + HALO)
            back(slice(start, start + PAD), end_ref[u * HALO : u * HALO + PAD, cols])
            rows = slice(u * frames, (u + 1) * frames)
            xhat, act, dbn = back(slice(start + PAD, start + PAD + frames), own_ref[rows, own_cols])
            act_ref[rows, cols] = act.astype(BF)
            bias += jnp.sum(dbn, axis=0, keepdims=True)
            gain += jnp.sum(dbn * xhat, axis=0, keepdims=True)
            back(
                slice(start + PAD + frames, start + HALO + frames),
                end_ref[u * HALO + PAD : (u + 1) * HALO, cols],
            )
        dsums_ref[0:1, cols] = bias
        dsums_ref[1:2, cols] = gain


def middle(utt, total, conv_out, sums, vec, left, right, end, after):
    rows = left.shape[0]
    d = conv_out.shape[1]
    return pl.pallas_call(
        functools.partial(middle_body, utt, total),
        in_specs=[WHOLE] * 6 + [ANYWHERE] * len(after),
        out_specs=[WHOLE] * 3,
        out_shape=[shape((rows, d), BF), near(conv_out.shape, F32), shape((2, d), F32)],
        compiler_params=params(VMEM_MIB),
        cost_estimate=cost(3),
        name="middle",
    )(conv_out, sums, vec, left, right, end, *after)


def grad_body(bits, ca_ref, cb_ref, acta_ref, actb_ref, *rest):
    out_refs = rest[-4:]
    blocks, per, rows = ca_ref.shape
    half = out_refs[0].shape[-1]
    ca = ca_ref[...].reshape(blocks * per, rows)
    cb = cb_ref[...].reshape(blocks * per, rows)
    for side, bit in enumerate(bits):
        send_ref, keep_ref = out_refs[2 * side], out_refs[2 * side + 1]
        for c in range(half // CW):
            cols = slice(c * CW, (c + 1) * CW)
            src = slice(side * half + c * CW, side * half + (c + 1) * CW)
            dw = jnp.dot(ca, acta_ref[:, src], preferred_element_type=F32)
            dw += jnp.dot(cb, actb_ref[:, src], preferred_element_type=F32)
            sent = kept = 0
            for j in range(blocks):
                block = dw[j * per : (j + 1) * per]
                if j & bit:
                    send_ref[sent, :, cols] = block.astype(BF)
                    sent += 1
                else:
                    keep_ref[kept, :, cols] = block
                    kept += 1


def grad(bits, cot_a, cot_b, act_a, act_b, after):
    blocks, per, _ = cot_a.shape
    d = act_a.shape[1]
    half = (blocks // 2, per, d // 2)
    return pl.pallas_call(
        functools.partial(grad_body, bits),
        in_specs=[WHOLE] * 4 + [ANYWHERE] * len(after),
        out_specs=[WHOLE] * 4,
        out_shape=[shape(half, BF), shape(half, F32)] * 2,
        compiler_params=params(VMEM_MIB),
        cost_estimate=cost(3.5),
        name="grad",
    )(cot_a, cot_b, act_a, act_b, *after)


def branch_body(start, x_ref, act_ref, w_ref, *rest):
    out_hbm, done_ref, out_ref, sem = rest[-4:]
    done_ref[...] = jnp.zeros(done_ref.shape, F32)
    copies = []
    for j in range(sem.shape[0]):
        cols = slice(start + j * CW, start + (j + 1) * CW)
        here = slice(j * CW, (j + 1) * CW)
        part = lax.dot_general(
            act_ref[...], w_ref[cols, :], (((1,), (1,)), ((), ())), preferred_element_type=F32
        )
        out_ref[:, here] = (x_ref[:, cols].astype(F32) + part).astype(BF)
        copies.append(pltpu.make_async_copy(out_ref.at[:, here], out_hbm.at[:, cols], sem.at[j]))
        copies[-1].start()
    for copy in copies:
        copy.wait()


def branch(start, width, x, act, w_out, some, after):
    rows, d = x.shape
    return pl.pallas_call(
        functools.partial(branch_body, start),
        in_specs=[WHOLE] * 3 + [FAR] * len(some) + [ANYWHERE] * len(after),
        out_specs=[FAR, WHOLE],
        out_shape=[pltpu.HBM((rows, d), BF), near((8, LANES), F32)],
        scratch_shapes=[pltpu.VMEM((rows, width), BF), pltpu.SemaphoreType.DMA((width // CW,))],
        input_output_aliases={3: 0} if some else {},
        compiler_params=params(VMEM_MIB),
        cost_estimate=cost(2),
        name="branch",
    )(x, act, w_out, *some, *after)


def grad_taps_body(
    utt, total, dbn_ref, conv_ref, sums_ref, dsums_ref, vec_ref, g_ref,
    dk_ref, seq_ref, bias_ref, gain_ref, pad_ref, held_ref, acc_ref,
):
    d = g_ref.shape[1]
    frames = g_ref.shape[0] // utt
    count = frames // PHASES
    taps = dk_ref.shape[0]
    per = taps // PHASES
    _, _, keep_lo, keep_hi = place()
    bias_ref[...] = dsums_ref[0:1, :].reshape(d)
    gain_ref[...] = dsums_ref[1:2, :].reshape(d)

    def work(group, lanes, slot):
        mean = sums_ref[0:1, lanes] * (1.0 / total)
        var = sums_ref[1:2, lanes] * (1.0 / total) - mean * mean
        rstd = lax.rsqrt(var + EPSILON)
        scale = rstd * vec_ref[1:2, lanes]
        cross = scale * rstd * (dsums_ref[1:2, lanes] * (1.0 / total))
        mean_grad = scale * (dsums_ref[0:1, lanes] * (1.0 / total))

        def d_conv(at):
            return dbn_ref[at, lanes] * scale - mean_grad - (conv_ref[at, lanes] - mean) * cross

        for u in range(utt):
            start = u * (frames + HALO)
            end = start + PAD + frames
            rows = slice(u * frames, (u + 1) * frames)
            pad = pad_ref.at[slot, u]
            pad[0:PAD, :] = d_conv(slice(start, start + PAD)) * keep_lo
            pad[PAD : PAD + frames, :] = d_conv(slice(start + PAD, end))
            pad[PAD + frames : HALO + frames, :] = d_conv(slice(end, end + PAD)) * keep_hi
            fill_sequences(pad_ref.at[slot, u], 0, seq_ref.at[group, u], count + per)
            pad_ref[slot, u, 0:frames, :] = g_ref[rows, lanes].astype(F32)
            g = [pad_ref[slot, u, phase(i, count), :] for i in range(PHASES)]
            for i, piece in enumerate(combined(g)):
                held_ref[slot, u, i] = piece

        def products():
            for i in range(PIECES):
                sums = [jnp.zeros((8, LANES), F32)] * per
                for u in range(utt):
                    for base in range(0, count, 32):
                        g = held_ref[slot, u, i, base : base + 32, :]
                        for a in range(per):
                            prod = g * seq_ref[group, u, i, base + a : base + a + 32, :]
                            sums[a] = sums[a] + jnp.sum(prod.reshape(4, 8, LANES), axis=0)
                yield jnp.stack(sums)

        for i, y in assembled(products()):
            for a in range(per):
                acc_ref[slot, taps - 1 - (PHASES * a + i)] = y[a]
        dk_ref[:, lanes] = jnp.sum(acc_ref[slot], axis=1).astype(BF)

    lane_groups(0, d, work)


def grad_taps(utt, total, taps, dbn, conv_out, sums, dsums, vec, gated):
    rows, d = gated.shape
    frames = rows // utt
    long = frames // PHASES + taps // PHASES
    return pl.pallas_call(
        functools.partial(grad_taps_body, utt, total),
        in_specs=[WHOLE] * 6,
        out_specs=[WHOLE] * 4,
        out_shape=[
            shape((taps, d), BF),
            near((d // LANES, utt, PIECES, long, LANES), F32),
            shape((d,), F32),
            shape((d,), F32),
        ],
        scratch_shapes=[
            pltpu.VMEM((2, utt, frames + 2 * PAD + 8, LANES), F32),
            pltpu.VMEM((2, utt, PIECES, frames // PHASES, LANES), F32),
            pltpu.VMEM((2, taps, 8, LANES), F32),
        ],
        compiler_params=params(VMEM_MIB),
        cost_estimate=cost(9),
        name="grad_taps",
    )(dbn, conv_out, sums, dsums, vec, gated)


def grad_proj_body(utt, start, seq_ref, k_ref, p_ref, q_ref, *rest):
    dv_ref, dg_ref, out_ref, taps_ref = rest[-4:]
    rows, width = dv_ref.shape
    frames = rows // utt
    count = frames // PHASES
    per = k_ref.shape[0] // PHASES

    def work(group, out, slot):
        lanes = pl.ds(pl.multiple_of(out.start + start, LANES), LANES)
        out_ref[slot, 0 : per * PHASES, :] = k_ref[:, lanes]
        k = [out_ref[slot, phase(PHASES - 1 - i, per), :] for i in range(PHASES)]
        for i, piece in enumerate(combined(k)):
            taps_ref[slot, i] = piece
        for u in range(utt):
            products = filtered(
                [seq_ref.at[group + start // LANES, u]],
                taps_ref.at[slot],
                lambda a: per - 1 - a,
                count,
            )
            for i, y in assembled(products):
                out_ref[slot, phase(u * frames + i, count), :] = y
        acc = out_ref[slot]
        dv_ref[:, out] = (acc * p_ref[:, lanes].astype(F32)).astype(BF)
        dg_ref[:, out] = (acc * q_ref[:, lanes].astype(F32)).astype(BF)

    lane_groups(0, width, work)


def grad_proj(utt, start, width, seqs, kernel, p, q, after):
    rows = p.shape[0]
    out = near((rows, width), BF)
    return pl.pallas_call(
        functools.partial(grad_proj_body, utt, start),
        in_specs=[WHOLE] * 4 + [ANYWHERE] * len(after),
        out_specs=[WHOLE] * 2,
        out_shape=[out, out],
        scratch_shapes=[
            pltpu.VMEM((2, rows, LANES), F32),
            pltpu.VMEM((2, PIECES, kernel.shape[0] // PHASES, LANES), F32),
        ],
        compiler_params=params(VMEM_MIB),
        cost_estimate=cost(4),
        name="grad_proj",
    )(seqs, kernel, p, q, *after)


def back_proj_body(start, vec_ref, w_ref, *rest):
    pieces = rest[:4]
    out_ref = rest[-1]
    wide = pieces[0].shape[1]
    dims = (((1,), (1,)), ((), ()))
    for j in range(out_ref.shape[1] // CW):
        cols = slice(start + j * CW, start + (j + 1) * CW)
        part = 0.0
        for k, piece in enumerate(pieces):
            part += lax.dot_general(
                piece[...], w_ref[cols, k * wide : (k + 1) * wide], dims, preferred_element_type=F32
            )
        out_ref[:, j * CW : (j + 1) * CW] = part * vec_ref[0:1, cols]


def back_proj(start, width, vec, w_in, pieces, after):
    rows = pieces[0].shape[0]
    return pl.pallas_call(
        functools.partial(back_proj_body, start),
        in_specs=[WHOLE] * 6 + [ANYWHERE] * len(after),
        out_specs=WHOLE,
        out_shape=near((rows, width), F32),
        compiler_params=params(VMEM_MIB),
        cost_estimate=cost(2.6),
        name="back_proj",
    )(vec, w_in, *pieces, *after)


def back_norm_body(hat_ref, rstd_ref, cot_ref, left_ref, right_ref, *rest):
    out_hbm, done_ref, out_ref, sem = rest[-4:]
    done_ref[...] = jnp.zeros(done_ref.shape, F32)
    copies = []
    rows, d = hat_ref.shape
    span = rows // sem.shape[0]
    for i in range(0, rows, 16):
        at = slice(i, i + 16)
        hats = [hat_ref[at, : d // 2].astype(F32), hat_ref[at, d // 2 :].astype(F32)]
        grads = [left_ref[at, :], right_ref[at, :]]
        m1 = sum(jnp.sum(g, axis=-1, keepdims=True) for g in grads) * (1.0 / d)
        m2 = sum(jnp.sum(g * h, axis=-1, keepdims=True) for g, h in zip(grads, hats)) * (1.0 / d)
        rstd = rstd_ref[at, :]
        for k, cols in enumerate((slice(0, d // 2), slice(d // 2, d))):
            layer = rstd * (grads[k] - m1 - hats[k] * m2)
            out_ref[at, cols] = (cot_ref[at, cols].astype(F32) + layer).astype(BF)
        if (i + 16) % span == 0:
            piece = pl.ds(i + 16 - span, span)
            copies.append(
                pltpu.make_async_copy(out_ref.at[piece], out_hbm.at[piece], sem.at[i // span])
            )
            copies[-1].start()
    for copy in copies:
        copy.wait()


def back_norm(hat, rstd, cot, left, right, after):
    rows, d = hat.shape
    return pl.pallas_call(
        back_norm_body,
        in_specs=[WHOLE] * 5 + [ANYWHERE] * len(after),
        out_specs=[FAR, WHOLE],
        out_shape=[pltpu.HBM((rows, d), BF), near((8, LANES), F32)],
        scratch_shapes=[pltpu.VMEM((rows, d), BF), pltpu.SemaphoreType.DMA((8,))],
        compiler_params=params(VMEM_MIB),
        cost_estimate=cost(3),
        name="back_norm",
    )(hat, rstd, cot, left, right, *after)


def swap(block, axis, bit):
    count = lax.axis_size(axis)
    return lax.ppermute(block, axis, [(i, i ^ bit) for i in range(count)])


def is_power(count):
    return count & (count - 1) == 0


def add_body(own_ref, got_ref, *rest):
    out_ref = rest[-1]
    out_ref[...] = (own_ref[...].astype(F32) + got_ref[...].astype(F32)).astype(out_ref.dtype)


def add(own, got, dtype, after):
    return pl.pallas_call(
        add_body,
        in_specs=[WHOLE] * 2 + [ANYWHERE] * len(after),
        out_specs=WHOLE,
        out_shape=shape(own.shape, dtype),
        compiler_params=params(4),
        cost_estimate=cost(0.5),
        name="add",
    )(own, got, *after)


def last_add_body(a_ref, b_ref, c_ref, d_ref, *rest):
    one_ref, two_ref = rest[-2:]
    one_ref[...] = a_ref[...].astype(F32) + b_ref[...].astype(F32)
    two_ref[...] = c_ref[...].astype(F32) + d_ref[...].astype(F32)


def last_add(one, two, after):
    return pl.pallas_call(
        last_add_body,
        in_specs=[WHOLE] * 4 + [ANYWHERE] * len(after),
        out_specs=[WHOLE] * 2,
        out_shape=[shape(one[0].shape, F32), shape(two[0].shape, F32)],
        compiler_params=params(4),
        cost_estimate=cost(0.7),
        name="last_add",
    )(*one, *two, *after)


def all_sum(block, axis, fill=(), order=None, whole=True):
    count = lax.axis_size(axis)
    if not is_power(count):
        for work in fill:
            work([])
        return lax.psum(block.astype(F32), axis)
    bits = [1 << i for i in range(count.bit_length() - 1)]
    if order is not None:
        bits = order(bits)
    for step, bit in enumerate(bits):
        other = swap(block, axis, bit)
        after = fill[step]([block]) if step < len(fill) else []
        if bit == bits[-1] and not whole:
            return (block, other), after
        block = add(block, other, F32 if bit == bits[-1] else block.dtype, after)
    return block


def nothing(_):
    return []


def beside(a, b, axis):
    count = lax.axis_size(axis)
    pairs = []
    for low in range(1, count - 1, 2):
        pairs += [(low, low + 1), (low + 1, low)]
    return swap(a, axis, 1), lax.ppermute(b, axis, pairs)


def merge_body(sides, after, *refs):
    keep_out, send_out = refs[2 * sides + after :]
    blocks = refs[0].shape[0]
    wide = refs[0].shape[2]
    for side in range(sides):
        keep_ref, got_ref = refs[2 * side : 2 * side + 2]
        cols = slice(side * wide, (side + 1) * wide)
        for j in range(blocks):
            total = keep_ref[j] + got_ref[j].astype(F32)
            if j % 2:
                send_out[j // 2, :, cols] = total.astype(BF)
            else:
                keep_out[j // 2, :, cols] = total


def merge(pairs, after):
    blocks, per, wide = pairs[0][0].shape
    dims = (blocks // 2, per, wide * len(pairs))
    return pl.pallas_call(
        functools.partial(merge_body, len(pairs), len(after)),
        in_specs=[WHOLE] * (2 * len(pairs)) + [ANYWHERE] * len(after),
        out_specs=[WHOLE] * 2,
        out_shape=[shape(dims, F32), shape(dims, BF)],
        compiler_params=params(8),
        cost_estimate=cost(1),
        name="merge",
    )(*[a for pair in pairs for a in pair], *after)


def first_swaps(parts, axis, after):
    return [
        merge([(keep, swap(send, axis, device_bit))], after)
        for (keep, send), device_bit in zip(parts, (2, 4))
    ]


def last_swaps(held, axis, after):
    count = lax.axis_size(axis)
    after = list(after)
    pairs = [
        (keep, swap(send, axis, device_bit)) for (keep, send), device_bit in zip(held, (4, 2))
    ]
    bit = 8
    if bit == count:
        both = [jnp.concatenate(side, axis=-1)[0] for side in zip(*pairs)]
        return both[0], both[1]
    while True:
        keep, send = merge(pairs, after.pop(0) if after else [])
        got = swap(send, axis, bit)
        bit *= 2
        if bit == count:
            return keep[0], got[0]
        pairs = [(keep, got)]


def on_device(inputs, ln_gain, w_in, kernel, bn_gain, bn_bias, w_out, cotangent):
    axis = AXIS
    n = lax.axis_size(axis)
    me = lax.axis_index(axis).astype(jnp.int32)
    utt, frames, d = inputs.shape
    rows = utt * frames
    half = d // 2
    total = rows * n
    x = inputs.reshape(rows, d)
    cot = cotangent.reshape(rows, d)
    by_owner = is_power(n) and n >= 8 and d % n == 0 and (d // n) % 16 == 0

    gated, p, q, hat, rstd, vec, ga, gb = front(utt, x, ln_gain, bn_gain, bn_bias, w_in, cot)
    ga, gb = beside(ga, gb, axis)
    conv_some, sums_some = conv_mid(utt, gated, kernel)
    conv_out, sums = conv_end(utt, gated, ga, gb, kernel, conv_some, sums_some, [])
    made = {}
    half = d // 2

    def act_grading(start):
        def work(after):
            made["d_act", start] = act_grad(start, half, cot, w_out, after)
            return [made["d_act", start]]

        return work

    def ending(after):
        made["d_act_end"] = act_grad_end(ga, gb, w_out, after)
        if not by_owner:
            return [made["d_act_end"]]
        made["cot"], other = turn(n, cot, after)
        made["cot_beside"] = swap(other, axis, 1)
        return [made["d_act_end"], made["cot"]]

    sums = all_sum(sums, axis, [nothing, act_grading(0), act_grading(half), nothing, ending])
    act, dbn, dsums = middle(
        utt, total, conv_out, sums, vec, made["d_act", 0], made["d_act", half], made["d_act_end"], []
    )

    def branching(start):
        def work(after):
            some = [made["outputs"]] if start else []
            made["outputs"], done = branch(start, half, x, act, w_out, some, after)
            return [done]

        return work

    def grading(after):
        if not by_owner:
            return []
        act_b = swap(act, axis, 1)
        made["grad"] = grad((1, 2), made["cot"], made["cot_beside"], act, act_b, after)
        return [made["grad"][0]]

    dsums = all_sum(
        dsums, axis, [branching(0), branching(half), grading], lambda bits: bits[1:] + bits[:1]
    )
    if by_owner:
        send_l, keep_l, send_r, keep_r = made["grad"]
        held = first_swaps([(keep_l, send_l), (keep_r, send_r)], axis, [dsums])
    else:
        dw = lax.dot_general(cot, act, (((0,), (0,)), ((), ())), preferred_element_type=F32)
        d_w_out = lax.psum_scatter(dw, axis, scatter_dimension=0, tiled=True)

    d_kernel, d_conv, d_bn_bias, d_bn_gain = grad_taps(
        utt, total, kernel.shape[0], dbn, conv_out, sums, dsums, vec, gated
    )

    def projecting(after):
        for start in (0, half):
            made[start] = grad_proj(utt, start, half, d_conv, kernel, p, q, after)
        return [made[0][0], made[half][0]]

    def back_projecting(start):
        def work(after):
            left, right = made[0], made[half]
            pieces = (left[0], right[0], left[1], right[1])
            made["far"] = after
            made["grads", start] = back_proj(start, half, vec, w_in, pieces, after)
            return [made["grads", start]]

        return work

    def norming(after):
        made["d_inputs"], done = back_norm(
            hat, rstd, cot, made["grads", 0], made["grads", half], after
        )
        return [done]

    terms = all_sum(
        d_kernel,
        axis,
        [nothing, projecting, back_projecting(0), back_projecting(half), norming],
        lambda bits: bits[:1] + bits[:2:-1] + bits[1:3],
        whole=not by_owner,
    )
    if by_owner:
        terms, after = terms
        own = last_swaps(held, axis, [made["far"], [made["grads", half]]])
        d_w_out, d_kernel_sum = last_add(own, terms, after)
    else:
        d_kernel_sum = terms
    return (
        made["outputs"].reshape(inputs.shape), made["d_inputs"].reshape(inputs.shape), d_w_out,
        d_kernel_sum, d_bn_gain, d_bn_bias,
    )


def solution(mesh):
    return jax.shard_map(
        on_device,
        mesh=mesh,
        in_specs=(P(None, "seq", None), P(), P(), P(), P(), P(), P(), P(None, "seq", None)),
        out_specs=(P(None, "seq", None), P(None, "seq", None), P("seq", None), P(), P(), P()),
        check_vma=False,
    )
```

```python
import functools

import jax
import jax.numpy as jnp
from jax import lax
from jax.experimental import pallas as pl
from jax.experimental.pallas import tpu as pltpu
from jax.sharding import PartitionSpec as P

EPSILON = 1e-05
BF = jnp.bfloat16
F32 = jnp.float32
LANES = 128
PAD = 16
HALO = 2 * PAD
MIB = 1 << 20
AXIS = "seq"
VMEM_MIB = 8


def params(mib):
    return pltpu.CompilerParams(vmem_limit_bytes=mib * MIB)


WHOLE = pl.BlockSpec(memory_space=pltpu.VMEM)
ANYWHERE = pl.BlockSpec(memory_space=pl.ANY)
FAR = pl.BlockSpec(memory_space=pltpu.HBM)
CW = 256


def cost(micros):
    return pl.CostEstimate(flops=0, bytes_accessed=int(micros * 3.0e6), transcendentals=0)


def shape(dims, dtype):
    return jax.ShapeDtypeStruct(dims, dtype)


def place():
    me = lax.axis_index(AXIS)
    last = lax.axis_size(AXIS) - 1
    return me % 2, me // 2, (me > 0).astype(F32), (me < last).astype(F32)


def far(array):
    return pltpu.with_memory_space_constraint(array, pltpu.HBM)


def near(dims, dtype):
    return pltpu.VMEM(dims, dtype)


def turn_body(cot_ref, *rest):
    mine_ref, other_ref, held_ref = rest[-3:]
    blocks = mine_ref.shape[0]
    per = mine_ref.shape[1]
    held_ref[...] = cot_ref[...].T
    core, half, _, _ = place()

    def step(j, _):
        row = pl.multiple_of(lax.bitwise_xor(half, j) * (2 * per), 2 * per)
        mine_ref[j] = held_ref[pl.ds(pl.multiple_of(row + core * per, per), per), :]
        other_ref[j] = held_ref[pl.ds(pl.multiple_of(row + (1 - core) * per, per), per), :]
        return 0

    lax.fori_loop(0, blocks, step, 0, unroll=2)


def turn(n, cot, after):
    rows, d = cot.shape
    out = shape((n // 2, d // n, rows), BF)
    return pl.pallas_call(
        turn_body,
        in_specs=[WHOLE] + [ANYWHERE] * len(after),
        out_specs=[WHOLE] * 2,
        out_shape=[out] * 2,
        scratch_shapes=[pltpu.VMEM((d, rows), BF)],
        compiler_params=params(VMEM_MIB),
        cost_estimate=cost(2),
        name="turn",
    )(cot, *after)


def edges_out(odd, first, last, a_ref, b_ref):
    @pl.when(odd == 0)
    def _():
        a_ref[...] = last
        b_ref[...] = first

    @pl.when(odd != 0)
    def _():
        a_ref[...] = first
        b_ref[...] = last


def front_body(
    utt, x_hbm, ln_hbm, gain_hbm, bias_hbm, w_hbm, cot_hbm,
    gated_ref, p_ref, q_ref, hat_ref, rstd_ref, vec_ref, a_ref, b_ref, normed_ref, x_ref, w_ref, cot_ref,
    ln_ref, gain_ref, bias_ref, x_sem, w_sem, cot_sem, row_sem,
):
    rows, d = x_ref.shape
    frames = rows // utt
    pieces = x_sem.shape[0]
    span = rows // pieces
    steps = d // CW

    def x_copy(i):
        at = pl.ds(i * span, span)
        return pltpu.make_async_copy(x_hbm.at[at], x_ref.at[at], x_sem.at[i])

    def w_copy(j, half):
        at = pl.ds(half * d + j * CW, CW)
        return pltpu.make_async_copy(w_hbm.at[:, at], w_ref.at[:, at], w_sem.at[j, half])

    row_copies = [
        pltpu.make_async_copy(source, target, row_sem.at[i])
        for i, (source, target) in enumerate(
            ((ln_hbm, ln_ref), (gain_hbm, gain_ref), (bias_hbm, bias_ref))
        )
    ]
    for copy in row_copies:
        copy.start()
    for i in range(pieces):
        x_copy(i).start()
    for half in range(2):
        w_copy(0, half).start()
    cots = []
    for u in range(utt):
        for side, at in enumerate((u * frames, (u + 1) * frames - PAD)):
            cots.append(
                pltpu.make_async_copy(
                    cot_hbm.at[pl.ds(at, PAD)], cot_ref.at[u, side], cot_sem.at[u, side]
                )
            )
            cots[-1].start()
    for copy in row_copies:
        copy.wait()
    for i, row_ref in enumerate((ln_ref, gain_ref, bias_ref)):
        vec_ref[i : i + 1, :] = row_ref[...].reshape(1, d)

    for i in range(pieces):
        x_copy(i).wait()
        for j in range(1 + 3 * i, min(steps, 4 + 3 * i)):
            for half in range(2):
                w_copy(j, half).start()

        for k in range(i * span, (i + 1) * span, 16):
            at = slice(k, k + 16)
            x = x_ref[at, :].astype(F32)
            mu = jnp.sum(x, axis=-1, keepdims=True) * (1.0 / d)
            c = x - mu
            var = jnp.sum(c * c, axis=-1, keepdims=True) * (1.0 / d)
            rstd = lax.rsqrt(var + EPSILON)
            hat = c * rstd
            rstd_ref[at, :] = rstd
            hat_ref[at, :] = hat.astype(BF)
            normed_ref[at, :] = (hat * vec_ref[0:1, :]).astype(BF)

    odd = place()[0] != 0
    for j in range(steps):
        cols = slice(j * CW, (j + 1) * CW)
        for half in range(2):
            w_copy(j, half).wait()
        value = jnp.dot(normed_ref[...], w_ref[:, cols], preferred_element_type=F32)
        gate = jnp.dot(
            normed_ref[...], w_ref[:, d + j * CW : d + (j + 1) * CW], preferred_element_type=F32
        )
        sig = jax.nn.sigmoid(gate)
        gated = value * sig
        held = gated.astype(BF)
        gated_ref[:, cols] = held
        p_ref[:, cols] = sig.astype(BF)
        q_ref[:, cols] = (gated * (1.0 - sig)).astype(BF)
        shaped = held.reshape(utt, frames, CW)
        first, last = shaped[:, :HALO], shaped[:, frames - HALO :]
        a_ref[:, :HALO, cols] = jnp.where(odd, first, last)
        b_ref[:, :HALO, cols] = jnp.where(odd, last, first)
    for copy in cots:
        copy.wait()
    first, last = cot_ref[:, 0], cot_ref[:, 1]
    a_ref[:, HALO:, :] = jnp.where(odd, first, last)
    b_ref[:, HALO:, :] = jnp.where(odd, last, first)


def front(utt, x, ln_gain, bn_gain, bn_bias, w_in, cot):
    rows, d = x.shape
    out = near((rows, d), BF)
    edge = shape((utt, HALO + PAD, d), BF)
    return pl.pallas_call(
        functools.partial(front_body, utt),
        in_specs=[FAR] * 6,
        out_specs=[WHOLE] * 8,
        out_shape=[out] * 4 + [near((rows, 1), F32), near((3, d), F32)] + [edge] * 2,
        scratch_shapes=[
            pltpu.VMEM((rows, d), BF),
            pltpu.VMEM((rows, d), BF),
            pltpu.VMEM((d, 2 * d), BF),
            pltpu.VMEM((utt, 2, PAD, d), BF),
            pltpu.VMEM((d,), F32),
            pltpu.VMEM((d,), F32),
            pltpu.VMEM((d,), F32),
            pltpu.SemaphoreType.DMA((2,)),
            pltpu.SemaphoreType.DMA((d // CW, 2)),
            pltpu.SemaphoreType.DMA((utt, 2)),
            pltpu.SemaphoreType.DMA((3,)),
        ],
        compiler_params=params(24),
        cost_estimate=cost(10),
        name="front",
    )(*[far(a) for a in (x, ln_gain, bn_gain, bn_bias, w_in, cot)])


def lane_groups(first, last, work):
    def step(i, _):
        for slot in range(2):
            group = 2 * i + slot
            work(group, pl.ds(pl.multiple_of(group * LANES, LANES), LANES), slot)
        return 0

    lax.fori_loop(first // (2 * LANES), last // (2 * LANES), step, 0)


PHASES = 4
PIECES = 9


def thirds(x0, x1, x2):
    return [x1, x0 - x1, x2 - x1]


def sequences(x):
    tops = [
        (x[1], x[3], x[5]),
        (x[0] - x[1], x[2] - x[3], x[4] - x[5]),
        (x[2] - x[1], x[4] - x[3], x[6] - x[5]),
    ]
    return [piece for top in tops for piece in thirds(*top)]


def combined(h):
    tops = [(h[0] + h[1], h[2] + h[3]), (h[0], h[2]), (h[1], h[3])]
    return [piece for a, b in tops for piece in (a + b, a, b)]


def assembled(products):
    halves = []
    for top in range(3):
        m, p, q = (next(products) for _ in range(3))
        halves.append((m + p, m + q))
        if top:
            for j in range(2):
                yield 2 * j + top - 1, halves[0][j] + halves[top][j]


def phase(first, size):
    return pl.ds(first, size, PHASES)


def fill_sequences(pad_ref, shift, seq_ref, size):
    x = [pad_ref[phase(j + shift, size), :] for j in range(2 * PHASES - 1)]
    for i, piece in enumerate(sequences(x)):
        seq_ref[i] = piece


def filtered(seq_refs, taps_ref, order, count):
    for i in range(PIECES):
        acc = jnp.zeros((count * len(seq_refs), LANES), F32)
        for a in range(taps_ref.shape[1]):
            row = order(a)
            rows = [seq_ref[i, a : a + count, :] for seq_ref in seq_refs]
            acc = acc + taps_ref[i, row : row + 1, :] * jnp.concatenate(rows, axis=0)
        yield acc


def tap_factors(k_ref, lanes, held_ref, taps_ref):
    per = k_ref.shape[0] // PHASES
    held_ref[0 : per * PHASES, :] = k_ref[:, lanes]
    for i, piece in enumerate(combined([held_ref[phase(i, per), :] for i in range(PHASES)])):
        taps_ref[i] = piece


def conv_pieces(pad_refs, seq_refs, taps_ref, count):
    for pad_ref, seq_ref in zip(pad_refs, seq_refs):
        fill_sequences(pad_ref, 1, seq_ref, count + taps_ref.shape[1])
    for i, y in assembled(filtered(seq_refs, taps_ref, lambda a: a, count)):
        for j, pad_ref in enumerate(pad_refs):
            pad_ref[phase(i, count), :] = y[j * count : (j + 1) * count]


def squares(values):
    values = values.reshape(values.shape[0] // 8, 8, LANES)
    return jnp.sum(values, axis=0), jnp.sum(values * values, axis=0)


def conv_mid_body(utt, g_ref, k_ref, conv_ref, sums_ref, pad_ref, seq_ref, taps_ref):
    d = g_ref.shape[1]
    frames = g_ref.shape[0] // utt
    mid = frames - HALO

    def work(_, lanes, slot):
        first = square = jnp.zeros((8, LANES), F32)
        tap_factors(k_ref, lanes, pad_ref.at[slot, 0], taps_ref.at[slot])
        for u in range(utt):
            pad = pad_ref.at[slot, u]
            pad[0:frames, :] = g_ref[u * frames : (u + 1) * frames, lanes].astype(F32)
            conv_pieces([pad], [seq_ref.at[slot, u]], taps_ref.at[slot], mid // PHASES)
            y = pad[0:mid, :]
            start = u * (frames + HALO) + HALO
            conv_ref[start : start + mid, lanes] = y
            one, two = squares(y)
            first, square = first + one, square + two
        sums_ref[0:1, lanes] = jnp.sum(first, axis=0, keepdims=True)
        sums_ref[1:2, lanes] = jnp.sum(square, axis=0, keepdims=True)

    lane_groups(0, d, work)


def conv_scratch(utt, pieces, frames, count, per):
    return [
        pltpu.VMEM((2, utt * pieces, frames + 8, LANES), F32),
        pltpu.VMEM((2, utt * pieces, PIECES, count + per, LANES), F32),
        pltpu.VMEM((2, PIECES, per, LANES), F32),
    ]


def conv_mid(utt, gated, kernel):
    rows, d = gated.shape
    frames = rows // utt
    per = kernel.shape[0] // PHASES
    return pl.pallas_call(
        functools.partial(conv_mid_body, utt),
        in_specs=[WHOLE] * 2,
        out_specs=[WHOLE] * 2,
        out_shape=[near((utt * (frames + HALO), d), F32), near((2, d), F32)],
        scratch_shapes=conv_scratch(utt, 1, frames, (frames - HALO) // PHASES, per),
        compiler_params=params(VMEM_MIB),
        cost_estimate=cost(5),
        name="conv_mid",
    )(gated, kernel)


def conv_end_body(utt, g_ref, a_ref, b_ref, k_ref, _, some_ref, *rest):
    conv_ref, sums_ref, pad_ref, seq_ref, taps_ref = rest[-5:]
    d = g_ref.shape[1]
    frames = g_ref.shape[0] // utt
    odd = place()[0] != 0

    def work(_, lanes, slot):
        first = square = jnp.zeros((8, LANES), F32)
        tap_factors(k_ref, lanes, pad_ref.at[slot, 0], taps_ref.at[slot])
        for u in range(utt):
            a = a_ref[u, :HALO, lanes].astype(F32)
            b = b_ref[u, :HALO, lanes].astype(F32)
            for side in range(2):
                pad = pad_ref.at[slot, 2 * u + side]
                at = u * frames + side * (frames - HALO)
                here = g_ref[at : at + HALO, lanes].astype(F32)
                beside = jnp.where(odd, b, a) if side else jnp.where(odd, a, b)
                pad[side * HALO : (side + 1) * HALO, :] = beside
                pad[(1 - side) * HALO : (2 - side) * HALO, :] = here
        conv_pieces(
            [pad_ref.at[slot, j] for j in range(2 * utt)],
            [seq_ref.at[slot, j] for j in range(2 * utt)],
            taps_ref.at[slot],
            HALO // PHASES,
        )
        for u in range(utt):
            for side in range(2):
                pad = pad_ref.at[slot, 2 * u + side]
                out = u * (frames + HALO) + side * frames
                conv_ref[out : out + HALO, lanes] = pad[0:HALO, :]
                own = (1 - side) * PAD
                one, two = squares(pad[own : own + PAD, :])
                first, square = first + one, square + two
        sums_ref[0:1, lanes] = some_ref[0:1, lanes] + jnp.sum(first, axis=0, keepdims=True)
        sums_ref[1:2, lanes] = some_ref[1:2, lanes] + jnp.sum(square, axis=0, keepdims=True)

    lane_groups(0, d, work)


def conv_end(utt, gated, a, b, kernel, conv_some, sums_some, after):
    rows, d = gated.shape
    per = kernel.shape[0] // PHASES
    return pl.pallas_call(
        functools.partial(conv_end_body, utt),
        in_specs=[WHOLE] * 6 + [ANYWHERE] * len(after),
        out_specs=[WHOLE] * 2,
        out_shape=[near(conv_some.shape, F32), shape((2, d), F32)],
        scratch_shapes=conv_scratch(utt, 2, 2 * HALO, HALO // PHASES, per),
        input_output_aliases={4: 0},
        compiler_params=params(VMEM_MIB),
        cost_estimate=cost(2),
        name="conv_end",
    )(gated, a, b, kernel, conv_some, sums_some, *after)


def act_grad_body(start, cot_ref, w_ref, *rest):
    out_ref = rest[-1]
    for j in range(out_ref.shape[1] // CW):
        cols = slice(j * CW, (j + 1) * CW)
        source = slice(start + j * CW, start + (j + 1) * CW)
        out_ref[:, cols] = jnp.dot(cot_ref[...], w_ref[:, source], preferred_element_type=F32)


def act_grad(start, width, cot, w_out, after):
    return pl.pallas_call(
        functools.partial(act_grad_body, start),
        in_specs=[WHOLE] * 2 + [ANYWHERE] * len(after),
        out_specs=WHOLE,
        out_shape=near((cot.shape[0], width), F32),
        compiler_params=params(VMEM_MIB),
        cost_estimate=cost(1.5),
        name="act_grad",
    )(cot, w_out, *after)


def act_grad_end_body(a_ref, b_ref, w_ref, *rest):
    out_ref = rest[-1]
    utt = a_ref.shape[0]
    odd = place()[0] != 0
    pieces = []
    for u in range(utt):
        a, b = a_ref[u, HALO:, :], b_ref[u, HALO:, :]
        pieces += [jnp.where(odd, a, b), jnp.where(odd, b, a)]
    cot = jnp.concatenate(pieces, axis=0)
    out_ref[...] = jnp.dot(cot, w_ref[...], preferred_element_type=F32)


def act_grad_end(a, b, w_out, after):
    utt, _, d = a.shape
    return pl.pallas_call(
        act_grad_end_body,
        in_specs=[WHOLE] * 3 + [ANYWHERE] * len(after),
        out_specs=WHOLE,
        out_shape=near((utt * HALO, d), F32),
        compiler_params=params(VMEM_MIB),
        cost_estimate=cost(2),
        name="act_grad_end",
    )(a, b, w_out, *after)


def middle_body(utt, total, conv_ref, sums_ref, vec_ref, left_ref, right_ref, end_ref, *rest):
    act_ref, dbn_ref, dsums_ref = rest[-3:]
    d = conv_ref.shape[1]
    frames = left_ref.shape[0] // utt
    per_half = left_ref.shape[1] // CW
    for j in range(d // CW):
        cols = slice(j * CW, (j + 1) * CW)
        own_ref = (left_ref, right_ref)[j // per_half]
        own_cols = slice(j % per_half * CW, (j % per_half + 1) * CW)
        mean = sums_ref[0:1, cols] * (1.0 / total)
        var = sums_ref[1:2, cols] * (1.0 / total) - mean * mean
        rstd = lax.rsqrt(var + EPSILON)

        def back(at, d_act):
            xhat = (conv_ref[at, cols] - mean) * rstd
            out = xhat * vec_ref[1:2, cols] + vec_ref[2:3, cols]
            sig = jax.nn.sigmoid(out)
            act = out * sig
            dbn = d_act * (sig + act * (1.0 - sig))
            dbn_ref[at, cols] = dbn
            return xhat, act, dbn

        bias = gain = 0.0
        for u in range(utt):
            start = u * (frames + HALO)
            back(slice(start, start + PAD), end_ref[u * HALO : u * HALO + PAD, cols])
            rows = slice(u * frames, (u + 1) * frames)
            xhat, act, dbn = back(slice(start + PAD, start + PAD + frames), own_ref[rows, own_cols])
            act_ref[rows, cols] = act.astype(BF)
            bias += jnp.sum(dbn, axis=0, keepdims=True)
            gain += jnp.sum(dbn * xhat, axis=0, keepdims=True)
            back(
                slice(start + PAD + frames, start + HALO + frames),
                end_ref[u * HALO + PAD : (u + 1) * HALO, cols],
            )
        dsums_ref[0:1, cols] = bias
        dsums_ref[1:2, cols] = gain


def middle(utt, total, conv_out, sums, vec, left, right, end, after):
    rows = left.shape[0]
    d = conv_out.shape[1]
    return pl.pallas_call(
        functools.partial(middle_body, utt, total),
        in_specs=[WHOLE] * 6 + [ANYWHERE] * len(after),
        out_specs=[WHOLE] * 3,
        out_shape=[shape((rows, d), BF), near(conv_out.shape, F32), shape((2, d), F32)],
        compiler_params=params(VMEM_MIB),
        cost_estimate=cost(3),
        name="middle",
    )(conv_out, sums, vec, left, right, end, *after)


def grad_body(bits, ca_ref, cb_ref, acta_ref, actb_ref, *rest):
    out_refs = rest[-4:]
    blocks, per, rows = ca_ref.shape
    half = out_refs[0].shape[-1]
    ca = ca_ref[...].reshape(blocks * per, rows)
    cb = cb_ref[...].reshape(blocks * per, rows)
    for side, bit in enumerate(bits):
        send_ref, keep_ref = out_refs[2 * side], out_refs[2 * side + 1]
        for c in range(half // CW):
            cols = slice(c * CW, (c + 1) * CW)
            src = slice(side * half + c * CW, side * half + (c + 1) * CW)
            dw = jnp.dot(ca, acta_ref[:, src], preferred_element_type=F32)
            dw += jnp.dot(cb, actb_ref[:, src], preferred_element_type=F32)
            sent = kept = 0
            for j in range(blocks):
                block = dw[j * per : (j + 1) * per]
                if j & bit:
                    send_ref[sent, :, cols] = block.astype(BF)
                    sent += 1
                else:
                    keep_ref[kept, :, cols] = block
                    kept += 1


def grad(bits, cot_a, cot_b, act_a, act_b, after):
    blocks, per, _ = cot_a.shape
    d = act_a.shape[1]
    half = (blocks // 2, per, d // 2)
    return pl.pallas_call(
        functools.partial(grad_body, bits),
        in_specs=[WHOLE] * 4 + [ANYWHERE] * len(after),
        out_specs=[WHOLE] * 4,
        out_shape=[shape(half, BF), shape(half, F32)] * 2,
        compiler_params=params(VMEM_MIB),
        cost_estimate=cost(3.5),
        name="grad",
    )(cot_a, cot_b, act_a, act_b, *after)


def branch_body(start, x_ref, act_ref, w_ref, *rest):
    out_hbm, done_ref, out_ref, sem = rest[-4:]
    done_ref[...] = jnp.zeros(done_ref.shape, F32)
    copies = []
    for j in range(sem.shape[0]):
        cols = slice(start + j * CW, start + (j + 1) * CW)
        here = slice(j * CW, (j + 1) * CW)
        part = lax.dot_general(
            act_ref[...], w_ref[cols, :], (((1,), (1,)), ((), ())), preferred_element_type=F32
        )
        out_ref[:, here] = (x_ref[:, cols].astype(F32) + part).astype(BF)
        copies.append(pltpu.make_async_copy(out_ref.at[:, here], out_hbm.at[:, cols], sem.at[j]))
        copies[-1].start()
    for copy in copies:
        copy.wait()


def branch(start, width, x, act, w_out, some, after):
    rows, d = x.shape
    return pl.pallas_call(
        functools.partial(branch_body, start),
        in_specs=[WHOLE] * 3 + [FAR] * len(some) + [ANYWHERE] * len(after),
        out_specs=[FAR, WHOLE],
        out_shape=[pltpu.HBM((rows, d), BF), near((8, LANES), F32)],
        scratch_shapes=[pltpu.VMEM((rows, width), BF), pltpu.SemaphoreType.DMA((width // CW,))],
        input_output_aliases={3: 0} if some else {},
        compiler_params=params(VMEM_MIB),
        cost_estimate=cost(2),
        name="branch",
    )(x, act, w_out, *some, *after)


def grad_taps_body(
    utt, total, dbn_ref, conv_ref, sums_ref, dsums_ref, vec_ref, g_ref,
    dk_ref, seq_ref, bias_ref, gain_ref, pad_ref, held_ref, acc_ref,
):
    d = g_ref.shape[1]
    frames = g_ref.shape[0] // utt
    count = frames // PHASES
    taps = dk_ref.shape[0]
    per = taps // PHASES
    _, _, keep_lo, keep_hi = place()
    bias_ref[...] = dsums_ref[0:1, :].reshape(d)
    gain_ref[...] = dsums_ref[1:2, :].reshape(d)

    def work(group, lanes, slot):
        mean = sums_ref[0:1, lanes] * (1.0 / total)
        var = sums_ref[1:2, lanes] * (1.0 / total) - mean * mean
        rstd = lax.rsqrt(var + EPSILON)
        scale = rstd * vec_ref[1:2, lanes]
        cross = scale * rstd * (dsums_ref[1:2, lanes] * (1.0 / total))
        mean_grad = scale * (dsums_ref[0:1, lanes] * (1.0 / total))

        def d_conv(at):
            return dbn_ref[at, lanes] * scale - mean_grad - (conv_ref[at, lanes] - mean) * cross

        for u in range(utt):
            start = u * (frames + HALO)
            end = start + PAD + frames
            rows = slice(u * frames, (u + 1) * frames)
            pad = pad_ref.at[slot, u]
            pad[0:PAD, :] = d_conv(slice(start, start + PAD)) * keep_lo
            pad[PAD : PAD + frames, :] = d_conv(slice(start + PAD, end))
            pad[PAD + frames : HALO + frames, :] = d_conv(slice(end, end + PAD)) * keep_hi
            fill_sequences(pad_ref.at[slot, u], 0, seq_ref.at[group, u], count + per)
            pad_ref[slot, u, 0:frames, :] = g_ref[rows, lanes].astype(F32)
            g = [pad_ref[slot, u, phase(i, count), :] for i in range(PHASES)]
            for i, piece in enumerate(combined(g)):
                held_ref[slot, u, i] = piece

        def products():
            for i in range(PIECES):
                sums = [jnp.zeros((8, LANES), F32)] * per
                for u in range(utt):
                    for base in range(0, count, 32):
                        g = held_ref[slot, u, i, base : base + 32, :]
                        for a in range(per):
                            prod = g * seq_ref[group, u, i, base + a : base + a + 32, :]
                            sums[a] = sums[a] + jnp.sum(prod.reshape(4, 8, LANES), axis=0)
                yield jnp.stack(sums)

        for i, y in assembled(products()):
            for a in range(per):
                acc_ref[slot, taps - 1 - (PHASES * a + i)] = y[a]
        dk_ref[:, lanes] = jnp.sum(acc_ref[slot], axis=1).astype(BF)

    lane_groups(0, d, work)


def grad_taps(utt, total, taps, dbn, conv_out, sums, dsums, vec, gated):
    rows, d = gated.shape
    frames = rows // utt
    long = frames // PHASES + taps // PHASES
    return pl.pallas_call(
        functools.partial(grad_taps_body, utt, total),
        in_specs=[WHOLE] * 6,
        out_specs=[WHOLE] * 4,
        out_shape=[
            shape((taps, d), BF),
            near((d // LANES, utt, PIECES, long, LANES), F32),
            shape((d,), F32),
            shape((d,), F32),
        ],
        scratch_shapes=[
            pltpu.VMEM((2, utt, frames + 2 * PAD + 8, LANES), F32),
            pltpu.VMEM((2, utt, PIECES, frames // PHASES, LANES), F32),
            pltpu.VMEM((2, taps, 8, LANES), F32),
        ],
        compiler_params=params(VMEM_MIB),
        cost_estimate=cost(9),
        name="grad_taps",
    )(dbn, conv_out, sums, dsums, vec, gated)


def grad_proj_body(utt, start, seq_ref, k_ref, p_ref, q_ref, *rest):
    dv_ref, dg_ref, out_ref, taps_ref = rest[-4:]
    rows, width = dv_ref.shape
    frames = rows // utt
    count = frames // PHASES
    per = k_ref.shape[0] // PHASES

    def work(group, out, slot):
        lanes = pl.ds(pl.multiple_of(out.start + start, LANES), LANES)
        out_ref[slot, 0 : per * PHASES, :] = k_ref[:, lanes]
        k = [out_ref[slot, phase(PHASES - 1 - i, per), :] for i in range(PHASES)]
        for i, piece in enumerate(combined(k)):
            taps_ref[slot, i] = piece
        for u in range(utt):
            products = filtered(
                [seq_ref.at[group + start // LANES, u]],
                taps_ref.at[slot],
                lambda a: per - 1 - a,
                count,
            )
            for i, y in assembled(products):
                out_ref[slot, phase(u * frames + i, count), :] = y
        acc = out_ref[slot, 0:rows, :]
        dv_ref[:, out] = (acc * p_ref[:, lanes].astype(F32)).astype(BF)
        dg_ref[:, out] = (acc * q_ref[:, lanes].astype(F32)).astype(BF)

    lane_groups(0, width, work)


def grad_proj(utt, start, width, seqs, kernel, p, q, after):
    rows = p.shape[0]
    out = near((rows, width), BF)
    return pl.pallas_call(
        functools.partial(grad_proj_body, utt, start),
        in_specs=[WHOLE] * 4 + [ANYWHERE] * len(after),
        out_specs=[WHOLE] * 2,
        out_shape=[out, out],
        scratch_shapes=[
            pltpu.VMEM((2, rows + 8, LANES), F32),
            pltpu.VMEM((2, PIECES, kernel.shape[0] // PHASES, LANES), F32),
        ],
        compiler_params=params(VMEM_MIB),
        cost_estimate=cost(4),
        name="grad_proj",
    )(seqs, kernel, p, q, *after)


def back_proj_body(start, vec_ref, w_ref, *rest):
    pieces = rest[:4]
    out_ref = rest[-1]
    wide = pieces[0].shape[1]
    dims = (((1,), (1,)), ((), ()))
    for j in range(out_ref.shape[1] // CW):
        cols = slice(start + j * CW, start + (j + 1) * CW)
        part = 0.0
        for k, piece in enumerate(pieces):
            part += lax.dot_general(
                piece[...], w_ref[cols, k * wide : (k + 1) * wide], dims, preferred_element_type=F32
            )
        out_ref[:, j * CW : (j + 1) * CW] = part * vec_ref[0:1, cols]


def back_proj(start, width, vec, w_in, pieces, after):
    rows = pieces[0].shape[0]
    return pl.pallas_call(
        functools.partial(back_proj_body, start),
        in_specs=[WHOLE] * 6 + [ANYWHERE] * len(after),
        out_specs=WHOLE,
        out_shape=near((rows, width), F32),
        compiler_params=params(VMEM_MIB),
        cost_estimate=cost(2.6),
        name="back_proj",
    )(vec, w_in, *pieces, *after)


def back_norm_body(hat_ref, rstd_ref, cot_ref, left_ref, right_ref, *rest):
    out_hbm, done_ref, out_ref, sem = rest[-4:]
    done_ref[...] = jnp.zeros(done_ref.shape, F32)
    copies = []
    rows, d = hat_ref.shape
    span = rows // sem.shape[0]
    for i in range(0, rows, 16):
        at = slice(i, i + 16)
        hats = [hat_ref[at, : d // 2].astype(F32), hat_ref[at, d // 2 :].astype(F32)]
        grads = [left_ref[at, :], right_ref[at, :]]
        m1 = sum(jnp.sum(g, axis=-1, keepdims=True) for g in grads) * (1.0 / d)
        m2 = sum(jnp.sum(g * h, axis=-1, keepdims=True) for g, h in zip(grads, hats)) * (1.0 / d)
        rstd = rstd_ref[at, :]
        for k, cols in enumerate((slice(0, d // 2), slice(d // 2, d))):
            layer = rstd * (grads[k] - m1 - hats[k] * m2)
            out_ref[at, cols] = (cot_ref[at, cols].astype(F32) + layer).astype(BF)
        if (i + 16) % span == 0:
            piece = pl.ds(i + 16 - span, span)
            copies.append(
                pltpu.make_async_copy(out_ref.at[piece], out_hbm.at[piece], sem.at[i // span])
            )
            copies[-1].start()
    for copy in copies:
        copy.wait()


def back_norm(hat, rstd, cot, left, right, after):
    rows, d = hat.shape
    return pl.pallas_call(
        back_norm_body,
        in_specs=[WHOLE] * 5 + [ANYWHERE] * len(after),
        out_specs=[FAR, WHOLE],
        out_shape=[pltpu.HBM((rows, d), BF), near((8, LANES), F32)],
        scratch_shapes=[pltpu.VMEM((rows, d), BF), pltpu.SemaphoreType.DMA((8,))],
        compiler_params=params(VMEM_MIB),
        cost_estimate=cost(3),
        name="back_norm",
    )(hat, rstd, cot, left, right, *after)


def swap(block, axis, bit):
    count = lax.axis_size(axis)
    return lax.ppermute(block, axis, [(i, i ^ bit) for i in range(count)])


def is_power(count):
    return count & (count - 1) == 0


def add_body(own_ref, got_ref, *rest):
    out_ref = rest[-1]
    out_ref[...] = (own_ref[...].astype(F32) + got_ref[...].astype(F32)).astype(out_ref.dtype)


def add(own, got, dtype, after):
    return pl.pallas_call(
        add_body,
        in_specs=[WHOLE] * 2 + [ANYWHERE] * len(after),
        out_specs=WHOLE,
        out_shape=shape(own.shape, dtype),
        compiler_params=params(4),
        cost_estimate=cost(0.5),
        name="add",
    )(own, got, *after)


def last_add_body(a_ref, b_ref, c_ref, d_ref, *rest):
    one_ref, two_ref = rest[-2:]
    one_ref[...] = a_ref[...].astype(F32) + b_ref[...].astype(F32)
    two_ref[...] = c_ref[...].astype(F32) + d_ref[...].astype(F32)


def last_add(one, two, after):
    return pl.pallas_call(
        last_add_body,
        in_specs=[WHOLE] * 4 + [ANYWHERE] * len(after),
        out_specs=[WHOLE] * 2,
        out_shape=[shape(one[0].shape, F32), shape(two[0].shape, F32)],
        compiler_params=params(4),
        cost_estimate=cost(0.7),
        name="last_add",
    )(*one, *two, *after)


def all_sum(block, axis, fill=(), order=None, whole=True):
    count = lax.axis_size(axis)
    if not is_power(count):
        for work in fill:
            work([])
        return lax.psum(block.astype(F32), axis)
    bits = [1 << i for i in range(count.bit_length() - 1)]
    if order is not None:
        bits = order(bits)
    for step, bit in enumerate(bits):
        other = swap(block, axis, bit)
        after = fill[step]([block]) if step < len(fill) else []
        if bit == bits[-1] and not whole:
            return (block, other), after
        block = add(block, other, F32 if bit == bits[-1] else block.dtype, after)
    return block


def nothing(_):
    return []


def beside(a, b, axis):
    count = lax.axis_size(axis)
    pairs = []
    for low in range(1, count - 1, 2):
        pairs += [(low, low + 1), (low + 1, low)]
    return swap(a, axis, 1), lax.ppermute(b, axis, pairs)


def merge_body(sides, after, *refs):
    keep_out, send_out = refs[2 * sides + after :]
    blocks = refs[0].shape[0]
    wide = refs[0].shape[2]
    for side in range(sides):
        keep_ref, got_ref = refs[2 * side : 2 * side + 2]
        cols = slice(side * wide, (side + 1) * wide)
        for j in range(blocks):
            total = keep_ref[j] + got_ref[j].astype(F32)
            if j % 2:
                send_out[j // 2, :, cols] = total.astype(BF)
            else:
                keep_out[j // 2, :, cols] = total


def merge(pairs, after):
    blocks, per, wide = pairs[0][0].shape
    dims = (blocks // 2, per, wide * len(pairs))
    return pl.pallas_call(
        functools.partial(merge_body, len(pairs), len(after)),
        in_specs=[WHOLE] * (2 * len(pairs)) + [ANYWHERE] * len(after),
        out_specs=[WHOLE] * 2,
        out_shape=[shape(dims, F32), shape(dims, BF)],
        compiler_params=params(8),
        cost_estimate=cost(1),
        name="merge",
    )(*[a for pair in pairs for a in pair], *after)


def first_swaps(parts, axis, after):
    return [
        merge([(keep, swap(send, axis, device_bit))], after)
        for (keep, send), device_bit in zip(parts, (2, 4))
    ]


def last_swaps(held, axis, after):
    count = lax.axis_size(axis)
    after = list(after)
    pairs = [
        (keep, swap(send, axis, device_bit)) for (keep, send), device_bit in zip(held, (4, 2))
    ]
    bit = 8
    if bit == count:
        both = [jnp.concatenate(side, axis=-1)[0] for side in zip(*pairs)]
        return both[0], both[1]
    while True:
        keep, send = merge(pairs, after.pop(0) if after else [])
        got = swap(send, axis, bit)
        bit *= 2
        if bit == count:
            return keep[0], got[0]
        pairs = [(keep, got)]


def on_device(inputs, ln_gain, w_in, kernel, bn_gain, bn_bias, w_out, cotangent):
    axis = AXIS
    n = lax.axis_size(axis)
    me = lax.axis_index(axis).astype(jnp.int32)
    utt, frames, d = inputs.shape
    rows = utt * frames
    half = d // 2
    total = rows * n
    x = inputs.reshape(rows, d)
    cot = cotangent.reshape(rows, d)
    by_owner = is_power(n) and n >= 8 and d % n == 0 and (d // n) % 16 == 0

    gated, p, q, hat, rstd, vec, ga, gb = front(utt, x, ln_gain, bn_gain, bn_bias, w_in, cot)
    ga, gb = beside(ga, gb, axis)
    conv_some, sums_some = conv_mid(utt, gated, kernel)
    conv_out, sums = conv_end(utt, gated, ga, gb, kernel, conv_some, sums_some, [])
    made = {}
    half = d // 2

    def act_grading(start):
        def work(after):
            made["d_act", start] = act_grad(start, half, cot, w_out, after)
            return [made["d_act", start]]

        return work

    def ending(after):
        made["d_act_end"] = act_grad_end(ga, gb, w_out, after)
        if not by_owner:
            return [made["d_act_end"]]
        made["cot"], other = turn(n, cot, after)
        made["cot_beside"] = swap(other, axis, 1)
        return [made["d_act_end"], made["cot"]]

    sums = all_sum(sums, axis, [nothing, act_grading(0), act_grading(half), nothing, ending])
    act, dbn, dsums = middle(
        utt, total, conv_out, sums, vec, made["d_act", 0], made["d_act", half], made["d_act_end"], []
    )

    def branching(start):
        def work(after):
            some = [made["outputs"]] if start else []
            made["outputs"], done = branch(start, half, x, act, w_out, some, after)
            return [done]

        return work

    def grading(after):
        if not by_owner:
            return []
        act_b = swap(act, axis, 1)
        made["grad"] = grad((1, 2), made["cot"], made["cot_beside"], act, act_b, after)
        return [made["grad"][0]]

    dsums = all_sum(
        dsums, axis, [branching(0), branching(half), grading], lambda bits: bits[1:] + bits[:1]
    )
    if by_owner:
        send_l, keep_l, send_r, keep_r = made["grad"]
        held = first_swaps([(keep_l, send_l), (keep_r, send_r)], axis, [dsums])
    else:
        dw = lax.dot_general(cot, act, (((0,), (0,)), ((), ())), preferred_element_type=F32)
        d_w_out = lax.psum_scatter(dw, axis, scatter_dimension=0, tiled=True)

    d_kernel, d_conv, d_bn_bias, d_bn_gain = grad_taps(
        utt, total, kernel.shape[0], dbn, conv_out, sums, dsums, vec, gated
    )

    def projecting(after):
        for start in (0, half):
            made[start] = grad_proj(utt, start, half, d_conv, kernel, p, q, after)
        return [made[0][0], made[half][0]]

    def back_projecting(start):
        def work(after):
            left, right = made[0], made[half]
            pieces = (left[0], right[0], left[1], right[1])
            made["far"] = after
            made["grads", start] = back_proj(start, half, vec, w_in, pieces, after)
            return [made["grads", start]]

        return work

    def norming(after):
        made["d_inputs"], done = back_norm(
            hat, rstd, cot, made["grads", 0], made["grads", half], after
        )
        return [done]

    terms = all_sum(
        d_kernel,
        axis,
        [nothing, projecting, back_projecting(0), back_projecting(half), norming],
        lambda bits: bits[:1] + bits[:2:-1] + bits[1:3],
        whole=not by_owner,
    )
    if by_owner:
        terms, after = terms
        own = last_swaps(held, axis, [made["far"], [made["grads", half]]])
        d_w_out, d_kernel_sum = last_add(own, terms, after)
    else:
        d_kernel_sum = terms
    return (
        made["outputs"].reshape(inputs.shape), made["d_inputs"].reshape(inputs.shape), d_w_out,
        d_kernel_sum, d_bn_gain, d_bn_bias,
    )


def solution(mesh):
    return jax.shard_map(
        on_device,
        mesh=mesh,
        in_specs=(P(None, "seq", None), P(), P(), P(), P(), P(), P(), P(None, "seq", None)),
        out_specs=(P(None, "seq", None), P(None, "seq", None), P("seq", None), P(), P(), P()),
        check_vma=False,
    )
```
